512 devices in a mesh: dp: 64 (over z, y_lo, x), fsdp: 8 (over y_hi, core).
Axes of the slice: x: 4, y: 8 (y_hi: 4, y_lo: 2; y = y_hi * 2 + y_lo), z: 8, core: 2. Of those that a mesh axis runs over, the one named last changes fastest.
Arguments:
- adapter_in: bfloat16 [65536, 8192], P(('dp', 'fsdp')), may hold values from -6 to 6
- frozen: bfloat16 [65536, 8192], P(('dp', 'fsdp')), may hold values from -8 to 8
- gain: float32 [8192], replicated, may hold values from 0.25 to 1.75
- adapter_a: bfloat16 [8192, 64], P('fsdp'), may hold values from -0.0625 to 0.0625
- adapter_up_matrix: bfloat16 [64, 8192], P(None, 'fsdp'), may hold values from -0.75 to 0.75
- passages: bfloat16 [2048, 8192], P('dp', 'fsdp'), may hold values from -8 to 8
- positive: int32 [2048], P('dp'), may hold values from 0 to 2047, as said below
Outputs:
- adapter_grads: float32 [2, 64, 8192], P(None, 'fsdp', 'dp')
- loss: float32 [], replicated
The draws below stay inside these ranges and needn't reach their ends.
Inputs may be any that keep to these rules, and one draw needn't show every extreme that they name: Query i of group g (i from g * 32) has its positive among the passages of the same group, and every passage is the positive of exactly one query.
All inputs are finite; a program needn't handle non-finite values.
Results may differ from the reference program's by a relative error of at most 0.017.
Values may be sent and summed in bfloat16 or wider, within the bound.
No kernel may reach another device: no remote copies, remote signals or barrier semaphores. Data moves between devices by JAX's collectives and lax.ppermute only.
A program may use at most 64 MiB of HBM per device.

```python
import jax
import jax.numpy as jnp
from jax import lax

D = 8192
R = 64
LEN = 32
SEQ_DEV = 4
GROUP_PAIRS = 32
PAIRS = 2048
TOKENS = 65536


topic_share = 0.5477226


own_share = 0.83666


passage_signal = 0.35


passage_rest = 0.9367497


frozen_signal = 0.6


frozen_rest = 0.8


def pairing(key):
    groups = PAIRS // GROUP_PAIRS
    shuffle_key = jax.random.fold_in(key, 11)
    ranks = jax.random.randint(shuffle_key, (groups, GROUP_PAIRS), 0, 2 ** 20)
    ranked = ranks * GROUP_PAIRS + jnp.arange(GROUP_PAIRS, dtype=jnp.int32)[None, :]
    owners_local = jnp.argsort(ranked, axis=1).astype(jnp.int32)
    positive_local = jnp.argsort(owners_local, axis=1).astype(jnp.int32)
    offsets = (jnp.arange(groups, dtype=jnp.int32) * GROUP_PAIRS)[:, None]
    owners = (owners_local + offsets).reshape(PAIRS)
    positive = (positive_local + offsets).reshape(PAIRS)
    return (owners, positive)


def directions(key):
    topics = PAIRS // GROUP_PAIRS
    topic_table = jax.random.normal(jax.random.fold_in(key, 21), (topics, D), jnp.float32)
    topic_ids = jax.random.randint(jax.random.fold_in(key, 22), (PAIRS,), 0, topics)
    own_part = jax.random.normal(jax.random.fold_in(key, 23), (PAIRS, D), jnp.float32)
    return topic_share * topic_table[topic_ids] + own_share * own_part


def column_profile(factor):
    place = jnp.arange(D, dtype=jnp.float32) / (D - 1.0)
    return jnp.exp(jnp.log(factor) * (place - 0.5))[None, :]


def draw_positive(key, part):
    owners, positive = pairing(key)
    return positive


def draw_frozen(key, part):
    own_key = jax.random.fold_in(key, 5)
    base_dir = directions(key)
    token_noise = jax.random.normal(own_key, (PAIRS, LEN, D), jnp.float32)
    values = frozen_signal * base_dir[:, None, :] + frozen_rest * token_noise
    return jnp.clip(values, -8.0, 8.0).reshape(TOKENS, D).astype(jnp.bfloat16)


def draw_passages(key, part):
    own_key = jax.random.fold_in(key, 7)
    owners, positive = pairing(key)
    base_dir = directions(key)
    passage_noise = jax.random.normal(own_key, (PAIRS, D), jnp.float32)
    row_scale = jnp.ones((PAIRS, 1), jnp.float32)
    profile = column_profile(3.0)
    values = row_scale * profile * (passage_signal * base_dir[owners] + passage_rest * passage_noise)
    return jnp.clip(values, -8.0, 8.0).astype(jnp.bfloat16)


def shard_levels(key, shape, shards, smallest, top_value):
    level, own = 1.0, jax.random.fold_in(key, 6)
    for axis_at, parts in shards:
        draws = jnp.exp(jax.random.uniform(jax.random.fold_in(own, axis_at), (parts,), jnp.float32, smallest / len(shards), top_value / len(shards)))
        level = level * jnp.repeat(draws, shape[axis_at] // parts).reshape([-1 if axis == axis_at else 1 for axis in range(len(shape))])
    return level


def gaussian(key, shape, scale, most, cuts=(), kind=jnp.bfloat16):
    level = shard_levels(key, shape, cuts, -0.22, 0.18) if cuts else 1.0
    drawn = jax.random.normal(key, shape, jnp.float32) * scale * level
    return jnp.minimum(jnp.maximum(drawn, -most), most).astype(kind)


def setup_inputs(seed: int = 0) -> dict:
    key_list = jax.random.split(jax.random.key(seed), 8)
    return {
        "adapter_in": gaussian(key_list[0], (TOKENS, D), 1.0, 6.0, ((0, 512),)),
        "frozen": draw_frozen(jax.random.fold_in(key_list[7], 71), 0),
        "gain": jnp.clip(1.0 + 0.15 * jax.random.normal(key_list[2], (D,), jnp.float32), 0.25, 1.75),
        "adapter_a": gaussian(key_list[3], (D, R), D ** -0.5, 0.0625, ((0, 8),)),
        "adapter_up_matrix": gaussian(key_list[4], (R, D), R ** -0.5, 0.75, ((1, 8),)),
        "passages": draw_passages(jax.random.fold_in(key_list[7], 71), 0),
        "positive": draw_positive(jax.random.fold_in(key_list[7], 71), 0),
    }


adapter_scale_factor = 0.25
inv_temp = 20.0
norm_eps = 1e-05

def forward_block(block_in, frozen_block_slice, gain, adapter_a, adapter_up_matrix):
    latent_code = jnp.dot(block_in, adapter_a, preferred_element_type=jnp.float32).astype(jnp.bfloat16)
    hidden_state = frozen_block_slice.astype(jnp.float32) + adapter_scale_factor * jnp.dot(latent_code, adapter_up_matrix, preferred_element_type=jnp.float32)
    inv_rms = lax.rsqrt(lax.optimization_barrier(jnp.mean(hidden_state * hidden_state, axis=-1, keepdims=True)) + norm_eps)
    normed = hidden_state * inv_rms * gain
    pooled = lax.optimization_barrier(jnp.mean(normed.reshape(-1, LEN, D), axis=1))
    length = jnp.sqrt(lax.optimization_barrier(jnp.sum(pooled * pooled, axis=-1, keepdims=True)))
    return (latent_code, hidden_state, inv_rms, pooled, length)

def reference(adapter_in, frozen, gain, adapter_a, adapter_up_matrix, passages, positive):
    blocks = PAIRS // SEQ_DEV
    tok_blocks = adapter_in.reshape(blocks, SEQ_DEV * LEN, D)
    frozen_blocks = frozen.reshape(blocks, SEQ_DEV * LEN, D)

    def query_of(pair):
        outs = forward_block(pair[0], pair[1], gain, adapter_a, adapter_up_matrix)
        return (outs[3] / outs[4]).astype(jnp.bfloat16)
    query_unit = lax.map(query_of, (tok_blocks, frozen_blocks)).reshape(PAIRS, D)
    pas = passages.astype(jnp.float32)
    passage_unit = (pas / jnp.sqrt(lax.optimization_barrier(jnp.sum(pas * pas, axis=-1, keepdims=True)))).astype(jnp.bfloat16)
    scores = inv_temp * jnp.dot(query_unit, passage_unit.T, preferred_element_type=jnp.float32)
    expo = jnp.exp(scores - inv_temp)
    row_sum = lax.optimization_barrier(jnp.sum(expo, axis=1))
    col_sum = lax.optimization_barrier(jnp.sum(expo, axis=0))
    onehot = (positive[:, None] == jnp.arange(PAIRS, dtype=jnp.int32)[None, :]).astype(jnp.float32)
    loss = (jnp.sum(jnp.log(row_sum)) + jnp.sum(jnp.log(col_sum)) - 2.0 * jnp.sum(scores * onehot)) / (2.0 * PAIRS) + inv_temp
    weights = (0.5 * (expo / row_sum[:, None] + expo / col_sum[None, :]) - onehot).astype(jnp.bfloat16)
    query_grad = inv_temp * jnp.dot(weights, passage_unit, preferred_element_type=jnp.float32)
    grad_blocks = query_grad.reshape(blocks, SEQ_DEV, D)

    def step(total, items):
        block_in, frozen_block_slice, block_grad = items
        latent_code, hidden_state, inv_rms, pooled, length = forward_block(block_in, frozen_block_slice, gain, adapter_a, adapter_up_matrix)
        unit = pooled / length
        pooled_grad = (block_grad - unit * lax.optimization_barrier(jnp.sum(unit * block_grad, axis=-1, keepdims=True))) / length
        normed_grad = jnp.repeat(pooled_grad / LEN, LEN, axis=0)
        scaled = normed_grad * gain
        hidden_state_gradient = (inv_rms * scaled - hidden_state * inv_rms ** 3 * lax.optimization_barrier(jnp.mean(scaled * hidden_state, axis=-1, keepdims=True))).astype(jnp.bfloat16)
        latent_code_gradient = (adapter_scale_factor * jnp.dot(hidden_state_gradient, adapter_up_matrix.T, preferred_element_type=jnp.float32)).astype(jnp.bfloat16)
        grad_a_t = jnp.dot(latent_code_gradient.T, block_in, preferred_element_type=jnp.float32)
        up_matrix_gradient = adapter_scale_factor * jnp.dot(latent_code.T, hidden_state_gradient, preferred_element_type=jnp.float32)
        part = jnp.stack([grad_a_t, up_matrix_gradient]).astype(jnp.bfloat16)
        return (total + part.astype(jnp.float32), None)
    start = jnp.zeros((2, R, D), jnp.float32)
    adapter_grads, unused = lax.scan(step, start, (tok_blocks, frozen_blocks, grad_blocks))
    return (adapter_grads, loss)
```

```python
import jax
import jax.numpy as jnp
from jax import lax
from jax.sharding import Mesh
from jax.sharding import PartitionSpec as P

LEN = 32


adapter_scale_factor = 0.25
inv_temp = 20.0
norm_eps = 1e-05

AXES = ("z", "yl", "x", "yh", "c")
SIZES = (4, 2, 8, 4, 2)


def contracted_row_product(left, right):
    return lax.dot_general(
        left, right, (((1,), (1,)), ((), ())), preferred_element_type=jnp.float32
    )


def exchange(blocks, axes):
    return lax.all_to_all(blocks, axes, 0, 0, tiled=True)


def to_all(block, axes, devices):
    return exchange(jnp.broadcast_to(block[None], (devices, *block.shape)), axes)


def swap_cores(value):
    return lax.ppermute(value, "c", [(0, 1), (1, 0)])


def shards(sizes, adapter_in, frozen, gain, adapter_a, adapter_up_matrix, passages, positive):
    nz, nyl, nx, nyh, nc = sizes
    ny = nyl * nyh
    iz, iyl, ix, iyh, ic = (lax.axis_index(axis) for axis in AXES)
    rank = adapter_up_matrix.shape[0]
    feats = passages.shape[1]
    half = nyh * feats
    width = half * nc
    queries = adapter_in.shape[0] // LEN
    group = passages.shape[0]
    rows = group // nyh

    sent = jnp.broadcast_to(passages.reshape(1, nyh, rows, feats), (nz, nyh, rows, feats))
    got = exchange(sent.reshape(nz * nyh, rows, feats), ("z", "yh"))
    got = got.reshape(nz, nyh, rows, feats).transpose(0, 2, 1, 3).reshape(nz * rows, half)
    got, adapter_a, adapter_up_matrix = lax.optimization_barrier(
        (got, adapter_a, adapter_up_matrix)
    )
    block = lax.all_gather(got, "x", axis=0, tiled=True)

    mine = jnp.where(iyl == 0, adapter_a.T, adapter_up_matrix)
    own = to_all(mine, ("yl", "yh"), ny).reshape(nyl, nyh, rank, feats)
    other = swap_cores(own)
    pair = jnp.where(ic == 0, jnp.stack([own, other]), jnp.stack([other, own]))
    whole = pair.transpose(1, 3, 2, 0, 4).reshape(nyl, rank, width)
    whole_a_t, full_up_matrix = whole[0], whole[1]

    latent_code = contracted_row_product(adapter_in, whole_a_t).astype(jnp.bfloat16)
    hidden_state = frozen.astype(jnp.float32) + adapter_scale_factor * jnp.dot(
        latent_code, full_up_matrix, preferred_element_type=jnp.float32
    )
    inv_rms = lax.rsqrt(jnp.mean(hidden_state * hidden_state, axis=-1, keepdims=True) + norm_eps)
    normed = hidden_state * inv_rms * gain
    pooled = jnp.mean(normed.reshape(queries, LEN, width), axis=1)
    length = jnp.sqrt(jnp.sum(pooled * pooled, axis=-1, keepdims=True))
    unit = pooled / length

    halves = unit.astype(jnp.bfloat16).reshape(queries, nyh, nc, feats).transpose(2, 0, 1, 3)
    halves = jnp.broadcast_to(halves.reshape(1, nc, queries, half), (ny, nc, queries, half))
    ring = ny * nc
    query_feat = exchange(halves.reshape(ring, queries, half), ("yl", "yh", "c"))
    query_feat = query_feat.reshape(ring * queries, half)

    part = contracted_row_product(query_feat, block)
    wide = block.astype(jnp.float32)
    squares = jnp.sum(wide * wide, axis=-1)
    both = jnp.concatenate([part, jnp.broadcast_to(squares[None], (8, squares.shape[0]))])
    both = both + swap_cores(both)
    count = ring * queries
    inv_norm = 1.0 / jnp.sqrt(both[count])
    scores = inv_temp * (both[:count] * inv_norm)
    expo = jnp.exp(scores - inv_temp)

    columns = block.shape[0]
    at = lax.iota(jnp.int32, columns)
    at_x, at_z, at_row = at // (nz * rows), at // rows % nz, at % rows
    passage_id = ((at_z * nyl + iyl) * nx + at_x) * group + iyh * rows + at_row
    own_pos = jnp.where(
        lax.iota(jnp.int32, nyl)[:, None] == iyl, positive[None, :], -1
    ).reshape(count)
    onehot = (own_pos[:, None] == passage_id[None, :]).astype(jnp.float32)

    row_sum = jnp.sum(to_all(jnp.sum(expo, axis=1), ("yl", "yh"), ny), axis=0)
    local_term = jnp.sum(jnp.log(row_sum)) / ny - 2.0 * jnp.sum(scores * onehot)
    sums = jnp.concatenate([jnp.sum(expo, axis=0), jnp.full((128,), local_term)])
    sums = jnp.sum(to_all(sums, ("z", "x"), nz * nx), axis=0)
    col_sum = sums[:columns]
    loss_term = sums[columns] + jnp.sum(jnp.log(col_sum))
    weights = 0.5 * (expo / row_sum[:, None] + expo / col_sum[None, :]) - onehot
    weights = (weights * inv_norm).astype(jnp.bfloat16)
    grad_feat = inv_temp * jnp.dot(weights, block, preferred_element_type=jnp.float32)
    grad_feat = grad_feat.astype(jnp.bfloat16).reshape(ring, queries, half)
    query_grad = exchange(grad_feat, ("yl", "yh", "c")).astype(jnp.float32)
    query_grad = jnp.sum(query_grad.reshape(ny, nc, queries, nyh, feats), axis=0)
    query_grad = query_grad.transpose(1, 2, 0, 3).reshape(queries, width)

    pooled_grad = (query_grad - unit * jnp.sum(unit * query_grad, axis=-1, keepdims=True)) / length
    normed_grad = jnp.repeat(pooled_grad / LEN, LEN, axis=0)
    scaled = normed_grad * gain
    hidden_state_gradient = (
        inv_rms * scaled
        - hidden_state * inv_rms**3 * jnp.mean(scaled * hidden_state, axis=-1, keepdims=True)
    ).astype(jnp.bfloat16)
    latent_code_gradient = (
        adapter_scale_factor * contracted_row_product(hidden_state_gradient, full_up_matrix)
    ).astype(jnp.bfloat16)
    grad_a_t = jnp.dot(latent_code_gradient.T, adapter_in, preferred_element_type=jnp.float32)
    up_matrix_gradient = adapter_scale_factor * jnp.dot(
        latent_code.T, hidden_state_gradient, preferred_element_type=jnp.float32
    )
    out_rows = rank // (nyh * nc)
    cols = width // (nz * nyl * nx)
    stacked = jnp.stack([grad_a_t, up_matrix_gradient]).astype(jnp.bfloat16)
    stacked = stacked.reshape(2, nyh, nc, out_rows, nz, nyl, nx, cols)
    stacked = stacked.transpose(2, 6, 4, 5, 1, 0, 3, 7).reshape(
        nc, nx, nz * ny, 2 * out_rows, cols
    )
    keep = lax.dynamic_index_in_dim(stacked, ic, 0, keepdims=False)
    send = lax.dynamic_index_in_dim(stacked, 1 - ic, 0, keepdims=False)
    chip = (keep.astype(jnp.float32) + swap_cores(send).astype(jnp.float32)).astype(jnp.bfloat16)
    line = jnp.sum(exchange(chip, "x").astype(jnp.float32), axis=0)
    line = jnp.concatenate(
        [line, jnp.broadcast_to(loss_term, (line.shape[0], 8, cols))], axis=1
    )
    last = jnp.sum(exchange(line, ("z", "yl", "yh")), axis=0)
    adapter_grads = last[: 2 * out_rows].reshape(2, out_rows, cols)
    total_pairs = group * nz * nyl * nx
    loss = last[2 * out_rows, 0] / nz / (2.0 * total_pairs) + inv_temp
    return (adapter_grads, loss)


def build(mesh, sizes):
    split = Mesh(mesh.devices.reshape(sizes), AXES)
    dp, fsdp = ("z", "yl", "x"), ("yh", "c")
    placed = (
        P(AXES, None),
        P(AXES, None),
        P(),
        P(fsdp, None),
        P(None, fsdp),
        P(dp, fsdp),
        P(dp),
    )
    return jax.shard_map(
        lambda *args: shards(sizes, *args),
        mesh=split,
        in_specs=placed,
        out_specs=(P(None, fsdp, dp), P()),
        check_vma=False,
    )


def solution(mesh):
    return build(mesh, SIZES)
```

```python
import functools

import jax
import jax.numpy as jnp
from jax import lax
from jax.experimental import pallas as pl
from jax.experimental.pallas import tpu as pltpu
from jax.sharding import Mesh
from jax.sharding import PartitionSpec as P

LEN = 32


adapter_scale_factor = 0.25
inv_temp = 20.0
norm_eps = 1e-05

AXES = ("z", "yl", "x", "yh", "c")
SIZES = (4, 2, 8, 4, 2)
MIB = 1 << 20
f32, bf16 = jnp.float32, jnp.bfloat16


def dot(left, right):
    return jnp.dot(left, right, preferred_element_type=f32)


def dot_rows(left, right):
    return lax.dot_general(left, right, (((1,), (1,)), ((), ())), preferred_element_type=f32)


def exchange(blocks, axes):
    return lax.all_to_all(blocks, axes, 0, 0, tiled=True)


def swap_cores(value):
    return lax.ppermute(value, "c", [(0, 1), (1, 0)])


def call(kernel, outs, args, scratch=(), scalars=0, flops=0):
    size = sum(a.size * a.dtype.itemsize for a in list(args[scalars:]) + list(outs))
    spare = [pltpu.VMEM(shape, kind) for shape, kind in scratch]
    spare_size = sum(a.size * a.dtype.itemsize for a in map(shape_of, scratch))
    return pl.pallas_call(
        kernel,
        out_shape=outs,
        in_specs=[pl.BlockSpec(memory_space=pltpu.SMEM)] * scalars
        + [pl.BlockSpec(memory_space=pltpu.VMEM)] * (len(args) - scalars),
        out_specs=[pl.BlockSpec(memory_space=pltpu.VMEM)] * len(outs),
        scratch_shapes=spare,
        compiler_params=pltpu.CompilerParams(
            vmem_limit_bytes=min(48 * MIB, size + spare_size + 12 * MIB)
        ),
        cost_estimate=pl.CostEstimate(flops=flops, bytes_accessed=size, transcendentals=0),
    )(*args)


def shape_of(pair):
    return jax.ShapeDtypeStruct(*pair)


def forward(nyh, nc, in_ref, frozen_ref, gain_ref, mats_ref,
            latent_ref, hidden_ref, inv_ref, unit_ref, length_ref, send_ref, part_ref):
    slices, both, feats = mats_ref.shape
    rank = both // 2
    tokens, width = in_ref.shape
    queries = tokens // LEN
    acc = jnp.zeros((tokens, rank), f32)
    acc_t = jnp.zeros((rank, tokens), f32)
    for f in range(slices):
        part = in_ref[:, f * feats:(f + 1) * feats]
        down = mats_ref[f, :rank]
        acc += dot_rows(part, down)
        acc_t += dot_rows(down, part)
    latent = acc.astype(bf16)
    latent_ref[...] = acc_t.astype(bf16)
    squares = jnp.zeros((tokens, 1), f32)
    for f in range(slices):
        at = slice(f * feats, (f + 1) * feats)
        hidden = frozen_ref[:, at].astype(f32) + adapter_scale_factor * dot(
            latent, mats_ref[f, rank:]
        )
        hidden_ref[:, at] = hidden
        squares += jnp.sum(hidden * hidden, axis=1, keepdims=True)
    inv = lax.rsqrt(squares / width + norm_eps)
    inv_ref[...] = jnp.broadcast_to(inv, inv_ref.shape)
    total = jnp.zeros((queries, 1), f32)
    for f in range(slices):
        at = slice(f * feats, (f + 1) * feats)
        scaled = hidden_ref[:, at] * inv
        for q in range(queries):
            one = jnp.sum(scaled[q * LEN:(q + 1) * LEN], axis=0, keepdims=True)
            unit_ref[q:q + 1, at] = one * gain_ref[:, at] / LEN
        pooled = unit_ref[:, at]
        total += jnp.sum(pooled * pooled, axis=1, keepdims=True)
    length = jnp.sqrt(total)
    length_ref[...] = jnp.broadcast_to(length, length_ref.shape)
    for f in range(slices):
        at = slice(f * feats, (f + 1) * feats)
        unit = unit_ref[:, at] / length
        unit_ref[:, at] = unit
        part_ref[f % nc, f // nc * queries:(f // nc + 1) * queries, :] = unit
    for c in range(nc):
        rows = part_ref[c].astype(bf16)
        for y in range(send_ref.shape[0] // nc):
            send_ref[y * nc + c] = rows


def row_index(shape):
    return lax.broadcasted_iota(jnp.int32, shape, 0)


def score(nyh, query_ref, block_ref, out_ref):
    ring, rows, feats = query_ref.shape
    queries = rows // nyh
    columns = block_ref.shape[0]
    query = query_ref[...].reshape(ring * rows, feats)
    mine = row_index((ring * rows, columns)) // queries % nyh
    total = jnp.zeros((ring * rows, columns), f32)
    gram = jnp.zeros((columns, columns), f32)
    for k in range(nyh):
        part = block_ref[:, k * feats:(k + 1) * feats]
        total = jnp.where(mine == k, dot_rows(query, part), total)
        gram += dot_rows(part, part)
    total = total.reshape(ring, rows // 8, 8, columns)
    total = functools.reduce(jnp.add, [total[:, i] for i in range(rows // 8)])
    total = total.reshape(ring * 8, columns)
    count = ring * 8
    upper = row_index(total.shape) % 8 < 4
    total += jnp.where(upper, pltpu.roll(total, count - 4, 0), pltpu.roll(total, 4, 0))
    same = row_index(gram.shape) == lax.broadcasted_iota(jnp.int32, gram.shape, 1)
    norms = jnp.sum(jnp.where(same, gram, 0.0), axis=0, keepdims=True)
    out_ref[:count] = total
    out_ref[count:] = jnp.broadcast_to(norms, (8, columns))


def across(row):
    n = row.size
    return jnp.transpose(jnp.broadcast_to(row, (n, n)))


def widen(row, lanes):
    if row.shape[1] == lanes:
        return row
    return jnp.concatenate([row, jnp.zeros((1, lanes - row.shape[1]), f32)], axis=1)


def exponentials(members, iy_ref, own_ref, other_ref, onehot_ref, expo_ref, aux_ref, send_ref):
    count = expo_ref.shape[0]
    columns = expo_ref.shape[1]
    inv_norm = 1.0 / jnp.sqrt(own_ref[count:count + 1] + other_ref[count:count + 1])
    scores = inv_temp * ((own_ref[:count] + other_ref[:count]) * inv_norm)
    expo = jnp.exp(scores - inv_temp)
    expo_ref[...] = expo
    hits = 0.5 * jnp.sum(scores * onehot_ref[...])
    aux_ref[0:1] = inv_norm
    aux_ref[1:2] = jnp.full((1, columns), hits)
    row = across(jnp.sum(expo, axis=1, keepdims=True))[0:1]
    row = widen(row, send_ref.shape[1])
    col = widen(0.5 * jnp.sum(expo, axis=0, keepdims=True), send_ref.shape[1])
    same_y = row_index(send_ref.shape) // members == iy_ref[0]
    send_ref[...] = jnp.where(same_y, col, row)


def weigh(nyh, members, iy_ref, ixz_ref, expo_ref, aux_ref, onehot_ref, sums_ref, block_ref,
          out_ref, loss_ref, total_ref):
    count, columns = expo_ref.shape
    ring, rows, feats = out_ref.shape
    queries = rows // nyh
    sums = sums_ref[...]
    peer = row_index(sums.shape)
    same_y = peer // members == iy_ref[0]
    col = jnp.sum(jnp.where(same_y, sums, 0.0), axis=0, keepdims=True)[:, :columns]
    same_xz = jnp.logical_and(peer % members == ixz_ref[0], jnp.logical_not(same_y))
    rest = jnp.sum(jnp.where(same_xz, sums, 0.0), axis=0, keepdims=True)[:, :count]
    expo = expo_ref[...]
    row = across(rest)[:, :1] + jnp.sum(expo, axis=1, keepdims=True)
    peers = sums.shape[0]
    loss = (
        0.5 * jnp.sum(jnp.log(row), axis=0, keepdims=True) / (peers // members)
        + jnp.sum(jnp.log(col), axis=1, keepdims=True) / members
        - 2.0 * aux_ref[1:2, 0:1]
    )
    loss_ref[...] = jnp.broadcast_to(loss, loss_ref.shape)
    weights = 0.5 * (expo / row + expo / col) - onehot_ref[...]
    weights = (weights * aux_ref[0:1]).reshape(ring, 1, 8, columns)
    weights = jnp.broadcast_to(weights, (ring, rows // 8, 8, columns))
    weights = weights.reshape(ring * rows, columns).astype(bf16)
    mine = row_index((ring * rows, feats)) // queries % nyh
    for k in range(nyh):
        part = inv_temp * dot(weights, block_ref[:, k * feats:(k + 1) * feats])
        if k == 0:
            total_ref[...] = part
        else:
            total_ref[...] = jnp.where(mine == k, part, total_ref[...])
    out_ref[...] = total_ref[...].astype(bf16).reshape(out_ref.shape)


def backward(nyh, nc, core_ref, got_ref, unit_ref, length_ref, inv_ref, hidden_ref, gain_ref,
             in_ref, mats_ref, latent_ref, keep_ref, send_ref, grad_ref, scaled_ref, up_ref, hg_ref):
    slices, both, feats = mats_ref.shape
    rank = both // 2
    tokens, width = in_ref.shape
    queries = tokens // LEN
    nx, _, pair_rows, cols = keep_ref.shape
    out_rows = pair_rows // 2
    for c in range(nc):
        total = got_ref[c].astype(f32)
        for y in range(1, got_ref.shape[0] // nc):
            total += got_ref[y * nc + c].astype(f32)
        grad_ref[c] = total
    inner = jnp.zeros((queries, 1), f32)
    for f in range(slices):
        at = slice(f * feats, (f + 1) * feats)
        grad = grad_ref[f % nc, f // nc * queries:(f // nc + 1) * queries, :]
        inner += jnp.sum(unit_ref[:, at] * grad, axis=1, keepdims=True)
    length = length_ref[:, :1]
    mean = [jnp.zeros((LEN, 1), f32) for q in range(queries)]
    for f in range(slices):
        at = slice(f * feats, (f + 1) * feats)
        grad = grad_ref[f % nc, f // nc * queries:(f // nc + 1) * queries, :]
        pooled_grad = (grad - unit_ref[:, at] * inner) / length
        scaled_ref[:, at] = pooled_grad / LEN * gain_ref[:, at]
        for q in range(queries):
            product = hidden_ref[q * LEN:(q + 1) * LEN, at] * scaled_ref[q:q + 1, at]
            mean[q] += jnp.sum(product, axis=1, keepdims=True)
    inv = inv_ref[:, :1]
    factor = inv * inv * inv * (jnp.concatenate(mean, axis=0) / width)
    latent_t = latent_ref[...]
    acc = jnp.zeros((rank, tokens), f32)
    for f in range(slices):
        at = slice(f * feats, (f + 1) * feats)
        for q in range(queries):
            of = slice(q * LEN, (q + 1) * LEN)
            hg_ref[of] = (
                inv[of] * scaled_ref[q:q + 1, at] - hidden_ref[of, at] * factor[of]
            ).astype(bf16)
        hidden_grad = hg_ref[...]
        acc += dot_rows(mats_ref[f, rank:], hidden_grad)
        up_ref[:, at] = adapter_scale_factor * dot(latent_t, hidden_grad)
    latent_grad = (adapter_scale_factor * acc).astype(bf16)
    first = core_ref[0] == 0
    for f in range(slices):
        down = dot(latent_grad, in_ref[:, f * feats:(f + 1) * feats])
        for x in range(nx):
            lanes = slice(x * cols, (x + 1) * cols)
            spot = slice(f * feats + x * cols, f * feats + (x + 1) * cols)
            for yh in range(nyh):
                tiles = []
                for c in range(nc):
                    of = slice((yh * nc + c) * out_rows, (yh * nc + c + 1) * out_rows)
                    tiles.append(
                        jnp.concatenate([down[of, lanes], up_ref[of, spot]], axis=0).astype(bf16)
                    )
                keep_ref[x, f * nyh + yh] = jnp.where(first, tiles[0], tiles[1])
                send_ref[x, f * nyh + yh] = jnp.where(first, tiles[1], tiles[0])


def join(keep_ref, got_ref, loss_ref, out_ref):
    nx, blocks, rows, cols = keep_ref.shape
    high = loss_ref[0:1].astype(bf16).astype(f32)
    rest = loss_ref[0:1] - high
    middle = rest.astype(bf16).astype(f32)
    low = rest - middle
    at = row_index((rows, loss_ref.shape[1]))
    parts = jnp.where(at == 0, high, jnp.where(at == 1, middle, jnp.where(at == 2, low, 0.0)))
    parts = jnp.concatenate([parts] * (cols // loss_ref.shape[1]), axis=1).astype(bf16)
    for x in range(nx):
        out_ref[x, :blocks] = (
            keep_ref[x].astype(f32) + got_ref[x].astype(f32)
        ).astype(bf16)
        out_ref[x, blocks] = parts


def add_line(got_ref, out_ref):
    total = got_ref[0].astype(f32)
    for x in range(1, got_ref.shape[0]):
        total += got_ref[x].astype(f32)
    blocks, _, cols = out_ref.shape
    rows = got_ref.shape[2]
    loss = jnp.sum(total[blocks], axis=0, keepdims=True)
    out_ref[:, :rows] = total[:blocks]
    out_ref[:, rows:] = jnp.broadcast_to(loss[None], (blocks, 8, cols))


def shards(sizes, adapter_in, frozen, gain, adapter_a, adapter_up_matrix, passages, positive):
    nz, nyl, nx, nyh, nc = sizes
    ny = nyl * nyh
    iz, iyl, ix, iyh, ic = (lax.axis_index(axis) for axis in AXES)
    rank = adapter_up_matrix.shape[0]
    feats = passages.shape[1]
    half = nyh * feats
    width = half * nc
    tokens = adapter_in.shape[0]
    queries = tokens // LEN
    group = passages.shape[0]
    rows = group // nyh
    ring = ny * nc
    members = nz * nx
    shape = jax.ShapeDtypeStruct
    gain = gain.reshape(1, width)

    mine = jnp.concatenate([adapter_a.T, adapter_up_matrix], axis=0)
    mats = lax.all_gather(mine, ("yh", "c"), axis=0, tiled=False)

    sent = jnp.broadcast_to(passages.reshape(1, nyh, rows, feats), (nz, nyh, rows, feats))
    got = exchange(sent.reshape(nz * nyh, rows, feats), ("z", "yh"))
    got = got.reshape(nz, nyh, rows, feats).transpose(0, 2, 1, 3).reshape(nz * rows, half)
    got = jnp.broadcast_to(got[None], (nx, nz * rows, half))
    block = exchange(got, "x").reshape(nx * nz * rows, half)
    columns = block.shape[0]

    latent_t, hidden, inv, unit, length, sent = call(
        functools.partial(forward, nyh, nc),
        [
            shape((rank, tokens), bf16),
            shape((tokens, width), f32),
            shape((tokens, 128), f32),
            shape((queries, width), f32),
            shape((queries, 128), f32),
            shape((ring, nyh * queries, feats), bf16),
        ],
        [adapter_in, frozen, gain, mats],
        scratch=[((nc, nyh * queries, feats), f32)],
        flops=6 * tokens * rank * width,
    )
    query = exchange(sent, ("yl", "yh", "c"))

    count = ring * 8
    at = lax.iota(jnp.int32, columns)
    at_x, at_z, at_row = at // (nz * rows), at // rows % nz, at % rows
    passage_id = ((at_z * nyl + iyl) * nx + at_x) * group + iyh * rows + at_row
    own_pos = jnp.where(
        lax.iota(jnp.int32, nyl)[:, None] == iyl, positive[None, :], -1
    ).reshape(ring, 1, queries)
    own_pos = jnp.broadcast_to(own_pos, (ring, 8 // queries, queries)).reshape(count)
    onehot = (own_pos[:, None] == passage_id[None, :]).astype(f32)
    iy = (iyl * nyh + iyh).astype(jnp.int32).reshape(1)
    ixz = (iz * nx + ix).astype(jnp.int32).reshape(1)

    (own,) = call(
        functools.partial(score, nyh),
        [shape((count + 8, columns), f32)],
        [query, block],
        flops=4 * ring * nyh * queries * columns * half,
    )
    other = swap_cores(own)
    expo, aux, sent = call(
        functools.partial(exponentials, members),
        [shape((count, columns), f32), shape((8, columns), f32), shape((ny * members, max(columns, count)), f32)],
        [iy, own, other, onehot],
        scalars=1,
    )
    sums = exchange(sent, ("yl", "yh", "z", "x"))
    sent, loss = call(
        functools.partial(weigh, nyh, members),
        [shape((ring, nyh * queries, feats), bf16), shape((8, 128), f32)],
        [iy, ixz, expo, aux, onehot, sums, block],
        scratch=[((ring * nyh * queries, feats), f32)],
        scalars=2,
        flops=2 * ring * nyh * queries * columns * half,
    )
    got = exchange(sent, ("yl", "yh", "c"))

    out_rows = rank // (nyh * nc)
    cols = width // (nz * nyl * nx)
    blocks = nz * ny
    keep, send = call(
        functools.partial(backward, nyh, nc),
        [shape((nx, blocks, 2 * out_rows, cols), bf16)] * 2,
        [ic.astype(jnp.int32).reshape(1), got, unit, length, inv, hidden, gain, adapter_in, mats, latent_t],
        scratch=[
            ((nc, nyh * queries, feats), f32),
            ((queries, width), f32),
            ((rank, width), f32),
            ((tokens, feats), bf16),
        ],
        scalars=1,
        flops=6 * tokens * rank * width,
    )
    (chip,) = call(
        join,
        [shape((nx, blocks + 1, 2 * out_rows, cols), bf16)],
        [keep, swap_cores(send), loss],
    )
    (line,) = call(
        add_line, [shape((blocks, 2 * out_rows + 8, cols), f32)], [exchange(chip, "x")]
    )
    last = jnp.sum(exchange(line, ("z", "yl", "yh")), axis=0)
    adapter_grads = last[: 2 * out_rows].reshape(2, out_rows, cols)
    total_pairs = group * nz * nyl * nx
    loss = last[2 * out_rows, 0] / (2.0 * total_pairs) + inv_temp
    return (adapter_grads, loss)


def build(mesh, sizes):
    split = Mesh(mesh.devices.reshape(sizes), AXES)
    dp, fsdp = ("z", "yl", "x"), ("yh", "c")
    placed = (
        P(AXES, None),
        P(AXES, None),
        P(),
        P(fsdp, None),
        P(None, fsdp),
        P(dp, fsdp),
        P(dp),
    )
    return jax.shard_map(
        lambda *args: shards(sizes, *args),
        mesh=split,
        in_specs=placed,
        out_specs=(P(None, fsdp, dp), P()),
        check_vma=False,
    )


def solution(mesh):
    return build(mesh, SIZES)
```

```python
import functools

import jax
import jax.numpy as jnp
from jax import lax
from jax.experimental import pallas as pl
from jax.experimental.pallas import tpu as pltpu
from jax.sharding import Mesh
from jax.sharding import PartitionSpec as P

LEN = 32


adapter_scale_factor = 0.25
inv_temp = 20.0
norm_eps = 1e-05

AXES = ("z", "yl", "x", "yh", "c")
SIZES = (4, 2, 8, 4, 2)
MIB = 1 << 20
f32, bf16 = jnp.float32, jnp.bfloat16


def dot(left, right):
    return jnp.dot(left, right, preferred_element_type=f32)


def dot_rows(left, right):
    return lax.dot_general(left, right, (((1,), (1,)), ((), ())), preferred_element_type=f32)


def exchange(blocks, axes):
    return lax.all_to_all(blocks, axes, 0, 0, tiled=True)


def swap_cores(value):
    return lax.ppermute(value, "c", [(0, 1), (1, 0)])


def call(kernel, outs, args, scratch=(), scalars=0, flops=0):
    size = sum(a.size * a.dtype.itemsize for a in list(args[scalars:]) + list(outs))
    spare = [pltpu.VMEM(shape, kind) for shape, kind in scratch]
    spare_size = sum(a.size * a.dtype.itemsize for a in map(shape_of, scratch))
    return pl.pallas_call(
        kernel,
        out_shape=outs,
        in_specs=[pl.BlockSpec(memory_space=pltpu.SMEM)] * scalars
        + [pl.BlockSpec(memory_space=pltpu.VMEM)] * (len(args) - scalars),
        out_specs=[pl.BlockSpec(memory_space=pltpu.VMEM)] * len(outs),
        scratch_shapes=spare,
        compiler_params=pltpu.CompilerParams(
            vmem_limit_bytes=spare_size + 8 * MIB
        ),
        cost_estimate=pl.CostEstimate(flops=flops, bytes_accessed=size, transcendentals=0),
    )(*args)


def shape_of(pair):
    return jax.ShapeDtypeStruct(*pair)


def adapter_slices(place_ref, own_ref, other_ref):
    nyh, _, feats = own_ref.shape
    for k in range(nyh):
        for ref, core in ((own_ref, place_ref[1]), (other_ref, 1 - place_ref[1])):
            at = (lax.rem(place_ref[0] + k, nyh) * 2 + core) * feats
            yield ref.at[k], pl.ds(pl.multiple_of(at, feats), feats)


def forward(nyh, nc, place_ref, in_ref, frozen_ref, gain_ref, own_ref, other_ref,
            latent_ref, hidden_ref, inv_ref, unit_ref, length_ref, send_ref, part_ref):
    _, both, feats = own_ref.shape
    slices = nyh * nc
    rank = both // 2
    tokens, width = in_ref.shape
    queries = tokens // LEN
    acc = jnp.zeros((tokens, rank), f32)
    acc_t = jnp.zeros((rank, tokens), f32)
    for mats_ref, at in adapter_slices(place_ref, own_ref, other_ref):
        part = in_ref[:, at]
        down = mats_ref[:rank]
        acc += dot_rows(part, down)
        acc_t += dot_rows(down, part)
    latent = acc.astype(bf16)
    latent_ref[...] = acc_t.astype(bf16)
    squares = jnp.zeros((tokens, 1), f32)
    for mats_ref, at in adapter_slices(place_ref, own_ref, other_ref):
        hidden = frozen_ref[:, at].astype(f32) + adapter_scale_factor * dot(
            latent, mats_ref[rank:]
        )
        hidden_ref[:, at] = hidden
        squares += jnp.sum(hidden * hidden, axis=1, keepdims=True)
    inv = lax.rsqrt(squares / width + norm_eps)
    inv_ref[...] = jnp.broadcast_to(inv, inv_ref.shape)
    total = jnp.zeros((queries, 1), f32)
    for f in range(slices):
        at = slice(f * feats, (f + 1) * feats)
        scaled = hidden_ref[:, at] * inv
        for q in range(queries):
            one = jnp.sum(scaled[q * LEN:(q + 1) * LEN], axis=0, keepdims=True)
            unit_ref[q:q + 1, at] = one * gain_ref[:, at] / LEN
        pooled = unit_ref[:, at]
        total += jnp.sum(pooled * pooled, axis=1, keepdims=True)
    length = jnp.sqrt(total)
    length_ref[...] = jnp.broadcast_to(length, length_ref.shape)
    for f in range(slices):
        at = slice(f * feats, (f + 1) * feats)
        unit = unit_ref[:, at] / length
        unit_ref[:, at] = unit
        part_ref[f % nc, f // nc * queries:(f // nc + 1) * queries, :] = unit
    for c in range(nc):
        rows = part_ref[c].astype(bf16)
        for y in range(send_ref.shape[0] // nc):
            send_ref[y * nc + c] = rows


def row_index(shape):
    return lax.broadcasted_iota(jnp.int32, shape, 0)


def score(nyh, query_ref, block_ref, out_ref):
    ring, rows, feats = query_ref.shape
    queries = rows // nyh
    columns = block_ref.shape[0]
    query = query_ref[...].reshape(ring * rows, feats)
    mine = row_index((ring * rows, columns)) // queries % nyh
    total = jnp.zeros((ring * rows, columns), f32)
    gram = jnp.zeros((columns, columns), f32)
    for k in range(nyh):
        part = block_ref[:, k * feats:(k + 1) * feats]
        total = jnp.where(mine == k, dot_rows(query, part), total)
        gram += dot_rows(part, part)
    total = total.reshape(ring, rows // 8, 8, columns)
    total = functools.reduce(jnp.add, [total[:, i] for i in range(rows // 8)])
    total = total.reshape(ring * 8, columns)
    count = ring * 8
    upper = row_index(total.shape) % 8 < 4
    total += jnp.where(upper, pltpu.roll(total, count - 4, 0), pltpu.roll(total, 4, 0))
    same = row_index(gram.shape) == lax.broadcasted_iota(jnp.int32, gram.shape, 1)
    norms = jnp.sum(jnp.where(same, gram, 0.0), axis=0, keepdims=True)
    out_ref[:count] = total
    out_ref[count:] = jnp.broadcast_to(norms, (8, columns))


def across(row):
    n = row.size
    return jnp.transpose(jnp.broadcast_to(row, (n, n)))


def widen(row, lanes):
    if row.shape[1] == lanes:
        return row
    return jnp.concatenate([row, jnp.zeros((1, lanes - row.shape[1]), f32)], axis=1)


def exponentials(members, iy_ref, own_ref, other_ref, onehot_ref, expo_ref, aux_ref, send_ref):
    count = expo_ref.shape[0]
    columns = expo_ref.shape[1]
    inv_norm = 1.0 / jnp.sqrt(own_ref[count:count + 1] + other_ref[count:count + 1])
    scores = inv_temp * ((own_ref[:count] + other_ref[:count]) * inv_norm)
    expo = jnp.exp(scores - inv_temp)
    expo_ref[...] = expo
    hits = 0.5 * jnp.sum(scores * onehot_ref[...])
    aux_ref[0:1] = inv_norm
    aux_ref[1:2] = jnp.full((1, columns), hits)
    row = across(jnp.sum(expo, axis=1, keepdims=True))[0:1]
    row = widen(row, send_ref.shape[1])
    col = widen(0.5 * jnp.sum(expo, axis=0, keepdims=True), send_ref.shape[1])
    same_y = row_index(send_ref.shape) // members == iy_ref[0]
    send_ref[...] = jnp.where(same_y, col, row)


def weigh(nyh, members, iy_ref, ixz_ref, expo_ref, aux_ref, onehot_ref, sums_ref, block_ref,
          out_ref, loss_ref, total_ref):
    count, columns = expo_ref.shape
    ring, rows, feats = out_ref.shape
    queries = rows // nyh
    sums = sums_ref[...]
    peer = row_index(sums.shape)
    same_y = peer // members == iy_ref[0]
    col = jnp.sum(jnp.where(same_y, sums, 0.0), axis=0, keepdims=True)[:, :columns]
    same_xz = jnp.logical_and(peer % members == ixz_ref[0], jnp.logical_not(same_y))
    rest = jnp.sum(jnp.where(same_xz, sums, 0.0), axis=0, keepdims=True)[:, :count]
    expo = expo_ref[...]
    row = across(rest)[:, :1] + jnp.sum(expo, axis=1, keepdims=True)
    peers = sums.shape[0]
    loss = (
        0.5 * jnp.sum(jnp.log(row), axis=0, keepdims=True) / (peers // members)
        + jnp.sum(jnp.log(col), axis=1, keepdims=True) / members
        - 2.0 * aux_ref[1:2, 0:1]
    )
    loss_ref[...] = jnp.broadcast_to(loss, loss_ref.shape)
    weights = 0.5 * (expo / row + expo / col) - onehot_ref[...]
    weights = (weights * aux_ref[0:1]).reshape(ring, 1, 8, columns)
    weights = jnp.broadcast_to(weights, (ring, rows // 8, 8, columns))
    weights = weights.reshape(ring * rows, columns).astype(bf16)
    mine = row_index((ring * rows, feats)) // queries % nyh
    for k in range(nyh):
        part = inv_temp * dot(weights, block_ref[:, k * feats:(k + 1) * feats])
        if k == 0:
            total_ref[...] = part
        else:
            total_ref[...] = jnp.where(mine == k, part, total_ref[...])
    out_ref[...] = total_ref[...].astype(bf16).reshape(out_ref.shape)


def backward(nyh, nc, place_ref, got_ref, unit_ref, length_ref, inv_ref, hidden_ref, gain_ref,
             in_ref, own_ref, other_ref, latent_ref, keep_ref, send_ref,
             grad_ref, scaled_ref, up_ref, hg_ref):
    _, both, feats = own_ref.shape
    slices = nyh * nc
    rank = both // 2
    tokens, width = in_ref.shape
    queries = tokens // LEN
    nx, _, pair_rows, cols = keep_ref.shape
    out_rows = pair_rows // 2
    for c in range(nc):
        total = got_ref[c].astype(f32)
        for y in range(1, got_ref.shape[0] // nc):
            total += got_ref[y * nc + c].astype(f32)
        grad_ref[c] = total
    inner = jnp.zeros((queries, 1), f32)
    for f in range(slices):
        at = slice(f * feats, (f + 1) * feats)
        grad = grad_ref[f % nc, f // nc * queries:(f // nc + 1) * queries, :]
        inner += jnp.sum(unit_ref[:, at] * grad, axis=1, keepdims=True)
    length = length_ref[:, :1]
    mean = [jnp.zeros((LEN, 1), f32) for q in range(queries)]
    for f in range(slices):
        at = slice(f * feats, (f + 1) * feats)
        grad = grad_ref[f % nc, f // nc * queries:(f // nc + 1) * queries, :]
        pooled_grad = (grad - unit_ref[:, at] * inner) / length
        scaled_ref[:, at] = pooled_grad / LEN * gain_ref[:, at]
        for q in range(queries):
            product = hidden_ref[q * LEN:(q + 1) * LEN, at] * scaled_ref[q:q + 1, at]
            mean[q] += jnp.sum(product, axis=1, keepdims=True)
    inv = inv_ref[:, :1]
    factor = inv * inv * inv * (jnp.concatenate(mean, axis=0) / width)
    latent_t = latent_ref[...]
    acc = jnp.zeros((rank, tokens), f32)
    for mats_ref, at in adapter_slices(place_ref, own_ref, other_ref):
        for q in range(queries):
            of = slice(q * LEN, (q + 1) * LEN)
            hg_ref[of] = (
                inv[of] * scaled_ref[q:q + 1, at] - hidden_ref[of, at] * factor[of]
            ).astype(bf16)
        hidden_grad = hg_ref[...]
        acc += dot_rows(mats_ref[rank:], hidden_grad)
        up_ref[:, at] = adapter_scale_factor * dot(latent_t, hidden_grad)
    latent_grad = (adapter_scale_factor * acc).astype(bf16)
    first = place_ref[1] == 0
    for f in range(slices):
        down = dot(latent_grad, in_ref[:, f * feats:(f + 1) * feats])
        for x in range(nx):
            lanes = slice(x * cols, (x + 1) * cols)
            spot = slice(f * feats + x * cols, f * feats + (x + 1) * cols)
            for yh in range(nyh):
                tiles = []
                for c in range(nc):
                    of = slice((yh * nc + c) * out_rows, (yh * nc + c + 1) * out_rows)
                    tiles.append(
                        jnp.concatenate([down[of, lanes], up_ref[of, spot]], axis=0).astype(bf16)
                    )
                keep_ref[x, f * nyh + yh] = jnp.where(first, tiles[0], tiles[1])
                send_ref[x, f * nyh + yh] = jnp.where(first, tiles[1], tiles[0])


def join(keep_ref, got_ref, loss_ref, out_ref):
    nx, blocks, rows, cols = keep_ref.shape
    high = loss_ref[0:1].astype(bf16).astype(f32)
    rest = loss_ref[0:1] - high
    middle = rest.astype(bf16).astype(f32)
    low = rest - middle
    at = row_index((rows, loss_ref.shape[1]))
    parts = jnp.where(at == 0, high, jnp.where(at == 1, middle, jnp.where(at == 2, low, 0.0)))
    parts = jnp.concatenate([parts] * (cols // loss_ref.shape[1]), axis=1).astype(bf16)
    for x in range(nx):
        out_ref[x, :blocks] = (
            keep_ref[x].astype(f32) + got_ref[x].astype(f32)
        ).astype(bf16)
        out_ref[x, blocks] = parts


def add_line(got_ref, out_ref):
    total = got_ref[0].astype(f32)
    for x in range(1, got_ref.shape[0]):
        total += got_ref[x].astype(f32)
    blocks, _, cols = out_ref.shape
    rows = got_ref.shape[2]
    loss = jnp.sum(total[blocks], axis=0, keepdims=True)
    out_ref[:, :rows] = total[:blocks]
    out_ref[:, rows:] = jnp.broadcast_to(loss[None], (blocks, 8, cols))


def shards(sizes, adapter_in, frozen, gain, adapter_a, adapter_up_matrix, passages, positive):
    nz, nyl, nx, nyh, nc = sizes
    ny = nyl * nyh
    iz, iyl, ix, iyh, ic = (lax.axis_index(axis) for axis in AXES)
    rank = adapter_up_matrix.shape[0]
    feats = passages.shape[1]
    half = nyh * feats
    width = half * nc
    tokens = adapter_in.shape[0]
    queries = tokens // LEN
    group = passages.shape[0]
    rows = group // nyh
    ring = ny * nc
    members = nz * nx
    shape = jax.ShapeDtypeStruct
    gain = gain.reshape(1, width)

    sent = jnp.broadcast_to(passages.reshape(1, nyh, rows, feats), (nz, nyh, rows, feats))
    got = exchange(sent.reshape(nz * nyh, rows, feats), ("z", "yh"))
    got = got.reshape(nz, nyh, rows, feats).transpose(0, 2, 1, 3).reshape(nz * rows, half)

    mine = jnp.concatenate([adapter_a.T, adapter_up_matrix], axis=0)
    pieces = [mine]
    for k in range(1, nyh):
        flip = 2 * k == nyh
        pairs = []
        for yl in range(nyl):
            for yh in range(nyh):
                source = (nyl - 1 - yl if flip else yl) * nyh + (yh + k) % nyh
                pairs.append((source, yl * nyh + yh))
        pieces.append(lax.ppermute(mine, ("yl", "yh"), pairs))
    own_mats, got = lax.optimization_barrier((jnp.stack(pieces), got))
    other_mats = swap_cores(own_mats)
    place = jnp.stack([iyh, ic]).astype(jnp.int32)

    got = jnp.broadcast_to(got[None], (nx, nz * rows, half))
    block = exchange(got, "x").reshape(nx * nz * rows, half)
    columns = block.shape[0]

    latent_t, hidden, inv, unit, length, sent = call(
        functools.partial(forward, nyh, nc),
        [
            shape((rank, tokens), bf16),
            shape((tokens, width), f32),
            shape((tokens, 128), f32),
            shape((queries, width), f32),
            shape((queries, 128), f32),
            shape((ring, nyh * queries, feats), bf16),
        ],
        [place, adapter_in, frozen, gain, own_mats, other_mats],
        scratch=[((nc, nyh * queries, feats), f32)],
        scalars=1,
        flops=6 * tokens * rank * width,
    )
    sent, block = lax.optimization_barrier((sent, block))
    query = exchange(sent, ("yl", "yh", "c"))

    count = ring * 8
    at = lax.iota(jnp.int32, columns)
    at_x, at_z, at_row = at // (nz * rows), at // rows % nz, at % rows
    passage_id = ((at_z * nyl + iyl) * nx + at_x) * group + iyh * rows + at_row
    own_pos = jnp.where(
        lax.iota(jnp.int32, nyl)[:, None] == iyl, positive[None, :], -1
    ).reshape(ring, 1, queries)
    own_pos = jnp.broadcast_to(own_pos, (ring, 8 // queries, queries)).reshape(count)
    onehot = (own_pos[:, None] == passage_id[None, :]).astype(f32)
    iy = (iyl * nyh + iyh).astype(jnp.int32).reshape(1)
    ixz = (iz * nx + ix).astype(jnp.int32).reshape(1)

    (own,) = call(
        functools.partial(score, nyh),
        [shape((count + 8, columns), f32)],
        [query, block],
        flops=4 * ring * nyh * queries * columns * half,
    )
    other = swap_cores(own)
    expo, aux, sent = call(
        functools.partial(exponentials, members),
        [shape((count, columns), f32), shape((8, columns), f32), shape((ny * members, max(columns, count)), f32)],
        [iy, own, other, onehot],
        scalars=1,
    )
    sums = exchange(sent, ("yl", "yh", "z", "x"))
    sent, loss = call(
        functools.partial(weigh, nyh, members),
        [shape((ring, nyh * queries, feats), bf16), shape((8, 128), f32)],
        [iy, ixz, expo, aux, onehot, sums, block],
        scratch=[((ring * nyh * queries, feats), f32)],
        scalars=2,
        flops=2 * ring * nyh * queries * columns * half,
    )
    got = exchange(sent, ("yl", "yh", "c"))

    out_rows = rank // (nyh * nc)
    cols = width // (nz * nyl * nx)
    blocks = nz * ny
    keep, send = call(
        functools.partial(backward, nyh, nc),
        [shape((nx, blocks, 2 * out_rows, cols), bf16)] * 2,
        [place, got, unit, length, inv, hidden, gain, adapter_in, own_mats, other_mats, latent_t],
        scratch=[
            ((nc, nyh * queries, feats), f32),
            ((queries, width), f32),
            ((rank, width), f32),
            ((tokens, feats), bf16),
        ],
        scalars=1,
        flops=6 * tokens * rank * width,
    )
    (chip,) = call(
        join,
        [shape((nx, blocks + 1, 2 * out_rows, cols), bf16)],
        [keep, swap_cores(send), loss],
    )
    (line,) = call(
        add_line, [shape((blocks, 2 * out_rows + 8, cols), f32)], [exchange(chip, "x")]
    )
    last = jnp.sum(exchange(line, ("z", "yl", "yh")), axis=0)
    adapter_grads = last[: 2 * out_rows].reshape(2, out_rows, cols)
    total_pairs = group * nz * nyl * nx
    loss = last[2 * out_rows, 0] / (2.0 * total_pairs) + inv_temp
    return (adapter_grads, loss)


def build(mesh, sizes):
    split = Mesh(mesh.devices.reshape(sizes), AXES)
    dp, fsdp = ("z", "yl", "x"), ("yh", "c")
    placed = (
        P(AXES, None),
        P(AXES, None),
        P(),
        P(fsdp, None),
        P(None, fsdp),
        P(dp, fsdp),
        P(dp),
    )
    return jax.shard_map(
        lambda *args: shards(sizes, *args),
        mesh=split,
        in_specs=placed,
        out_specs=(P(None, fsdp, dp), P()),
        check_vma=False,
    )


def solution(mesh):
    return build(mesh, SIZES)
```

```python
import functools

import jax
import jax.numpy as jnp
from jax import lax
from jax.experimental import pallas as pl
from jax.experimental.pallas import tpu as pltpu
from jax.sharding import Mesh
from jax.sharding import PartitionSpec as P

LEN = 32


adapter_scale_factor = 0.25
inv_temp = 20.0
norm_eps = 1e-05

AXES = ("z", "yl", "x", "yh", "c")
SIZES = (4, 2, 8, 4, 2)
MIB = 1 << 20
f32, bf16 = jnp.float32, jnp.bfloat16


def dot(left, right):
    return jnp.dot(left, right, preferred_element_type=f32)


def dot_rows(left, right):
    return lax.dot_general(left, right, (((1,), (1,)), ((), ())), preferred_element_type=f32)


def exchange(blocks, axes):
    return lax.all_to_all(blocks, axes, 0, 0, tiled=True)


def swap_cores(value):
    return lax.ppermute(value, "c", [(0, 1), (1, 0)])


def call(kernel, outs, args, scratch=(), scalars=0, flops=0):
    size = sum(a.size * a.dtype.itemsize for a in list(args[scalars:]) + list(outs))
    spare = [pltpu.VMEM(shape, kind) for shape, kind in scratch]
    spare_size = sum(a.size * a.dtype.itemsize for a in map(shape_of, scratch))
    return pl.pallas_call(
        kernel,
        out_shape=outs,
        in_specs=[pl.BlockSpec(memory_space=pltpu.SMEM)] * scalars
        + [pl.BlockSpec(memory_space=pltpu.VMEM)] * (len(args) - scalars),
        out_specs=[pl.BlockSpec(memory_space=pltpu.VMEM)] * len(outs),
        scratch_shapes=spare,
        compiler_params=pltpu.CompilerParams(
            vmem_limit_bytes=spare_size + 8 * MIB
        ),
        cost_estimate=pl.CostEstimate(flops=flops, bytes_accessed=size, transcendentals=0),
    )(*args)


def shape_of(pair):
    return jax.ShapeDtypeStruct(*pair)


def adapter_slices(place_ref, own_ref, other_ref):
    nyh, _, feats = own_ref.shape
    for k in range(nyh):
        for ref, core in ((own_ref, place_ref[1]), (other_ref, 1 - place_ref[1])):
            at = (lax.rem(place_ref[0] + k, nyh) * 2 + core) * feats
            yield ref.at[k], pl.ds(pl.multiple_of(at, feats), feats)


def forward(nyh, nc, place_ref, in_ref, frozen_ref, gain_ref, own_ref, other_ref,
            latent_ref, hidden_ref, inv_ref, unit_ref, length_ref, send_ref, part_ref):
    _, both, feats = own_ref.shape
    slices = nyh * nc
    rank = both // 2
    tokens, width = in_ref.shape
    queries = tokens // LEN
    acc = jnp.zeros((tokens, rank), f32)
    acc_t = jnp.zeros((rank, tokens), f32)
    for mats_ref, at in adapter_slices(place_ref, own_ref, other_ref):
        part = in_ref[:, at]
        down = mats_ref[:rank]
        acc += dot_rows(part, down)
        acc_t += dot_rows(down, part)
    latent = acc.astype(bf16)
    latent_ref[...] = acc_t.astype(bf16)
    squares = jnp.zeros((tokens, 1), f32)
    for mats_ref, at in adapter_slices(place_ref, own_ref, other_ref):
        hidden = frozen_ref[:, at].astype(f32) + adapter_scale_factor * dot(
            latent, mats_ref[rank:]
        )
        hidden_ref[:, at] = hidden
        squares += jnp.sum(hidden * hidden, axis=1, keepdims=True)
    inv = lax.rsqrt(squares / width + norm_eps)
    inv_ref[...] = jnp.broadcast_to(inv, inv_ref.shape)
    total = jnp.zeros((queries, 1), f32)
    for f in range(slices):
        at = slice(f * feats, (f + 1) * feats)
        scaled = hidden_ref[:, at] * inv
        for q in range(queries):
            one = jnp.sum(scaled[q * LEN:(q + 1) * LEN], axis=0, keepdims=True)
            unit_ref[q:q + 1, at] = one * gain_ref[:, at] / LEN
        pooled = unit_ref[:, at]
        total += jnp.sum(pooled * pooled, axis=1, keepdims=True)
    length = jnp.sqrt(total)
    length_ref[...] = jnp.broadcast_to(length, length_ref.shape)
    for f in range(slices):
        at = slice(f * feats, (f + 1) * feats)
        unit = unit_ref[:, at] / length
        unit_ref[:, at] = unit
        part_ref[f % nc, f // nc * queries:(f // nc + 1) * queries, :] = unit
    for c in range(nc):
        rows = part_ref[c].astype(bf16)
        for y in range(send_ref.shape[0] // nc):
            send_ref[y * nc + c] = rows


def row_index(shape):
    return lax.broadcasted_iota(jnp.int32, shape, 0)


def score(nyh, query_ref, block_ref, out_ref):
    ring, rows, feats = query_ref.shape
    queries = rows // nyh
    columns = block_ref.shape[0]
    query = query_ref[...].reshape(ring * rows, feats)
    mine = row_index((ring * rows, columns)) // queries % nyh
    total = jnp.zeros((ring * rows, columns), f32)
    gram = jnp.zeros((columns, columns), f32)
    for k in range(nyh):
        part = block_ref[:, k * feats:(k + 1) * feats]
        total = jnp.where(mine == k, dot_rows(query, part), total)
        gram += dot_rows(part, part)
    total = total.reshape(ring, rows // 8, 8, columns)
    total = functools.reduce(jnp.add, [total[:, i] for i in range(rows // 8)])
    total = total.reshape(ring * 8, columns)
    count = ring * 8
    upper = row_index(total.shape) % 8 < 4
    total += jnp.where(upper, pltpu.roll(total, count - 4, 0), pltpu.roll(total, 4, 0))
    same = row_index(gram.shape) == lax.broadcasted_iota(jnp.int32, gram.shape, 1)
    norms = jnp.sum(jnp.where(same, gram, 0.0), axis=0, keepdims=True)
    out_ref[:count] = total
    out_ref[count:] = jnp.broadcast_to(norms, (8, columns))


def across(row):
    n = row.size
    return jnp.transpose(jnp.broadcast_to(row, (n, n)))


def exponentials(own_ref, other_ref, onehot_ref, expo_ref, aux_ref, rows_ref, cols_ref):
    count, columns = expo_ref.shape
    inv_norm = 1.0 / jnp.sqrt(own_ref[count:count + 1] + other_ref[count:count + 1])
    scores = inv_temp * ((own_ref[:count] + other_ref[:count]) * inv_norm)
    expo = jnp.exp(scores - inv_temp)
    expo_ref[...] = expo
    hits = 0.5 * jnp.sum(scores * onehot_ref[...])
    aux_ref[0:1] = inv_norm
    aux_ref[1:2] = jnp.full((1, columns), hits)
    row = across(jnp.sum(expo, axis=1, keepdims=True))[0:1]
    for y in range(rows_ref.shape[0]):
        rows_ref[y] = row
    col = 0.5 * jnp.sum(expo, axis=0, keepdims=True)
    for i in range(cols_ref.shape[0]):
        cols_ref[i] = col


def weigh(nyh, expo_ref, aux_ref, onehot_ref, rows_ref, cols_ref, block_ref,
          out_ref, loss_ref, total_ref):
    count, columns = expo_ref.shape
    ring, rows, feats = out_ref.shape
    queries = rows // nyh
    ny, members = rows_ref.shape[0], cols_ref.shape[0]
    row = functools.reduce(jnp.add, [rows_ref[y] for y in range(ny)])
    col = functools.reduce(jnp.add, [cols_ref[i] for i in range(members)])
    loss = (
        0.5 * jnp.sum(jnp.log(row), axis=1, keepdims=True) / ny
        + jnp.sum(jnp.log(col), axis=1, keepdims=True) / members
        - 2.0 * aux_ref[1:2, 0:1]
    )
    loss_ref[...] = jnp.broadcast_to(loss, loss_ref.shape)
    expo = expo_ref[...]
    weights = 0.5 * (expo / across(row)[:, :1] + expo / col) - onehot_ref[...]
    weights = (weights * aux_ref[0:1]).reshape(ring, 1, 8, columns)
    weights = jnp.broadcast_to(weights, (ring, rows // 8, 8, columns))
    weights = weights.reshape(ring * rows, columns).astype(bf16)
    mine = row_index((ring * rows, feats)) // queries % nyh
    for k in range(nyh):
        part = inv_temp * dot(weights, block_ref[:, k * feats:(k + 1) * feats])
        if k == 0:
            total_ref[...] = part
        else:
            total_ref[...] = jnp.where(mine == k, part, total_ref[...])
    out_ref[...] = total_ref[...].astype(bf16).reshape(out_ref.shape)


def backward(nyh, nc, place_ref, got_ref, unit_ref, length_ref, inv_ref, hidden_ref, gain_ref,
             in_ref, own_ref, other_ref, latent_ref, keep_ref, send_ref,
             grad_ref, scaled_ref, up_ref, hg_ref):
    _, both, feats = own_ref.shape
    slices = nyh * nc
    rank = both // 2
    tokens, width = in_ref.shape
    queries = tokens // LEN
    nx, _, pair_rows, cols = keep_ref.shape
    out_rows = pair_rows // 2
    for c in range(nc):
        total = got_ref[c].astype(f32)
        for y in range(1, got_ref.shape[0] // nc):
            total += got_ref[y * nc + c].astype(f32)
        grad_ref[c] = total
    inner = jnp.zeros((queries, 1), f32)
    for f in range(slices):
        at = slice(f * feats, (f + 1) * feats)
        grad = grad_ref[f % nc, f // nc * queries:(f // nc + 1) * queries, :]
        inner += jnp.sum(unit_ref[:, at] * grad, axis=1, keepdims=True)
    length = length_ref[:, :1]
    mean = [jnp.zeros((LEN, 1), f32) for q in range(queries)]
    for f in range(slices):
        at = slice(f * feats, (f + 1) * feats)
        grad = grad_ref[f % nc, f // nc * queries:(f // nc + 1) * queries, :]
        pooled_grad = (grad - unit_ref[:, at] * inner) / length
        scaled_ref[:, at] = pooled_grad / LEN * gain_ref[:, at]
        for q in range(queries):
            product = hidden_ref[q * LEN:(q + 1) * LEN, at] * scaled_ref[q:q + 1, at]
            mean[q] += jnp.sum(product, axis=1, keepdims=True)
    inv = inv_ref[:, :1]
    factor = inv * inv * inv * (jnp.concatenate(mean, axis=0) / width)
    latent_t = latent_ref[...]
    acc = jnp.zeros((rank, tokens), f32)
    for mats_ref, at in adapter_slices(place_ref, own_ref, other_ref):
        for q in range(queries):
            of = slice(q * LEN, (q + 1) * LEN)
            hg_ref[of] = (
                inv[of] * scaled_ref[q:q + 1, at] - hidden_ref[of, at] * factor[of]
            ).astype(bf16)
        hidden_grad = hg_ref[...]
        acc += dot_rows(mats_ref[rank:], hidden_grad)
        up_ref[:, at] = adapter_scale_factor * dot(latent_t, hidden_grad)
    latent_grad = (adapter_scale_factor * acc).astype(bf16)
    first = place_ref[1] == 0
    for f in range(slices):
        down = dot(latent_grad, in_ref[:, f * feats:(f + 1) * feats])
        for x in range(nx):
            lanes = slice(x * cols, (x + 1) * cols)
            spot = slice(f * feats + x * cols, f * feats + (x + 1) * cols)
            for yh in range(nyh):
                tiles = []
                for c in range(nc):
                    of = slice((yh * nc + c) * out_rows, (yh * nc + c + 1) * out_rows)
                    tiles.append(
                        jnp.concatenate([down[of, lanes], up_ref[of, spot]], axis=0).astype(bf16)
                    )
                keep_ref[x, f * nyh + yh] = jnp.where(first, tiles[0], tiles[1])
                send_ref[x, f * nyh + yh] = jnp.where(first, tiles[1], tiles[0])


def split_rows(value, rows, cols):
    high = value.astype(bf16).astype(f32)
    middle = (value - high).astype(bf16).astype(f32)
    low = value - high - middle
    at = row_index((rows, value.shape[1]))
    parts = jnp.where(at == 0, high, jnp.where(at == 1, middle, jnp.where(at == 2, low, 0.0)))
    return jnp.concatenate([parts] * (cols // value.shape[1]), axis=1).astype(bf16)


def join(keep_ref, got_ref, loss_ref, out_ref):
    nx, blocks, rows, cols = keep_ref.shape
    parts = split_rows(loss_ref[0:1], rows, cols)
    for x in range(nx):
        out_ref[x, :blocks] = (
            keep_ref[x].astype(f32) + got_ref[x].astype(f32)
        ).astype(bf16)
        out_ref[x, blocks] = parts


def add_line(got_ref, out_ref):
    total = got_ref[0].astype(f32)
    for x in range(1, got_ref.shape[0]):
        total += got_ref[x].astype(f32)
    blocks, _, cols = out_ref.shape
    rows = got_ref.shape[2]
    loss = jnp.sum(total[blocks], axis=0, keepdims=True)[:, :128]
    out_ref[:, :rows] = total[:blocks].astype(bf16)
    out_ref[:, rows:] = jnp.broadcast_to(split_rows(loss, rows, cols)[None], (blocks, rows, cols))


def add_last(got_ref, out_ref):
    total = got_ref[0].astype(f32)
    for i in range(1, got_ref.shape[0]):
        total += got_ref[i].astype(f32)
    rows = out_ref.shape[0] - 8
    out_ref[:rows] = total[:rows]
    loss = jnp.sum(total[rows:], axis=0, keepdims=True)
    out_ref[rows:] = jnp.broadcast_to(loss, (8, out_ref.shape[1]))


def shards(sizes, adapter_in, frozen, gain, adapter_a, adapter_up_matrix, passages, positive):
    nz, nyl, nx, nyh, nc = sizes
    ny = nyl * nyh
    iz, iyl, ix, iyh, ic = (lax.axis_index(axis) for axis in AXES)
    rank = adapter_up_matrix.shape[0]
    feats = passages.shape[1]
    half = nyh * feats
    width = half * nc
    tokens = adapter_in.shape[0]
    queries = tokens // LEN
    group = passages.shape[0]
    rows = group // nyh
    ring = ny * nc
    members = nz * nx
    shape = jax.ShapeDtypeStruct
    gain = gain.reshape(1, width)

    sent = jnp.broadcast_to(passages.reshape(1, nyh, rows, feats), (nx, nyh, rows, feats))
    got = exchange(sent.reshape(nx * nyh, rows, feats), ("x", "yh"))
    got = got.reshape(nx, nyh, rows, feats).transpose(0, 2, 1, 3).reshape(nx * rows, half)

    mine = jnp.concatenate([adapter_a.T, adapter_up_matrix], axis=0)
    pieces = [mine]
    for k in range(1, nyh):
        flip = 2 * k == nyh
        pairs = []
        for yl in range(nyl):
            for yh in range(nyh):
                source = (nyl - 1 - yl if flip else yl) * nyh + (yh + k) % nyh
                pairs.append((source, yl * nyh + yh))
        pieces.append(lax.ppermute(mine, ("yl", "yh"), pairs))
    early = [k for k in range(1, nyh) if 2 * k != nyh]
    got, *arrived = lax.optimization_barrier((got, *[pieces[k] for k in early]))
    for k, piece in zip(early, arrived):
        pieces[k] = piece
    own_mats = jnp.stack(pieces)
    other_mats = swap_cores(own_mats)
    place = jnp.stack([iyh, ic]).astype(jnp.int32)

    got = jnp.broadcast_to(got[None], (nz, nx * rows, half))
    block = exchange(got, "z").reshape(members * rows, half)
    columns = block.shape[0]

    latent_t, hidden, inv, unit, length, sent = call(
        functools.partial(forward, nyh, nc),
        [
            shape((rank, tokens), bf16),
            shape((tokens, width), f32),
            shape((tokens, 128), f32),
            shape((queries, width), f32),
            shape((queries, 128), f32),
            shape((ring, nyh * queries, feats), bf16),
        ],
        [place, adapter_in, frozen, gain, own_mats, other_mats],
        scratch=[((nc, nyh * queries, feats), f32)],
        scalars=1,
        flops=6 * tokens * rank * width,
    )
    sent, block = lax.optimization_barrier((sent, block))
    query = exchange(sent, ("yl", "yh", "c"))

    count = ring * 8
    at = lax.iota(jnp.int32, columns)
    at_z, at_x, at_row = at // (nx * rows), at // rows % nx, at % rows
    passage_id = ((at_z * nyl + iyl) * nx + at_x) * group + iyh * rows + at_row
    own_pos = jnp.where(
        lax.iota(jnp.int32, nyl)[:, None] == iyl, positive[None, :], -1
    ).reshape(ring, 1, queries)
    own_pos = jnp.broadcast_to(own_pos, (ring, 8 // queries, queries)).reshape(count)
    onehot = (own_pos[:, None] == passage_id[None, :]).astype(f32)
    (own,) = call(
        functools.partial(score, nyh),
        [shape((count + 8, columns), f32)],
        [query, block],
        flops=4 * ring * nyh * queries * columns * half,
    )
    other = swap_cores(own)
    expo, aux, by_row, by_col = call(
        exponentials,
        [
            shape((count, columns), f32),
            shape((8, columns), f32),
            shape((ny, 1, count), f32),
            shape((members, 1, columns), f32),
        ],
        [own, other, onehot],
    )
    by_row = exchange(by_row, ("yl", "yh"))
    by_col = exchange(by_col, ("z", "x"))
    sent, loss = call(
        functools.partial(weigh, nyh),
        [shape((ring, nyh * queries, feats), bf16), shape((8, 128), f32)],
        [expo, aux, onehot, by_row, by_col, block],
        scratch=[((ring * nyh * queries, feats), f32)],
        flops=2 * ring * nyh * queries * columns * half,
    )
    got = exchange(sent, ("yl", "yh", "c"))

    out_rows = rank // (nyh * nc)
    cols = width // (nz * nyl * nx)
    blocks = nz * ny
    keep, send = call(
        functools.partial(backward, nyh, nc),
        [shape((nx, blocks, 2 * out_rows, cols), bf16)] * 2,
        [place, got, unit, length, inv, hidden, gain, adapter_in, own_mats, other_mats, latent_t],
        scratch=[
            ((nc, nyh * queries, feats), f32),
            ((queries, width), f32),
            ((rank, width), f32),
            ((tokens, feats), bf16),
        ],
        scalars=1,
        flops=6 * tokens * rank * width,
    )
    (chip,) = call(
        join,
        [shape((nx, blocks + 1, 2 * out_rows, cols), bf16)],
        [keep, swap_cores(send), loss],
    )
    (line,) = call(
        add_line, [shape((blocks, 4 * out_rows, cols), bf16)], [exchange(chip, "x")]
    )
    (last,) = call(
        add_last,
        [shape((2 * out_rows + 8, cols), f32)],
        [exchange(line, ("z", "yl", "yh"))],
    )
    adapter_grads = last[: 2 * out_rows].reshape(2, out_rows, cols)
    total_pairs = group * nz * nyl * nx
    loss = last[2 * out_rows, 0] / (2.0 * total_pairs) + inv_temp
    return (adapter_grads, loss)


def build(mesh, sizes):
    split = Mesh(mesh.devices.reshape(sizes), AXES)
    dp, fsdp = ("z", "yl", "x"), ("yh", "c")
    placed = (
        P(AXES, None),
        P(AXES, None),
        P(),
        P(fsdp, None),
        P(None, fsdp),
        P(dp, fsdp),
        P(dp),
    )
    return jax.shard_map(
        lambda *args: shards(sizes, *args),
        mesh=split,
        in_specs=placed,
        out_specs=(P(None, fsdp, dp), P()),
        check_vma=False,
    )


def solution(mesh):
    return build(mesh, SIZES)
```

```python
import functools

import jax
import jax.numpy as jnp
from jax import lax
from jax.experimental import pallas as pl
from jax.experimental.pallas import tpu as pltpu
from jax.sharding import Mesh
from jax.sharding import PartitionSpec as P

LEN = 32


adapter_scale_factor = 0.25
inv_temp = 20.0
norm_eps = 1e-05

AXES = ("zh", "zl", "yl", "x", "yh", "c")
SIZES = (4, 2, 2, 4, 4, 2)
ROW, COLUMN, RING = ("zl", "yh"), ("zh", "yl", "x"), ("zl", "yh", "c")
MIB = 1 << 20
f32, bf16 = jnp.float32, jnp.bfloat16


def dot(left, right):
    return jnp.dot(left, right, preferred_element_type=f32)


def dot_rows(left, right):
    return lax.dot_general(left, right, (((1,), (1,)), ((), ())), preferred_element_type=f32)


def exchange(blocks, axes):
    return lax.all_to_all(blocks, axes, 0, 0, tiled=True)


def swap_cores(value):
    return lax.ppermute(value, "c", [(0, 1), (1, 0)])


def call(kernel, outs, args, scratch=(), scalars=0, flops=0):
    size = sum(a.size * a.dtype.itemsize for a in list(args[scalars:]) + list(outs))
    spare = [pltpu.VMEM(shape, kind) for shape, kind in scratch]
    spare_size = sum(a.size * a.dtype.itemsize for a in map(shape_of, scratch))
    return pl.pallas_call(
        kernel,
        out_shape=outs,
        in_specs=[pl.BlockSpec(memory_space=pltpu.SMEM)] * scalars
        + [pl.BlockSpec(memory_space=pltpu.VMEM)] * (len(args) - scalars),
        out_specs=[pl.BlockSpec(memory_space=pltpu.VMEM)] * len(outs),
        scratch_shapes=spare,
        compiler_params=pltpu.CompilerParams(
            vmem_limit_bytes=spare_size + 8 * MIB
        ),
        cost_estimate=pl.CostEstimate(flops=flops, bytes_accessed=size, transcendentals=0),
    )(*args)


def shape_of(pair):
    return jax.ShapeDtypeStruct(*pair)


def pack(nyh, zh_ref, down_ref, up_ref, passages_ref, out_ref):
    peers, both, _ = out_ref.shape
    nzh = peers // nyh
    part = 2 * down_ref.shape[0] // nzh
    at = pl.ds(pl.multiple_of(lax.rem(zh_ref[0], nzh // 2) * part, part), part)
    mine = jnp.where(zh_ref[0] < nzh // 2, down_ref[at, :].astype(f32), up_ref[at, :].astype(f32))
    passages = passages_ref[...].astype(f32)
    rows = both - part
    for yh in range(nyh):
        block = jnp.concatenate([mine, passages[yh * rows:(yh + 1) * rows]], axis=0).astype(bf16)
        for zh in range(nzh):
            out_ref[zh * nyh + yh] = block


def unpack(nyh, got_ref, mats_ref, out_ref):
    peers, both, feats = got_ref.shape
    nzh = peers // nyh
    part = mats_ref.shape[1] // nzh
    for yh in range(nyh):
        passages = []
        for zh in range(nzh):
            block = got_ref[zh * nyh + yh].astype(f32)
            mats_ref[yh, zh * part:(zh + 1) * part, :] = block[:part].astype(bf16)
            passages.append(block[part:])
        passages = jnp.concatenate(passages, axis=0).astype(bf16)
        for i in range(out_ref.shape[0]):
            out_ref[i, :, yh * feats:(yh + 1) * feats] = passages


def adapter_slices(core_ref, own_ref, other_ref):
    nyh, _, feats = own_ref.shape
    for yh in range(nyh):
        for ref, core in ((own_ref, core_ref[0]), (other_ref, 1 - core_ref[0])):
            at = (yh * 2 + core) * feats
            yield ref.at[yh], pl.ds(pl.multiple_of(at, feats), feats)


def forward(nyh, nc, core_ref, in_ref, frozen_ref, gain_ref, own_ref, other_ref,
            latent_ref, hidden_ref, inv_ref, unit_ref, length_ref, send_ref, part_ref):
    _, both, feats = own_ref.shape
    slices = nyh * nc
    rank = both // 2
    tokens, width = in_ref.shape
    queries = tokens // LEN
    acc = jnp.zeros((tokens, rank), f32)
    acc_t = jnp.zeros((rank, tokens), f32)
    for mats_ref, at in adapter_slices(core_ref, own_ref, other_ref):
        part = in_ref[:, at]
        down = mats_ref[:rank]
        acc += dot_rows(part, down)
        acc_t += dot_rows(down, part)
    latent = acc.astype(bf16)
    latent_ref[...] = acc_t.astype(bf16)
    squares = jnp.zeros((tokens, 1), f32)
    for mats_ref, at in adapter_slices(core_ref, own_ref, other_ref):
        hidden = frozen_ref[:, at].astype(f32) + adapter_scale_factor * dot(
            latent, mats_ref[rank:]
        )
        hidden_ref[:, at] = hidden
        squares += jnp.sum(hidden * hidden, axis=1, keepdims=True)
    inv = lax.rsqrt(squares / width + norm_eps)
    inv_ref[...] = jnp.broadcast_to(inv, inv_ref.shape)
    total = jnp.zeros((queries, 1), f32)
    for f in range(slices):
        at = slice(f * feats, (f + 1) * feats)
        scaled = hidden_ref[:, at] * inv
        for q in range(queries):
            one = jnp.sum(scaled[q * LEN:(q + 1) * LEN], axis=0, keepdims=True)
            unit_ref[q:q + 1, at] = one * gain_ref[:, at] / LEN
        pooled = unit_ref[:, at]
        total += jnp.sum(pooled * pooled, axis=1, keepdims=True)
    length = jnp.sqrt(total)
    length_ref[...] = jnp.broadcast_to(length, length_ref.shape)
    for f in range(slices):
        at = slice(f * feats, (f + 1) * feats)
        unit = unit_ref[:, at] / length
        unit_ref[:, at] = unit
        part_ref[f % nc, f // nc * queries:(f // nc + 1) * queries, :] = unit
    for c in range(nc):
        rows = part_ref[c].astype(bf16)
        for y in range(send_ref.shape[0] // nc):
            send_ref[y * nc + c] = rows


def row_index(shape):
    return lax.broadcasted_iota(jnp.int32, shape, 0)


def score(nyh, query_ref, block_ref, out_ref):
    ring, rows, feats = query_ref.shape
    queries = rows // nyh
    columns = block_ref.shape[0]
    query = query_ref[...].reshape(ring * rows, feats)
    mine = row_index((ring * rows, columns)) // queries % nyh
    total = jnp.zeros((ring * rows, columns), f32)
    gram = jnp.zeros((columns, columns), f32)
    for k in range(nyh):
        part = block_ref[:, k * feats:(k + 1) * feats]
        total = jnp.where(mine == k, dot_rows(query, part), total)
        gram += dot_rows(part, part)
    total = total.reshape(ring, rows // 8, 8, columns)
    total = functools.reduce(jnp.add, [total[:, i] for i in range(rows // 8)])
    total = total.reshape(ring * 8, columns)
    count = ring * 8
    upper = row_index(total.shape) % 8 < 4
    total += jnp.where(upper, pltpu.roll(total, count - 4, 0), pltpu.roll(total, 4, 0))
    same = row_index(gram.shape) == lax.broadcasted_iota(jnp.int32, gram.shape, 1)
    norms = jnp.sum(jnp.where(same, gram, 0.0), axis=0, keepdims=True)
    out_ref[:count] = total
    out_ref[count:] = jnp.broadcast_to(norms, (8, columns))


def across(row):
    n = row.size
    return jnp.transpose(jnp.broadcast_to(row, (n, n)))


def exponentials(own_ref, other_ref, onehot_ref, expo_ref, aux_ref, rows_ref, cols_ref):
    count, columns = expo_ref.shape
    inv_norm = 1.0 / jnp.sqrt(own_ref[count:count + 1] + other_ref[count:count + 1])
    scores = inv_temp * ((own_ref[:count] + other_ref[:count]) * inv_norm)
    expo = jnp.exp(scores - inv_temp)
    expo_ref[...] = expo
    hits = 0.5 * jnp.sum(scores * onehot_ref[...])
    aux_ref[0:1] = inv_norm
    aux_ref[1:2] = jnp.full((1, columns), hits)
    row = across(jnp.sum(expo, axis=1, keepdims=True))[0:1]
    for y in range(rows_ref.shape[0]):
        rows_ref[y] = row
    col = 0.5 * jnp.sum(expo, axis=0, keepdims=True)
    for i in range(cols_ref.shape[0]):
        cols_ref[i] = col


def weigh(nyh, expo_ref, aux_ref, onehot_ref, rows_ref, cols_ref, block_ref,
          out_ref, loss_ref, total_ref):
    count, columns = expo_ref.shape
    ring, rows, feats = out_ref.shape
    queries = rows // nyh
    ny, members = rows_ref.shape[0], cols_ref.shape[0]
    row = functools.reduce(jnp.add, [rows_ref[y] for y in range(ny)])
    col = functools.reduce(jnp.add, [cols_ref[i] for i in range(members)])
    loss = (
        0.5 * jnp.sum(jnp.log(row), axis=1, keepdims=True) / ny
        + jnp.sum(jnp.log(col), axis=1, keepdims=True) / members
        - 2.0 * aux_ref[1:2, 0:1]
    )
    loss_ref[...] = jnp.broadcast_to(loss, loss_ref.shape)
    expo = expo_ref[...]
    weights = 0.5 * (expo / across(row)[:, :1] + expo / col) - onehot_ref[...]
    weights = (weights * aux_ref[0:1]).reshape(ring, 1, 8, columns)
    weights = jnp.broadcast_to(weights, (ring, rows // 8, 8, columns))
    weights = weights.reshape(ring * rows, columns).astype(bf16)
    mine = row_index((ring * rows, feats)) // queries % nyh
    for k in range(nyh):
        part = inv_temp * dot(weights, block_ref[:, k * feats:(k + 1) * feats])
        if k == 0:
            total_ref[...] = part
        else:
            total_ref[...] = jnp.where(mine == k, part, total_ref[...])
    out_ref[...] = total_ref[...].astype(bf16).reshape(out_ref.shape)


def backward(nyh, nc, core_ref, got_ref, unit_ref, length_ref, inv_ref, hidden_ref, gain_ref,
             in_ref, own_ref, other_ref, latent_ref, keep_ref, send_ref,
             grad_ref, scaled_ref, up_ref, hg_ref):
    _, both, feats = own_ref.shape
    slices = nyh * nc
    rank = both // 2
    tokens, width = in_ref.shape
    queries = tokens // LEN
    nx, _, pair_rows, cols = keep_ref.shape
    out_rows = pair_rows // 2
    for c in range(nc):
        total = got_ref[c].astype(f32)
        for y in range(1, got_ref.shape[0] // nc):
            total += got_ref[y * nc + c].astype(f32)
        grad_ref[c] = total
    inner = jnp.zeros((queries, 1), f32)
    for f in range(slices):
        at = slice(f * feats, (f + 1) * feats)
        grad = grad_ref[f % nc, f // nc * queries:(f // nc + 1) * queries, :]
        inner += jnp.sum(unit_ref[:, at] * grad, axis=1, keepdims=True)
    length = length_ref[:, :1]
    mean = [jnp.zeros((LEN, 1), f32) for q in range(queries)]
    for f in range(slices):
        at = slice(f * feats, (f + 1) * feats)
        grad = grad_ref[f % nc, f // nc * queries:(f // nc + 1) * queries, :]
        pooled_grad = (grad - unit_ref[:, at] * inner) / length
        scaled_ref[:, at] = pooled_grad / LEN * gain_ref[:, at]
        for q in range(queries):
            product = hidden_ref[q * LEN:(q + 1) * LEN, at] * scaled_ref[q:q + 1, at]
            mean[q] += jnp.sum(product, axis=1, keepdims=True)
    inv = inv_ref[:, :1]
    factor = inv * inv * inv * (jnp.concatenate(mean, axis=0) / width)
    latent_t = latent_ref[...]
    acc = jnp.zeros((rank, tokens), f32)
    for mats_ref, at in adapter_slices(core_ref, own_ref, other_ref):
        for q in range(queries):
            of = slice(q * LEN, (q + 1) * LEN)
            hg_ref[of] = (
                inv[of] * scaled_ref[q:q + 1, at] - hidden_ref[of, at] * factor[of]
            ).astype(bf16)
        hidden_grad = hg_ref[...]
        acc += dot_rows(mats_ref[rank:], hidden_grad)
        up_ref[:, at] = adapter_scale_factor * dot(latent_t, hidden_grad)
    latent_grad = (adapter_scale_factor * acc).astype(bf16)
    first = core_ref[0] == 0
    for f in range(slices):
        down = dot(latent_grad, in_ref[:, f * feats:(f + 1) * feats])
        for x in range(nx):
            lanes = slice(x * cols, (x + 1) * cols)
            spot = slice(f * feats + x * cols, f * feats + (x + 1) * cols)
            for yh in range(nyh):
                tiles = []
                for c in range(nc):
                    of = slice((yh * nc + c) * out_rows, (yh * nc + c + 1) * out_rows)
                    tiles.append(
                        jnp.concatenate([down[of, lanes], up_ref[of, spot]], axis=0).astype(bf16)
                    )
                keep_ref[x, f * nyh + yh] = jnp.where(first, tiles[0], tiles[1])
                send_ref[x, f * nyh + yh] = jnp.where(first, tiles[1], tiles[0])


def split_rows(value, rows, cols):
    high = value.astype(bf16).astype(f32)
    middle = (value - high).astype(bf16).astype(f32)
    low = value - high - middle
    at = row_index((rows, value.shape[1]))
    parts = jnp.where(at == 0, high, jnp.where(at == 1, middle, jnp.where(at == 2, low, 0.0)))
    return jnp.concatenate([parts] * (cols // value.shape[1]), axis=1).astype(bf16)


def join(keep_ref, got_ref, loss_ref, out_ref):
    nx, blocks, rows, cols = keep_ref.shape
    parts = split_rows(loss_ref[0:1], rows, cols)
    for x in range(nx):
        out_ref[x, :blocks] = (
            keep_ref[x].astype(f32) + got_ref[x].astype(f32)
        ).astype(bf16)
        out_ref[x, blocks] = parts


def add_line(got_ref, out_ref):
    total = got_ref[0].astype(f32)
    for x in range(1, got_ref.shape[0]):
        total += got_ref[x].astype(f32)
    blocks, _, cols = out_ref.shape
    rows = got_ref.shape[2]
    loss = jnp.sum(total[blocks], axis=0, keepdims=True)[:, :128]
    out_ref[:, :rows] = total[:blocks].astype(bf16)
    out_ref[:, rows:] = jnp.broadcast_to(split_rows(loss, rows, cols)[None], (blocks, rows, cols))


def add_last(got_ref, out_ref):
    total = got_ref[0].astype(f32)
    for i in range(1, got_ref.shape[0]):
        total += got_ref[i].astype(f32)
    rows = out_ref.shape[0] - 8
    out_ref[:rows] = total[:rows]
    loss = jnp.sum(total[rows:], axis=0, keepdims=True)
    out_ref[rows:] = jnp.broadcast_to(loss, (8, out_ref.shape[1]))


def shards(sizes, adapter_in, frozen, gain, adapter_a, adapter_up_matrix, passages, positive):
    nzh, nzl, nyl, nx, nyh, nc = sizes
    izh, izl, iyl, ix, iyh, ic = (lax.axis_index(axis) for axis in AXES)
    rank = adapter_up_matrix.shape[0]
    feats = passages.shape[1]
    half = nyh * feats
    width = half * nc
    tokens = adapter_in.shape[0]
    queries = tokens // LEN
    group = passages.shape[0]
    rows = group // nyh
    ny = nzl * nyh
    ring = ny * nc
    members = nzh * nyl * nx
    shape = jax.ShapeDtypeStruct
    gain = gain.reshape(1, width)
    core = ic.astype(jnp.int32).reshape(1)

    part = 2 * rank // nzh
    (sent,) = call(
        functools.partial(pack, nyh),
        [shape((nzh * nyh, part + rows, feats), bf16)],
        [izh.astype(jnp.int32).reshape(1), adapter_a.T, adapter_up_matrix, passages],
        scalars=1,
    )
    own_mats, sent = call(
        functools.partial(unpack, nyh),
        [
            shape((nyh, 2 * rank, feats), bf16),
            shape((nyl * nx, nzh * rows, half), bf16),
        ],
        [exchange(sent, ("zh", "yh"))],
    )
    other_mats = swap_cores(own_mats)
    block = exchange(sent, ("yl", "x")).reshape(members * rows, half)
    columns = block.shape[0]

    latent_t, hidden, inv, unit, length, sent = call(
        functools.partial(forward, nyh, nc),
        [
            shape((rank, tokens), bf16),
            shape((tokens, width), f32),
            shape((tokens, 128), f32),
            shape((queries, width), f32),
            shape((queries, 128), f32),
            shape((ring, nyh * queries, feats), bf16),
        ],
        [core, adapter_in, frozen, gain, own_mats, other_mats],
        scratch=[((nc, nyh * queries, feats), f32)],
        scalars=1,
        flops=6 * tokens * rank * width,
    )
    sent, block = lax.optimization_barrier((sent, block))
    query = exchange(sent, RING)

    count = ring * 8
    at = lax.iota(jnp.int32, columns)
    at_xy, at_zh, at_row = at // (nzh * rows), at // rows % nzh, at % rows
    passage_id = ((at_zh * nzl + izl) * nyl * nx + at_xy) * group + iyh * rows + at_row
    own_pos = jnp.where(
        lax.iota(jnp.int32, nzl)[:, None] == izl, positive[None, :], -1
    ).reshape(ring, 1, queries)
    own_pos = jnp.broadcast_to(own_pos, (ring, 8 // queries, queries)).reshape(count)
    onehot = (own_pos[:, None] == passage_id[None, :]).astype(f32)
    (own,) = call(
        functools.partial(score, nyh),
        [shape((count + 8, columns), f32)],
        [query, block],
        flops=4 * ring * nyh * queries * columns * half,
    )
    other = swap_cores(own)
    expo, aux, by_row, by_col = call(
        exponentials,
        [
            shape((count, columns), f32),
            shape((8, columns), f32),
            shape((ny, 1, count), f32),
            shape((members, 1, columns), f32),
        ],
        [own, other, onehot],
    )
    by_row = exchange(by_row, ROW)
    by_col = exchange(by_col, COLUMN)
    sent, loss = call(
        functools.partial(weigh, nyh),
        [shape((ring, nyh * queries, feats), bf16), shape((8, 128), f32)],
        [expo, aux, onehot, by_row, by_col, block],
        scratch=[((ring * nyh * queries, feats), f32)],
        flops=2 * ring * nyh * queries * columns * half,
    )
    got = exchange(sent, RING)

    out_rows = rank // (nyh * nc)
    cols = width // (nzh * nzl * nyl * nx)
    blocks = nzh * ny
    keep, send = call(
        functools.partial(backward, nyh, nc),
        [shape((nyl * nx, blocks, 2 * out_rows, cols), bf16)] * 2,
        [core, got, unit, length, inv, hidden, gain, adapter_in, own_mats, other_mats, latent_t],
        scratch=[
            ((nc, nyh * queries, feats), f32),
            ((queries, width), f32),
            ((rank, width), f32),
            ((tokens, feats), bf16),
        ],
        scalars=1,
        flops=6 * tokens * rank * width,
    )
    (chip,) = call(
        join,
        [shape((nyl * nx, blocks + 1, 2 * out_rows, cols), bf16)],
        [keep, swap_cores(send), loss],
    )
    (line,) = call(
        add_line, [shape((blocks, 4 * out_rows, cols), bf16)], [exchange(chip, ("yl", "x"))]
    )
    (last,) = call(
        add_last,
        [shape((2 * out_rows + 8, cols), f32)],
        [exchange(line, ("zh", "zl", "yh"))],
    )
    adapter_grads = last[: 2 * out_rows].reshape(2, out_rows, cols)
    total_pairs = group * nzl * members
    loss = last[2 * out_rows, 0] / (2.0 * total_pairs) + inv_temp
    return (adapter_grads, loss)


def build(mesh, sizes):
    split = Mesh(mesh.devices.reshape(sizes), AXES)
    dp, fsdp = ("zh", "zl", "yl", "x"), ("yh", "c")
    placed = (
        P(AXES, None),
        P(AXES, None),
        P(),
        P(fsdp, None),
        P(None, fsdp),
        P(dp, fsdp),
        P(dp),
    )
    return jax.shard_map(
        lambda *args: shards(sizes, *args),
        mesh=split,
        in_specs=placed,
        out_specs=(P(None, fsdp, dp), P()),
        check_vma=False,
    )


def solution(mesh):
    return build(mesh, SIZES)
```

```python
import functools

import jax
import jax.numpy as jnp
from jax import lax
from jax.experimental import pallas as pl
from jax.experimental.pallas import tpu as pltpu
from jax.sharding import Mesh
from jax.sharding import PartitionSpec as P

LEN = 32


adapter_scale_factor = 0.25
inv_temp = 20.0
norm_eps = 1e-05

AXES = ("zh", "zl", "yl", "x", "yh", "c")
SIZES = (4, 2, 2, 4, 4, 2)
ROW, COLUMN, RING = ("zl", "yh"), ("zh", "yl", "x"), ("zl", "yh", "c")
MIB = 1 << 20
f32, bf16 = jnp.float32, jnp.bfloat16


def dot(left, right):
    return jnp.dot(left, right, preferred_element_type=f32)


def dot_rows(left, right):
    return lax.dot_general(left, right, (((1,), (1,)), ((), ())), preferred_element_type=f32)


def exchange(blocks, axes):
    return lax.all_to_all(blocks, axes, 0, 0, tiled=True)


def swap_cores(value):
    return lax.ppermute(value, "c", [(0, 1), (1, 0)])


def swap_neighbours(value, nyl, nyh, outer):
    pairs = []
    for yh in range(nyh):
        first, second = yh, nyh + yh
        if outer:
            first, second = nyh + yh, (yh + 1) % nyh
        pairs += [(first, second), (second, first)]
    return lax.ppermute(value, ("yl", "yh"), pairs)


def call(kernel, outs, args, scratch=(), scalars=0, flops=0):
    size = sum(a.size * a.dtype.itemsize for a in list(args[scalars:]) + list(outs))
    spare = [pltpu.VMEM(shape, kind) for shape, kind in scratch]
    spare_size = sum(a.size * a.dtype.itemsize for a in map(shape_of, scratch))
    return pl.pallas_call(
        kernel,
        out_shape=outs,
        in_specs=[pl.BlockSpec(memory_space=pltpu.SMEM)] * scalars
        + [pl.BlockSpec(memory_space=pltpu.VMEM)] * (len(args) - scalars),
        out_specs=[pl.BlockSpec(memory_space=pltpu.VMEM)] * len(outs),
        scratch_shapes=spare,
        compiler_params=pltpu.CompilerParams(
            vmem_limit_bytes=spare_size + 8 * MIB
        ),
        cost_estimate=pl.CostEstimate(flops=flops, bytes_accessed=size, transcendentals=0),
    )(*args)


def shape_of(pair):
    return jax.ShapeDtypeStruct(*pair)


def adapter_slices(place_ref, own_ref, other_ref):
    slots, _, feats = own_ref.shape
    for k in range(slots):
        for ref, place in ((own_ref, place_ref[k]), (other_ref, place_ref[slots + k])):
            yield ref.at[k], pl.ds(pl.multiple_of(place * feats, feats), feats)


def forward(nyh, nc, place_ref, in_ref, frozen_ref, gain_ref, own_ref, other_ref,
            latent_ref, hidden_ref, inv_ref, unit_ref, length_ref, send_ref, part_ref):
    _, both, feats = own_ref.shape
    slices = nyh * nc
    rank = both // 2
    tokens, width = in_ref.shape
    queries = tokens // LEN
    acc = jnp.zeros((tokens, rank), f32)
    acc_t = jnp.zeros((rank, tokens), f32)
    for mats_ref, at in adapter_slices(place_ref, own_ref, other_ref):
        part = in_ref[:, at]
        down = mats_ref[:rank]
        acc += dot_rows(part, down)
        acc_t += dot_rows(down, part)
    latent = acc.astype(bf16)
    latent_ref[...] = acc_t.astype(bf16)
    squares = jnp.zeros((tokens, 1), f32)
    for mats_ref, at in adapter_slices(place_ref, own_ref, other_ref):
        hidden = frozen_ref[:, at].astype(f32) + adapter_scale_factor * dot(
            latent, mats_ref[rank:]
        )
        hidden_ref[:, at] = hidden
        squares += jnp.sum(hidden * hidden, axis=1, keepdims=True)
    inv = lax.rsqrt(squares / width + norm_eps)
    inv_ref[...] = jnp.broadcast_to(inv, inv_ref.shape)
    total = jnp.zeros((queries, 1), f32)
    for f in range(slices):
        at = slice(f * feats, (f + 1) * feats)
        scaled = hidden_ref[:, at] * inv
        for q in range(queries):
            one = jnp.sum(scaled[q * LEN:(q + 1) * LEN], axis=0, keepdims=True)
            unit_ref[q:q + 1, at] = one * gain_ref[:, at] / LEN
        pooled = unit_ref[:, at]
        total += jnp.sum(pooled * pooled, axis=1, keepdims=True)
    length = jnp.sqrt(total)
    length_ref[...] = jnp.broadcast_to(length, length_ref.shape)
    for f in range(slices):
        at = slice(f * feats, (f + 1) * feats)
        unit = unit_ref[:, at] / length
        unit_ref[:, at] = unit
        part_ref[f % nc, f // nc * queries:(f // nc + 1) * queries, :] = unit
    for c in range(nc):
        rows = part_ref[c].astype(bf16)
        for y in range(send_ref.shape[0] // nc):
            send_ref[y * nc + c] = rows


def row_index(shape):
    return lax.broadcasted_iota(jnp.int32, shape, 0)


def score(nyh, query_ref, block_ref, out_ref):
    ring, rows, feats = query_ref.shape
    queries = rows // nyh
    columns = block_ref.shape[0]
    query = query_ref[...].reshape(ring * rows, feats)
    mine = row_index((ring * rows, columns)) // queries % nyh
    total = jnp.zeros((ring * rows, columns), f32)
    gram = jnp.zeros((columns, columns), f32)
    for k in range(nyh):
        part = block_ref[:, k * feats:(k + 1) * feats]
        total = jnp.where(mine == k, dot_rows(query, part), total)
        gram += dot_rows(part, part)
    total = total.reshape(ring, rows // 8, 8, columns)
    total = functools.reduce(jnp.add, [total[:, i] for i in range(rows // 8)])
    total = total.reshape(ring * 8, columns)
    count = ring * 8
    upper = row_index(total.shape) % 8 < 4
    total += jnp.where(upper, pltpu.roll(total, count - 4, 0), pltpu.roll(total, 4, 0))
    same = row_index(gram.shape) == lax.broadcasted_iota(jnp.int32, gram.shape, 1)
    norms = jnp.sum(jnp.where(same, gram, 0.0), axis=0, keepdims=True)
    out_ref[:count] = total
    out_ref[count:] = jnp.broadcast_to(norms, (8, columns))


def across(row):
    n = row.size
    return jnp.transpose(jnp.broadcast_to(row, (n, n)))


def exponentials(own_ref, other_ref, onehot_ref, expo_ref, aux_ref, rows_ref, cols_ref):
    count, columns = expo_ref.shape
    inv_norm = 1.0 / jnp.sqrt(own_ref[count:count + 1] + other_ref[count:count + 1])
    scores = inv_temp * ((own_ref[:count] + other_ref[:count]) * inv_norm)
    expo = jnp.exp(scores - inv_temp)
    expo_ref[...] = expo
    hits = 0.5 * jnp.sum(scores * onehot_ref[...])
    aux_ref[0:1] = inv_norm
    aux_ref[1:2] = jnp.full((1, columns), hits)
    row = across(jnp.sum(expo, axis=1, keepdims=True))[0:1]
    for y in range(rows_ref.shape[0]):
        rows_ref[y] = row
    col = 0.5 * jnp.sum(expo, axis=0, keepdims=True)
    for i in range(cols_ref.shape[0]):
        cols_ref[i] = col


def weigh(nyh, expo_ref, aux_ref, onehot_ref, rows_ref, cols_ref, block_ref,
          out_ref, loss_ref, total_ref):
    count, columns = expo_ref.shape
    ring, rows, feats = out_ref.shape
    queries = rows // nyh
    ny, members = rows_ref.shape[0], cols_ref.shape[0]
    row = functools.reduce(jnp.add, [rows_ref[y] for y in range(ny)])
    col = functools.reduce(jnp.add, [cols_ref[i] for i in range(members)])
    loss = (
        0.5 * jnp.sum(jnp.log(row), axis=1, keepdims=True) / ny
        + jnp.sum(jnp.log(col), axis=1, keepdims=True) / members
        - 2.0 * aux_ref[1:2, 0:1]
    )
    loss_ref[...] = jnp.broadcast_to(loss, loss_ref.shape)
    expo = expo_ref[...]
    weights = 0.5 * (expo / across(row)[:, :1] + expo / col) - onehot_ref[...]
    weights = (weights * aux_ref[0:1]).reshape(ring, 1, 8, columns)
    weights = jnp.broadcast_to(weights, (ring, rows // 8, 8, columns))
    weights = weights.reshape(ring * rows, columns).astype(bf16)
    mine = row_index((ring * rows, feats)) // queries % nyh
    for k in range(nyh):
        part = inv_temp * dot(weights, block_ref[:, k * feats:(k + 1) * feats])
        if k == 0:
            total_ref[...] = part
        else:
            total_ref[...] = jnp.where(mine == k, part, total_ref[...])
    out_ref[...] = total_ref[...].astype(bf16).reshape(out_ref.shape)


def backward(nyh, nc, place_ref, got_ref, unit_ref, length_ref, inv_ref, hidden_ref, gain_ref,
             in_ref, own_ref, other_ref, latent_ref, keep_ref, send_ref,
             grad_ref, scaled_ref, up_ref, hg_ref):
    _, both, feats = own_ref.shape
    slices = nyh * nc
    rank = both // 2
    tokens, width = in_ref.shape
    queries = tokens // LEN
    nx, _, pair_rows, cols = keep_ref.shape
    out_rows = pair_rows // 2
    for c in range(nc):
        total = got_ref[c].astype(f32)
        for y in range(1, got_ref.shape[0] // nc):
            total += got_ref[y * nc + c].astype(f32)
        grad_ref[c] = total
    inner = jnp.zeros((queries, 1), f32)
    for f in range(slices):
        at = slice(f * feats, (f + 1) * feats)
        grad = grad_ref[f % nc, f // nc * queries:(f // nc + 1) * queries, :]
        inner += jnp.sum(unit_ref[:, at] * grad, axis=1, keepdims=True)
    length = length_ref[:, :1]
    mean = [jnp.zeros((LEN, 1), f32) for q in range(queries)]
    for f in range(slices):
        at = slice(f * feats, (f + 1) * feats)
        grad = grad_ref[f % nc, f // nc * queries:(f // nc + 1) * queries, :]
        pooled_grad = (grad - unit_ref[:, at] * inner) / length
        scaled_ref[:, at] = pooled_grad / LEN * gain_ref[:, at]
        for q in range(queries):
            product = hidden_ref[q * LEN:(q + 1) * LEN, at] * scaled_ref[q:q + 1, at]
            mean[q] += jnp.sum(product, axis=1, keepdims=True)
    inv = inv_ref[:, :1]
    factor = inv * inv * inv * (jnp.concatenate(mean, axis=0) / width)
    latent_t = latent_ref[...]
    acc = jnp.zeros((rank, tokens), f32)
    for mats_ref, at in adapter_slices(place_ref, own_ref, other_ref):
        for q in range(queries):
            of = slice(q * LEN, (q + 1) * LEN)
            hg_ref[of] = (
                inv[of] * scaled_ref[q:q + 1, at] - hidden_ref[of, at] * factor[of]
            ).astype(bf16)
        hidden_grad = hg_ref[...]
        acc += dot_rows(mats_ref[rank:], hidden_grad)
        up_ref[:, at] = adapter_scale_factor * dot(latent_t, hidden_grad)
    latent_grad = (adapter_scale_factor * acc).astype(bf16)
    first = place_ref[2 * own_ref.shape[0]] == 0
    for f in range(slices):
        down = dot(latent_grad, in_ref[:, f * feats:(f + 1) * feats])
        for x in range(nx):
            lanes = slice(x * cols, (x + 1) * cols)
            spot = slice(f * feats + x * cols, f * feats + (x + 1) * cols)
            for yh in range(nyh):
                tiles = []
                for c in range(nc):
                    of = slice((yh * nc + c) * out_rows, (yh * nc + c + 1) * out_rows)
                    tiles.append(
                        jnp.concatenate([down[of, lanes], up_ref[of, spot]], axis=0).astype(bf16)
                    )
                keep_ref[x, f * nyh + yh] = jnp.where(first, tiles[0], tiles[1])
                send_ref[x, f * nyh + yh] = jnp.where(first, tiles[1], tiles[0])


def split_rows(value, rows, cols):
    high = value.astype(bf16).astype(f32)
    middle = (value - high).astype(bf16).astype(f32)
    low = value - high - middle
    at = row_index((rows, value.shape[1]))
    parts = jnp.where(at == 0, high, jnp.where(at == 1, middle, jnp.where(at == 2, low, 0.0)))
    return jnp.concatenate([parts] * (cols // value.shape[1]), axis=1).astype(bf16)


def join(keep_ref, got_ref, loss_ref, out_ref):
    nx, blocks, rows, cols = keep_ref.shape
    parts = split_rows(loss_ref[0:1], rows, cols)
    for x in range(nx):
        out_ref[x, :blocks] = (
            keep_ref[x].astype(f32) + got_ref[x].astype(f32)
        ).astype(bf16)
        out_ref[x, blocks] = parts


def add_line(got_ref, out_ref):
    total = got_ref[0].astype(f32)
    for x in range(1, got_ref.shape[0]):
        total += got_ref[x].astype(f32)
    blocks, _, cols = out_ref.shape
    rows = got_ref.shape[2]
    loss = jnp.sum(total[blocks], axis=0, keepdims=True)[:, :128]
    out_ref[:, :rows] = total[:blocks].astype(bf16)
    out_ref[:, rows:] = jnp.broadcast_to(split_rows(loss, rows, cols)[None], (blocks, rows, cols))


def add_last(got_ref, out_ref):
    total = got_ref[0].astype(f32)
    for i in range(1, got_ref.shape[0]):
        total += got_ref[i].astype(f32)
    rows = out_ref.shape[0] - 8
    out_ref[:rows] = total[:rows]
    loss = jnp.sum(total[rows:], axis=0, keepdims=True)
    out_ref[rows:] = jnp.broadcast_to(loss, (8, out_ref.shape[1]))


def shards(sizes, adapter_in, frozen, gain, adapter_a, adapter_up_matrix, passages, positive):
    nzh, nzl, nyl, nx, nyh, nc = sizes
    izh, izl, iyl, ix, iyh, ic = (lax.axis_index(axis) for axis in AXES)
    rank = adapter_up_matrix.shape[0]
    feats = passages.shape[1]
    half = nyh * feats
    width = half * nc
    tokens = adapter_in.shape[0]
    queries = tokens // LEN
    group = passages.shape[0]
    rows = group // nyh
    ny = nzl * nyh
    ring = ny * nc
    members = nzh * nyl * nx
    shape = jax.ShapeDtypeStruct
    gain = gain.reshape(1, width)

    sent = jnp.broadcast_to(passages.reshape(1, nyh, rows, feats), (nzh, nyh, rows, feats))
    got = exchange(sent.reshape(nzh * nyh, rows, feats), ("zh", "yh"))

    mine = jnp.concatenate([adapter_a.T, adapter_up_matrix], axis=0)
    slots = [mine]
    for outer in (True, False, True)[: nyh - 1]:
        slots.append(swap_neighbours(slots[-1], nyl, nyh, outer))
        if len(slots) == 2:
            got, slots[1] = lax.optimization_barrier((got, slots[1]))
    own_mats = jnp.stack(slots)
    other_mats = swap_cores(own_mats)
    side = 1 - 2 * (1 - iyl)
    places = jnp.stack([iyh, iyh + side, iyh - side, iyh + 2][:nyh]).astype(jnp.int32) % nyh * nc
    place = jnp.concatenate([places + ic, places + 1 - ic, ic.reshape(1)]).astype(jnp.int32)

    got = got.reshape(nzh, nyh, rows, feats).transpose(0, 2, 1, 3).reshape(nzh * rows, half)
    got = jnp.broadcast_to(got[None], (nyl * nx, nzh * rows, half))
    block = exchange(got, ("yl", "x")).reshape(members * rows, half)
    columns = block.shape[0]

    latent_t, hidden, inv, unit, length, sent = call(
        functools.partial(forward, nyh, nc),
        [
            shape((rank, tokens), bf16),
            shape((tokens, width), f32),
            shape((tokens, 128), f32),
            shape((queries, width), f32),
            shape((queries, 128), f32),
            shape((ring, nyh * queries, feats), bf16),
        ],
        [place, adapter_in, frozen, gain, own_mats, other_mats],
        scratch=[((nc, nyh * queries, feats), f32)],
        scalars=1,
        flops=6 * tokens * rank * width,
    )
    sent, block = lax.optimization_barrier((sent, block))
    query = exchange(sent, RING)

    count = ring * 8
    at = lax.iota(jnp.int32, columns)
    at_xy, at_zh, at_row = at // (nzh * rows), at // rows % nzh, at % rows
    passage_id = ((at_zh * nzl + izl) * nyl * nx + at_xy) * group + iyh * rows + at_row
    own_pos = jnp.where(
        lax.iota(jnp.int32, nzl)[:, None] == izl, positive[None, :], -1
    ).reshape(ring, 1, queries)
    own_pos = jnp.broadcast_to(own_pos, (ring, 8 // queries, queries)).reshape(count)
    onehot = (own_pos[:, None] == passage_id[None, :]).astype(f32)
    (own,) = call(
        functools.partial(score, nyh),
        [shape((count + 8, columns), f32)],
        [query, block],
        flops=4 * ring * nyh * queries * columns * half,
    )
    other = swap_cores(own)
    expo, aux, by_row, by_col = call(
        exponentials,
        [
            shape((count, columns), f32),
            shape((8, columns), f32),
            shape((ny, 1, count), f32),
            shape((members, 1, columns), f32),
        ],
        [own, other, onehot],
    )
    by_row = exchange(by_row, ROW)
    by_col = exchange(by_col, COLUMN)
    sent, loss = call(
        functools.partial(weigh, nyh),
        [shape((ring, nyh * queries, feats), bf16), shape((8, 128), f32)],
        [expo, aux, onehot, by_row, by_col, block],
        scratch=[((ring * nyh * queries, feats), f32)],
        flops=2 * ring * nyh * queries * columns * half,
    )
    got = exchange(sent, RING)

    out_rows = rank // (nyh * nc)
    cols = width // (nzh * nzl * nyl * nx)
    blocks = nzh * ny
    keep, send = call(
        functools.partial(backward, nyh, nc),
        [shape((nyl * nx, blocks, 2 * out_rows, cols), bf16)] * 2,
        [place, got, unit, length, inv, hidden, gain, adapter_in, own_mats, other_mats, latent_t],
        scratch=[
            ((nc, nyh * queries, feats), f32),
            ((queries, width), f32),
            ((rank, width), f32),
            ((tokens, feats), bf16),
        ],
        scalars=1,
        flops=6 * tokens * rank * width,
    )
    (chip,) = call(
        join,
        [shape((nyl * nx, blocks + 1, 2 * out_rows, cols), bf16)],
        [keep, swap_cores(send), loss],
    )
    (line,) = call(
        add_line, [shape((blocks, 4 * out_rows, cols), bf16)], [exchange(chip, ("yl", "x"))]
    )
    (last,) = call(
        add_last,
        [shape((2 * out_rows + 8, cols), f32)],
        [exchange(line, ("zh", "zl", "yh"))],
    )
    adapter_grads = last[: 2 * out_rows].reshape(2, out_rows, cols)
    total_pairs = group * nzl * members
    loss = last[2 * out_rows, 0] / (2.0 * total_pairs) + inv_temp
    return (adapter_grads, loss)


def build(mesh, sizes):
    split = Mesh(mesh.devices.reshape(sizes), AXES)
    dp, fsdp = ("zh", "zl", "yl", "x"), ("yh", "c")
    placed = (
        P(AXES, None),
        P(AXES, None),
        P(),
        P(fsdp, None),
        P(None, fsdp),
        P(dp, fsdp),
        P(dp),
    )
    return jax.shard_map(
        lambda *args: shards(sizes, *args),
        mesh=split,
        in_specs=placed,
        out_specs=(P(None, fsdp, dp), P()),
        check_vma=False,
    )


def solution(mesh):
    return build(mesh, SIZES)
```

```python
import functools

import jax
import jax.numpy as jnp
from jax import lax
from jax.experimental import pallas as pl
from jax.experimental.pallas import tpu as pltpu
from jax.sharding import Mesh
from jax.sharding import PartitionSpec as P

LEN = 32


adapter_scale_factor = 0.25
inv_temp = 20.0
norm_eps = 1e-05

AXES = ("zh", "zl", "yl", "x", "yh", "c")
SIZES = (4, 2, 2, 4, 4, 2)
ROW, COLUMN, RING = ("yl", "yh"), ("zh", "zl", "x"), ("yl", "yh", "c")
MIB = 1 << 20
f32, bf16 = jnp.float32, jnp.bfloat16


def dot(left, right):
    return jnp.dot(left, right, preferred_element_type=f32)


def dot_rows(left, right):
    return lax.dot_general(left, right, (((1,), (1,)), ((), ())), preferred_element_type=f32)


def exchange(blocks, axes):
    return lax.all_to_all(blocks, axes, 0, 0, tiled=True)


def swap_cores(value):
    return lax.ppermute(value, "c", [(0, 1), (1, 0)])


def swap_neighbours(value, nyl, nyh, outer):
    pairs = []
    for yh in range(nyh):
        first, second = yh, nyh + yh
        if outer:
            first, second = nyh + yh, (yh + 1) % nyh
        pairs += [(first, second), (second, first)]
    return lax.ppermute(value, ("yl", "yh"), pairs)


def from_opposite(value, nyl, nyh):
    pairs = []
    for yh in range(nyh):
        for yl in range(nyl):
            pairs.append(((1 - yl) * nyh + (yh + 2) % nyh, yl * nyh + yh))
    return lax.ppermute(value, ("yl", "yh"), pairs)


def call(kernel, outs, args, scratch=(), scalars=0, flops=0):
    size = sum(a.size * a.dtype.itemsize for a in list(args[scalars:]) + list(outs))
    spare = [pltpu.VMEM(shape, kind) for shape, kind in scratch]
    spare_size = sum(a.size * a.dtype.itemsize for a in map(shape_of, scratch))
    return pl.pallas_call(
        kernel,
        out_shape=outs,
        in_specs=[pl.BlockSpec(memory_space=pltpu.SMEM)] * scalars
        + [pl.BlockSpec(memory_space=pltpu.VMEM)] * (len(args) - scalars),
        out_specs=[pl.BlockSpec(memory_space=pltpu.VMEM)] * len(outs),
        scratch_shapes=spare,
        compiler_params=pltpu.CompilerParams(
            vmem_limit_bytes=spare_size + 8 * MIB
        ),
        cost_estimate=pl.CostEstimate(flops=flops, bytes_accessed=size, transcendentals=0),
    )(*args)


def shape_of(pair):
    return jax.ShapeDtypeStruct(*pair)


def adapter_slices(place_ref, own_ref, other_ref):
    slots, _, feats = own_ref.shape
    for k in range(slots):
        for ref, place in ((own_ref, place_ref[k]), (other_ref, place_ref[slots + k])):
            yield ref.at[k], pl.ds(pl.multiple_of(place * feats, feats), feats)


def forward(nyh, nc, place_ref, in_ref, frozen_ref, gain_ref, own_ref, other_ref,
            latent_ref, hidden_ref, inv_ref, unit_ref, length_ref, send_ref, part_ref):
    _, both, feats = own_ref.shape
    slices = nyh * nc
    rank = both // 2
    tokens, width = in_ref.shape
    queries = tokens // LEN
    acc = jnp.zeros((tokens, rank), f32)
    acc_t = jnp.zeros((rank, tokens), f32)
    for mats_ref, at in adapter_slices(place_ref, own_ref, other_ref):
        part = in_ref[:, at]
        down = mats_ref[:rank]
        acc += dot_rows(part, down)
        acc_t += dot_rows(down, part)
    latent = acc.astype(bf16)
    latent_ref[...] = acc_t.astype(bf16)
    squares = jnp.zeros((tokens, 1), f32)
    for mats_ref, at in adapter_slices(place_ref, own_ref, other_ref):
        hidden = frozen_ref[:, at].astype(f32) + adapter_scale_factor * dot(
            latent, mats_ref[rank:]
        )
        hidden_ref[:, at] = hidden
        squares += jnp.sum(hidden * hidden, axis=1, keepdims=True)
    inv = lax.rsqrt(squares / width + norm_eps)
    inv_ref[...] = jnp.broadcast_to(inv, inv_ref.shape)
    total = jnp.zeros((queries, 1), f32)
    for f in range(slices):
        at = slice(f * feats, (f + 1) * feats)
        scaled = hidden_ref[:, at] * inv
        for q in range(queries):
            one = jnp.sum(scaled[q * LEN:(q + 1) * LEN], axis=0, keepdims=True)
            unit_ref[q:q + 1, at] = one * gain_ref[:, at] / LEN
        pooled = unit_ref[:, at]
        total += jnp.sum(pooled * pooled, axis=1, keepdims=True)
    length = jnp.sqrt(total)
    length_ref[...] = jnp.broadcast_to(length, length_ref.shape)
    for f in range(slices):
        at = slice(f * feats, (f + 1) * feats)
        unit = unit_ref[:, at] / length
        unit_ref[:, at] = unit
        part_ref[f % nc, f // nc * queries:(f // nc + 1) * queries, :] = unit
    for c in range(nc):
        rows = part_ref[c].astype(bf16)
        for y in range(send_ref.shape[0] // nc):
            send_ref[y * nc + c] = rows


def row_index(shape):
    return lax.broadcasted_iota(jnp.int32, shape, 0)


def score(nyh, query_ref, block_ref, out_ref):
    ring, rows, feats = query_ref.shape
    queries = rows // nyh
    columns = block_ref.shape[0]
    query = query_ref[...].reshape(ring * rows, feats)
    mine = row_index((ring * rows, columns)) // queries % nyh
    total = jnp.zeros((ring * rows, columns), f32)
    gram = jnp.zeros((columns, columns), f32)
    for k in range(nyh):
        part = block_ref[:, k * feats:(k + 1) * feats]
        total = jnp.where(mine == k, dot_rows(query, part), total)
        gram += dot_rows(part, part)
    total = total.reshape(ring, rows // 8, 8, columns)
    total = functools.reduce(jnp.add, [total[:, i] for i in range(rows // 8)])
    total = total.reshape(ring * 8, columns)
    count = ring * 8
    upper = row_index(total.shape) % 8 < 4
    total += jnp.where(upper, pltpu.roll(total, count - 4, 0), pltpu.roll(total, 4, 0))
    same = row_index(gram.shape) == lax.broadcasted_iota(jnp.int32, gram.shape, 1)
    norms = jnp.sum(jnp.where(same, gram, 0.0), axis=0, keepdims=True)
    out_ref[:count] = total
    out_ref[count:] = jnp.broadcast_to(norms, (8, columns))


def across(row):
    n = row.size
    return jnp.transpose(jnp.broadcast_to(row, (n, n)))


def exponentials(own_ref, other_ref, onehot_ref, expo_ref, aux_ref, rows_ref, cols_ref):
    count, columns = expo_ref.shape
    inv_norm = 1.0 / jnp.sqrt(own_ref[count:count + 1] + other_ref[count:count + 1])
    scores = inv_temp * ((own_ref[:count] + other_ref[:count]) * inv_norm)
    expo = jnp.exp(scores - inv_temp)
    expo_ref[...] = expo
    hits = 0.5 * jnp.sum(scores * onehot_ref[...])
    aux_ref[0:1] = inv_norm
    aux_ref[1:2] = jnp.full((1, columns), hits)
    row = across(jnp.sum(expo, axis=1, keepdims=True))[0:1]
    for y in range(rows_ref.shape[0]):
        rows_ref[y] = row
    col = 0.5 * jnp.sum(expo, axis=0, keepdims=True)
    for i in range(cols_ref.shape[0]):
        cols_ref[i] = col


def weigh(nyh, expo_ref, aux_ref, onehot_ref, rows_ref, cols_ref, block_ref,
          out_ref, loss_ref, total_ref):
    count, columns = expo_ref.shape
    ring, rows, feats = out_ref.shape
    queries = rows // nyh
    ny, members = rows_ref.shape[0], cols_ref.shape[0]
    row = functools.reduce(jnp.add, [rows_ref[y] for y in range(ny)])
    col = functools.reduce(jnp.add, [cols_ref[i] for i in range(members)])
    loss = (
        0.5 * jnp.sum(jnp.log(row), axis=1, keepdims=True) / ny
        + jnp.sum(jnp.log(col), axis=1, keepdims=True) / members
        - 2.0 * aux_ref[1:2, 0:1]
    )
    loss_ref[...] = jnp.broadcast_to(loss, loss_ref.shape)
    expo = expo_ref[...]
    weights = 0.5 * (expo / across(row)[:, :1] + expo / col) - onehot_ref[...]
    weights = (weights * aux_ref[0:1]).reshape(ring, 1, 8, columns)
    weights = jnp.broadcast_to(weights, (ring, rows // 8, 8, columns))
    weights = weights.reshape(ring * rows, columns).astype(bf16)
    mine = row_index((ring * rows, feats)) // queries % nyh
    for k in range(nyh):
        part = inv_temp * dot(weights, block_ref[:, k * feats:(k + 1) * feats])
        if k == 0:
            total_ref[...] = part
        else:
            total_ref[...] = jnp.where(mine == k, part, total_ref[...])
    out_ref[...] = total_ref[...].astype(bf16).reshape(out_ref.shape)


def backward(nyh, nc, place_ref, got_ref, unit_ref, length_ref, inv_ref, hidden_ref, gain_ref,
             in_ref, own_ref, other_ref, latent_ref, keep_ref, send_ref,
             grad_ref, scaled_ref, up_ref, hg_ref):
    _, both, feats = own_ref.shape
    slices = nyh * nc
    rank = both // 2
    tokens, width = in_ref.shape
    queries = tokens // LEN
    nx, _, pair_rows, cols = keep_ref.shape
    out_rows = pair_rows // 2
    for c in range(nc):
        total = got_ref[c].astype(f32)
        for y in range(1, got_ref.shape[0] // nc):
            total += got_ref[y * nc + c].astype(f32)
        grad_ref[c] = total
    inner = jnp.zeros((queries, 1), f32)
    for f in range(slices):
        at = slice(f * feats, (f + 1) * feats)
        grad = grad_ref[f % nc, f // nc * queries:(f // nc + 1) * queries, :]
        inner += jnp.sum(unit_ref[:, at] * grad, axis=1, keepdims=True)
    length = length_ref[:, :1]
    mean = [jnp.zeros((LEN, 1), f32) for q in range(queries)]
    for f in range(slices):
        at = slice(f * feats, (f + 1) * feats)
        grad = grad_ref[f % nc, f // nc * queries:(f // nc + 1) * queries, :]
        pooled_grad = (grad - unit_ref[:, at] * inner) / length
        scaled_ref[:, at] = pooled_grad / LEN * gain_ref[:, at]
        for q in range(queries):
            product = hidden_ref[q * LEN:(q + 1) * LEN, at] * scaled_ref[q:q + 1, at]
            mean[q] += jnp.sum(product, axis=1, keepdims=True)
    inv = inv_ref[:, :1]
    factor = inv * inv * inv * (jnp.concatenate(mean, axis=0) / width)
    latent_t = latent_ref[...]
    acc = jnp.zeros((rank, tokens), f32)
    for mats_ref, at in adapter_slices(place_ref, own_ref, other_ref):
        for q in range(queries):
            of = slice(q * LEN, (q + 1) * LEN)
            hg_ref[of] = (
                inv[of] * scaled_ref[q:q + 1, at] - hidden_ref[of, at] * factor[of]
            ).astype(bf16)
        hidden_grad = hg_ref[...]
        acc += dot_rows(mats_ref[rank:], hidden_grad)
        up_ref[:, at] = adapter_scale_factor * dot(latent_t, hidden_grad)
    latent_grad = (adapter_scale_factor * acc).astype(bf16)
    first = place_ref[2 * own_ref.shape[0]] == 0
    for f in range(slices):
        down = dot(latent_grad, in_ref[:, f * feats:(f + 1) * feats])
        for x in range(nx):
            lanes = slice(x * cols, (x + 1) * cols)
            spot = slice(f * feats + x * cols, f * feats + (x + 1) * cols)
            for yh in range(nyh):
                tiles = []
                for c in range(nc):
                    of = slice((yh * nc + c) * out_rows, (yh * nc + c + 1) * out_rows)
                    tiles.append(
                        jnp.concatenate([down[of, lanes], up_ref[of, spot]], axis=0).astype(bf16)
                    )
                keep_ref[x, f * nyh + yh] = jnp.where(first, tiles[0], tiles[1])
                send_ref[x, f * nyh + yh] = jnp.where(first, tiles[1], tiles[0])


def split_rows(value, rows, cols):
    high = value.astype(bf16).astype(f32)
    middle = (value - high).astype(bf16).astype(f32)
    low = value - high - middle
    at = row_index((rows, value.shape[1]))
    parts = jnp.where(at == 0, high, jnp.where(at == 1, middle, jnp.where(at == 2, low, 0.0)))
    return jnp.concatenate([parts] * (cols // value.shape[1]), axis=1).astype(bf16)


def join(keep_ref, got_ref, loss_ref, out_ref):
    nx, blocks, rows, cols = keep_ref.shape
    parts = split_rows(loss_ref[0:1], rows, cols)
    for x in range(nx):
        out_ref[x, :blocks] = (
            keep_ref[x].astype(f32) + got_ref[x].astype(f32)
        ).astype(bf16)
        out_ref[x, blocks] = parts


def add_line(got_ref, out_ref):
    total = got_ref[0].astype(f32)
    for x in range(1, got_ref.shape[0]):
        total += got_ref[x].astype(f32)
    blocks, _, cols = out_ref.shape
    rows = got_ref.shape[2]
    loss = jnp.sum(total[blocks], axis=0, keepdims=True)[:, :128]
    out_ref[:, :rows] = total[:blocks].astype(bf16)
    out_ref[:, rows:] = jnp.broadcast_to(split_rows(loss, rows, cols)[None], (blocks, rows, cols))


def add_last(got_ref, out_ref):
    total = got_ref[0].astype(f32)
    for i in range(1, got_ref.shape[0]):
        total += got_ref[i].astype(f32)
    rows = out_ref.shape[0] - 8
    out_ref[:rows] = total[:rows]
    loss = jnp.sum(total[rows:], axis=0, keepdims=True)
    out_ref[rows:] = jnp.broadcast_to(loss, (8, out_ref.shape[1]))


def shards(sizes, adapter_in, frozen, gain, adapter_a, adapter_up_matrix, passages, positive):
    nzh, nzl, nyl, nx, nyh, nc = sizes
    izh, izl, iyl, ix, iyh, ic = (lax.axis_index(axis) for axis in AXES)
    rank = adapter_up_matrix.shape[0]
    feats = passages.shape[1]
    half = nyh * feats
    width = half * nc
    tokens = adapter_in.shape[0]
    queries = tokens // LEN
    group = passages.shape[0]
    rows = group // nyh
    ny = nyl * nyh
    ring = ny * nc
    members = nzh * nzl * nx
    shape = jax.ShapeDtypeStruct
    gain = gain.reshape(1, width)

    sent = jnp.broadcast_to(passages.reshape(1, nyh, rows, feats), (nzh, nyh, rows, feats))
    got = exchange(sent.reshape(nzh * nyh, rows, feats), ("zh", "yh"))

    mine = jnp.concatenate([adapter_a.T, adapter_up_matrix], axis=0)
    slots = [mine]
    slots.append(swap_neighbours(mine, nyl, nyh, True))
    got, slots[1] = lax.optimization_barrier((got, slots[1]))
    if nyh == 4:
        slots.append(swap_neighbours(slots[1], nyl, nyh, False))
        slots.append(from_opposite(mine, nyl, nyh))
    own_mats = jnp.stack(slots)
    other_mats = swap_cores(own_mats)
    side = 1 - 2 * (1 - iyl)
    places = jnp.stack([iyh, iyh + side, iyh - side, iyh + 2][:nyh]).astype(jnp.int32) % nyh * nc
    place = jnp.concatenate([places + ic, places + 1 - ic, ic.reshape(1)]).astype(jnp.int32)

    got = got.reshape(nzh, nyh, rows, feats).transpose(0, 2, 1, 3).reshape(nzh * rows, half)
    got = jnp.broadcast_to(got[None], (nzl * nx, nzh * rows, half))
    block = exchange(got, ("zl", "x")).reshape(members * rows, half)
    columns = block.shape[0]

    latent_t, hidden, inv, unit, length, sent = call(
        functools.partial(forward, nyh, nc),
        [
            shape((rank, tokens), bf16),
            shape((tokens, width), f32),
            shape((tokens, 128), f32),
            shape((queries, width), f32),
            shape((queries, 128), f32),
            shape((ring, nyh * queries, feats), bf16),
        ],
        [place, adapter_in, frozen, gain, own_mats, other_mats],
        scratch=[((nc, nyh * queries, feats), f32)],
        scalars=1,
        flops=6 * tokens * rank * width,
    )
    sent, block = lax.optimization_barrier((sent, block))
    query = exchange(sent, RING)

    count = ring * 8
    at = lax.iota(jnp.int32, columns)
    at_zl, at_x, at_zh, at_row = (
        at // (nx * nzh * rows), at // (nzh * rows) % nx, at // rows % nzh, at % rows
    )
    passage_id = ((at_zh * nzl + at_zl) * nyl + iyl) * nx + at_x
    passage_id = passage_id * group + iyh * rows + at_row
    own_pos = jnp.where(
        lax.iota(jnp.int32, nyl)[:, None] == iyl, positive[None, :], -1
    ).reshape(ring, 1, queries)
    own_pos = jnp.broadcast_to(own_pos, (ring, 8 // queries, queries)).reshape(count)
    onehot = (own_pos[:, None] == passage_id[None, :]).astype(f32)
    (own,) = call(
        functools.partial(score, nyh),
        [shape((count + 8, columns), f32)],
        [query, block],
        flops=4 * ring * nyh * queries * columns * half,
    )
    other = swap_cores(own)
    expo, aux, by_row, by_col = call(
        exponentials,
        [
            shape((count, columns), f32),
            shape((8, columns), f32),
            shape((ny, 1, count), f32),
            shape((members, 1, columns), f32),
        ],
        [own, other, onehot],
    )
    by_row = exchange(by_row, ROW)
    by_col = exchange(by_col, COLUMN)
    sent, loss = call(
        functools.partial(weigh, nyh),
        [shape((ring, nyh * queries, feats), bf16), shape((8, 128), f32)],
        [expo, aux, onehot, by_row, by_col, block],
        scratch=[((ring * nyh * queries, feats), f32)],
        flops=2 * ring * nyh * queries * columns * half,
    )
    got = exchange(sent, RING)

    out_rows = rank // (nyh * nc)
    cols = width // (nzh * nzl * nyl * nx)
    blocks = nzh * nzl * nyh
    keep, send = call(
        functools.partial(backward, nyh, nc),
        [shape((nyl * nx, blocks, 2 * out_rows, cols), bf16)] * 2,
        [place, got, unit, length, inv, hidden, gain, adapter_in, own_mats, other_mats, latent_t],
        scratch=[
            ((nc, nyh * queries, feats), f32),
            ((queries, width), f32),
            ((rank, width), f32),
            ((tokens, feats), bf16),
        ],
        scalars=1,
        flops=6 * tokens * rank * width,
    )
    (chip,) = call(
        join,
        [shape((nyl * nx, blocks + 1, 2 * out_rows, cols), bf16)],
        [keep, swap_cores(send), loss],
    )
    (line,) = call(
        add_line, [shape((blocks, 4 * out_rows, cols), bf16)], [exchange(chip, ("yl", "x"))]
    )
    (last,) = call(
        add_last,
        [shape((2 * out_rows + 8, cols), f32)],
        [exchange(line, ("zh", "zl", "yh"))],
    )
    adapter_grads = last[: 2 * out_rows].reshape(2, out_rows, cols)
    total_pairs = group * nyl * members
    loss = last[2 * out_rows, 0] / (2.0 * total_pairs) + inv_temp
    return (adapter_grads, loss)


def build(mesh, sizes):
    split = Mesh(mesh.devices.reshape(sizes), AXES)
    dp, fsdp = ("zh", "zl", "yl", "x"), ("yh", "c")
    placed = (
        P(AXES, None),
        P(AXES, None),
        P(),
        P(fsdp, None),
        P(None, fsdp),
        P(dp, fsdp),
        P(dp),
    )
    return jax.shard_map(
        lambda *args: shards(sizes, *args),
        mesh=split,
        in_specs=placed,
        out_specs=(P(None, fsdp, dp), P()),
        check_vma=False,
    )


def solution(mesh):
    return build(mesh, SIZES)
```

```python
import functools

import jax
import jax.numpy as jnp
from jax import lax
from jax.experimental import pallas as pl
from jax.experimental.pallas import tpu as pltpu
from jax.sharding import Mesh
from jax.sharding import PartitionSpec as P

LEN = 32


adapter_scale_factor = 0.25
inv_temp = 20.0
norm_eps = 1e-05

AXES = ("zh", "zl", "yl", "x", "yh", "c")
SIZES = (4, 2, 2, 4, 4, 2)
ROW, COLUMN, RING = ("yl", "yh"), ("zh", "zl", "x"), ("yl", "yh", "c")
MIB = 1 << 20
f32, bf16 = jnp.float32, jnp.bfloat16


def dot(left, right):
    return jnp.dot(left, right, preferred_element_type=f32)


def dot_rows(left, right):
    return lax.dot_general(left, right, (((1,), (1,)), ((), ())), preferred_element_type=f32)


def exchange(blocks, axes):
    return lax.all_to_all(blocks, axes, 0, 0, tiled=True)


def swap_cores(value):
    return lax.ppermute(value, "c", [(0, 1), (1, 0)])


def swap_neighbours(value, nyl, nyh, outer):
    pairs = []
    for yh in range(nyh):
        first, second = yh, nyh + yh
        if outer:
            first, second = nyh + yh, (yh + 1) % nyh
        pairs += [(first, second), (second, first)]
    return lax.ppermute(value, ("yl", "yh"), pairs)


def from_opposite(value, nyl, nyh):
    pairs = []
    for yh in range(nyh):
        for yl in range(nyl):
            pairs.append(((1 - yl) * nyh + (yh + 2) % nyh, yl * nyh + yh))
    return lax.ppermute(value, ("yl", "yh"), pairs)


VMEM = pl.BlockSpec(memory_space=pltpu.VMEM)
SMEM = pl.BlockSpec(memory_space=pltpu.SMEM)
HBM = pl.BlockSpec(memory_space=pltpu.HBM)


def call(kernel, outs, args, spaces=None, out_spaces=None, scratch=(), copies=0, flops=0):
    spaces = spaces or [VMEM] * len(args)
    out_spaces = out_spaces or [VMEM] * len(outs)
    size = sum(a.size * a.dtype.itemsize for a in list(args) + list(outs))
    spare = [pltpu.VMEM(shape, kind) for shape, kind in scratch]
    spare_size = sum(
        a.size * a.dtype.itemsize for a in (jax.ShapeDtypeStruct(*pair) for pair in scratch)
    )
    if copies:
        spare.append(pltpu.SemaphoreType.DMA((copies,)))
    return pl.pallas_call(
        kernel,
        out_shape=outs,
        in_specs=spaces,
        out_specs=out_spaces,
        scratch_shapes=spare,
        compiler_params=pltpu.CompilerParams(vmem_limit_bytes=spare_size + 8 * MIB),
        cost_estimate=pl.CostEstimate(flops=flops, bytes_accessed=size, transcendentals=0),
    )(*args)


def adapter_slices(place_ref, own_ref, other_ref):
    slots, _, feats = own_ref.shape
    for k in range(slots):
        for ref, place in ((own_ref, place_ref[k]), (other_ref, place_ref[slots + k])):
            yield ref.at[k], pl.ds(pl.multiple_of(place * feats, feats), feats)


def project(place_ref, in_ref, own_ref, other_ref, latent_ref, latent_t_ref):
    rank = own_ref.shape[1] // 2
    tokens = in_ref.shape[0]
    acc = jnp.zeros((tokens, rank), f32)
    acc_t = jnp.zeros((rank, tokens), f32)
    for mats_ref, at in adapter_slices(place_ref, own_ref, other_ref):
        part = in_ref[:, at]
        down = mats_ref[:rank]
        acc += dot_rows(part, down)
        acc_t += dot_rows(down, part)
    latent_ref[...] = acc.astype(bf16)
    latent_t_ref[...] = acc_t.astype(bf16)


def hidden_slice(frozen_ref, latent, mats_ref, at):
    up = mats_ref[mats_ref.shape[0] // 2:]
    return frozen_ref[:, at].astype(f32) + adapter_scale_factor * dot(latent, up)


def forward(nyh, nc, place_ref, latent_ref, frozen_ref, gain_ref, own_ref, other_ref,
            inv_ref, unit_ref, length_ref, send_ref, hidden, part_ref):
    feats = own_ref.shape[2]
    slices = nyh * nc
    tokens, width = frozen_ref.shape
    queries = tokens // LEN
    latent = latent_ref[...]
    squares = jnp.zeros((tokens, 1), f32)
    for mats_ref, at in adapter_slices(place_ref, own_ref, other_ref):
        value = hidden_slice(frozen_ref, latent, mats_ref, at)
        hidden[:, at] = value
        squares += jnp.sum(value * value, axis=1, keepdims=True)
    inv = lax.rsqrt(squares / width + norm_eps)
    inv_ref[...] = jnp.broadcast_to(inv, inv_ref.shape)
    total = jnp.zeros((queries, 1), f32)
    for f in range(slices):
        at = slice(f * feats, (f + 1) * feats)
        scaled = hidden[:, at] * inv
        for q in range(queries):
            one = jnp.sum(scaled[q * LEN:(q + 1) * LEN], axis=0, keepdims=True)
            unit_ref[q:q + 1, at] = one * gain_ref[:, at] / LEN
        pooled = unit_ref[:, at]
        total += jnp.sum(pooled * pooled, axis=1, keepdims=True)
    length = jnp.sqrt(total)
    length_ref[...] = jnp.broadcast_to(length, length_ref.shape)
    for f in range(slices):
        at = slice(f * feats, (f + 1) * feats)
        unit = unit_ref[:, at] / length
        unit_ref[:, at] = unit
        part_ref[f % nc, f // nc * queries:(f // nc + 1) * queries, :] = unit
    for c in range(nc):
        rows = part_ref[c].astype(bf16)
        for y in range(send_ref.shape[0] // nc):
            send_ref[y * nc + c] = rows


def row_index(shape):
    return lax.broadcasted_iota(jnp.int32, shape, 0)


def start_slices(block_ref, parts, sems):
    feats = parts.shape[2]
    copies = [
        pltpu.make_async_copy(
            block_ref.at[:, k * feats:(k + 1) * feats], parts.at[k], sems.at[k]
        )
        for k in range(parts.shape[0])
    ]
    for copy in copies:
        copy.start()
    return copies


def score(nyh, query_ref, block_ref, out_ref, parts, sems):
    ring, rows, feats = query_ref.shape
    queries = rows // nyh
    columns = block_ref.shape[0]
    copies = start_slices(block_ref, parts, sems)
    query = query_ref[...].reshape(ring * rows, feats)
    mine = row_index((ring * rows, columns)) // queries % nyh
    total = jnp.zeros((ring * rows, columns), f32)
    gram = jnp.zeros((columns, columns), f32)
    for k in range(nyh):
        copies[k].wait()
        part = parts[k]
        total = jnp.where(mine == k, dot_rows(query, part), total)
        gram += dot_rows(part, part)
    total = total.reshape(ring, rows // 8, 8, columns)
    total = functools.reduce(jnp.add, [total[:, i] for i in range(rows // 8)])
    total = total.reshape(ring * 8, columns)
    count = ring * 8
    upper = row_index(total.shape) % 8 < 4
    total += jnp.where(upper, pltpu.roll(total, count - 4, 0), pltpu.roll(total, 4, 0))
    same = row_index(gram.shape) == lax.broadcasted_iota(jnp.int32, gram.shape, 1)
    norms = jnp.sum(jnp.where(same, gram, 0.0), axis=0, keepdims=True)
    out_ref[:count] = total
    out_ref[count:] = jnp.broadcast_to(norms, (8, columns))


def across(row):
    n = row.size
    return jnp.transpose(jnp.broadcast_to(row, (n, n)))


def exponentials(own_ref, other_ref, onehot_ref, expo_ref, aux_ref, sums_ref):
    count, columns = expo_ref.shape
    inv_norm = 1.0 / jnp.sqrt(own_ref[count:count + 1] + other_ref[count:count + 1])
    scores = inv_temp * ((own_ref[:count] + other_ref[:count]) * inv_norm)
    expo = jnp.exp(scores - inv_temp)
    expo_ref[...] = expo
    hits = 0.5 * jnp.sum(scores * onehot_ref[...])
    aux_ref[0:1] = inv_norm
    aux_ref[1:2] = jnp.full((1, columns), hits)
    row = across(jnp.sum(expo, axis=1, keepdims=True))[0:1]
    col = 0.5 * jnp.sum(expo, axis=0, keepdims=True)
    sums = jnp.concatenate([row, col], axis=1)
    for i in range(sums_ref.shape[0]):
        sums_ref[i] = sums


def combine(ny, place_ref, got_ref, row_ref, cols_ref):
    count = row_ref.shape[1]
    last = place_ref.shape[0] - 1
    first = place_ref[last - 1] * ny
    row = functools.reduce(jnp.add, [got_ref[first + y] for y in range(ny)])
    row_ref[...] = row[:, :count]
    peers = range(got_ref.shape[0] // ny)
    col = functools.reduce(jnp.add, [got_ref[zl * ny + place_ref[last]] for zl in peers])
    for i in range(cols_ref.shape[0]):
        cols_ref[i] = col[:, count:]


def weigh(nyh, ny, members, expo_ref, aux_ref, onehot_ref, row_ref, cols_ref, block_ref,
          out_ref, loss_ref, total_ref, parts, sems):
    count, columns = expo_ref.shape
    ring, rows, feats = out_ref.shape
    queries = rows // nyh
    copies = start_slices(block_ref, parts, sems)
    row = row_ref[...]
    col = functools.reduce(jnp.add, [cols_ref[i] for i in range(cols_ref.shape[0])])
    loss = (
        0.5 * jnp.sum(jnp.log(row), axis=1, keepdims=True) / ny
        + jnp.sum(jnp.log(col), axis=1, keepdims=True) / members
        - 2.0 * aux_ref[1:2, 0:1]
    )
    loss_ref[...] = jnp.broadcast_to(loss, loss_ref.shape)
    expo = expo_ref[...]
    weights = 0.5 * (expo / across(row)[:, :1] + expo / col) - onehot_ref[...]
    weights = (weights * aux_ref[0:1]).reshape(ring, 1, 8, columns)
    weights = jnp.broadcast_to(weights, (ring, rows // 8, 8, columns))
    weights = weights.reshape(ring * rows, columns).astype(bf16)
    mine = row_index((ring * rows, feats)) // queries % nyh
    for k in range(nyh):
        copies[k].wait()
        part = inv_temp * dot(weights, parts[k])
        if k == 0:
            total_ref[...] = part
        else:
            total_ref[...] = jnp.where(mine == k, part, total_ref[...])
    out_ref[...] = total_ref[...].astype(bf16).reshape(out_ref.shape)


def backward(nyh, nc, place_ref, got_ref, unit_ref, length_ref, inv_ref, frozen_ref, gain_ref,
             in_ref, own_ref, other_ref, latent_ref, latent_t_ref, keep_ref, send_ref,
             grad_ref, scaled_ref, up_ref, hg_ref, hidden):
    _, both, feats = own_ref.shape
    slices = nyh * nc
    rank = both // 2
    tokens, width = in_ref.shape
    queries = tokens // LEN
    nx, _, pair_rows, cols = keep_ref.shape
    out_rows = pair_rows // 2
    for c in range(nc):
        total = got_ref[c].astype(f32)
        for y in range(1, got_ref.shape[0] // nc):
            total += got_ref[y * nc + c].astype(f32)
        grad_ref[c] = total
    inner = jnp.zeros((queries, 1), f32)
    for f in range(slices):
        at = slice(f * feats, (f + 1) * feats)
        grad = grad_ref[f % nc, f // nc * queries:(f // nc + 1) * queries, :]
        inner += jnp.sum(unit_ref[:, at] * grad, axis=1, keepdims=True)
    length = length_ref[:, :1]
    latent = latent_ref[...]
    for mats_ref, at in adapter_slices(place_ref, own_ref, other_ref):
        hidden[:, at] = hidden_slice(frozen_ref, latent, mats_ref, at)
    mean = [jnp.zeros((LEN, 1), f32) for q in range(queries)]
    for f in range(slices):
        at = slice(f * feats, (f + 1) * feats)
        grad = grad_ref[f % nc, f // nc * queries:(f // nc + 1) * queries, :]
        pooled_grad = (grad - unit_ref[:, at] * inner) / length
        scaled_ref[:, at] = pooled_grad / LEN * gain_ref[:, at]
        for q in range(queries):
            product = hidden[q * LEN:(q + 1) * LEN, at] * scaled_ref[q:q + 1, at]
            mean[q] += jnp.sum(product, axis=1, keepdims=True)
    inv = inv_ref[:, :1]
    factor = inv * inv * inv * (jnp.concatenate(mean, axis=0) / width)
    latent_t = latent_t_ref[...]
    acc = jnp.zeros((rank, tokens), f32)
    for mats_ref, at in adapter_slices(place_ref, own_ref, other_ref):
        for q in range(queries):
            of = slice(q * LEN, (q + 1) * LEN)
            hg_ref[of] = (
                inv[of] * scaled_ref[q:q + 1, at] - hidden[of, at] * factor[of]
            ).astype(bf16)
        hidden_grad = hg_ref[...]
        acc += dot_rows(mats_ref[rank:], hidden_grad)
        up_ref[:, at] = adapter_scale_factor * dot(latent_t, hidden_grad)
    latent_grad = (adapter_scale_factor * acc).astype(bf16)
    first = place_ref[2 * own_ref.shape[0]] == 0
    for f in range(slices):
        down = dot(latent_grad, in_ref[:, f * feats:(f + 1) * feats])
        for x in range(nx):
            lanes = slice(x * cols, (x + 1) * cols)
            spot = slice(f * feats + x * cols, f * feats + (x + 1) * cols)
            for yh in range(nyh):
                tiles = []
                for c in range(nc):
                    of = slice((yh * nc + c) * out_rows, (yh * nc + c + 1) * out_rows)
                    tiles.append(
                        jnp.concatenate([down[of, lanes], up_ref[of, spot]], axis=0).astype(bf16)
                    )
                keep_ref[x, f * nyh + yh] = jnp.where(first, tiles[0], tiles[1])
                send_ref[x, f * nyh + yh] = jnp.where(first, tiles[1], tiles[0])


def split_rows(value, rows, cols):
    high = value.astype(bf16).astype(f32)
    middle = (value - high).astype(bf16).astype(f32)
    low = value - high - middle
    at = row_index((rows, value.shape[1]))
    parts = jnp.where(at == 0, high, jnp.where(at == 1, middle, jnp.where(at == 2, low, 0.0)))
    return jnp.concatenate([parts] * (cols // value.shape[1]), axis=1).astype(bf16)


def join(keep_ref, got_ref, loss_ref, out_ref):
    nx, blocks, rows, cols = keep_ref.shape
    parts = split_rows(loss_ref[0:1], rows, cols)
    for x in range(nx):
        out_ref[x, :blocks] = (
            keep_ref[x].astype(f32) + got_ref[x].astype(f32)
        ).astype(bf16)
        out_ref[x, blocks] = parts


def add_line(got_ref, out_ref):
    total = got_ref[0].astype(f32)
    for x in range(1, got_ref.shape[0]):
        total += got_ref[x].astype(f32)
    blocks, _, cols = out_ref.shape
    rows = got_ref.shape[2]
    loss = jnp.sum(total[blocks], axis=0, keepdims=True)[:, :128]
    out_ref[:, :rows] = total[:blocks].astype(bf16)
    out_ref[:, rows:] = jnp.broadcast_to(split_rows(loss, rows, cols)[None], (blocks, rows, cols))


def add_last(total_pairs, got_ref, out_ref, loss_ref):
    total = got_ref[0].astype(f32)
    for i in range(1, got_ref.shape[0]):
        total += got_ref[i].astype(f32)
    rows = out_ref.shape[1]
    out_ref[0] = total[:rows]
    out_ref[1] = total[rows:2 * rows]
    loss_ref[0, 0] = jnp.sum(total[2 * rows:, :1]) / (2.0 * total_pairs) + inv_temp


def shards(sizes, adapter_in, frozen, gain, adapter_a, adapter_up_matrix, passages, positive):
    nzh, nzl, nyl, nx, nyh, nc = sizes
    izh, izl, iyl, ix, iyh, ic = (lax.axis_index(axis) for axis in AXES)
    rank = adapter_up_matrix.shape[0]
    feats = passages.shape[1]
    half = nyh * feats
    width = half * nc
    tokens = adapter_in.shape[0]
    queries = tokens // LEN
    group = passages.shape[0]
    rows = group // nyh
    ny = nyl * nyh
    ring = ny * nc
    members = nzh * nzl * nx
    shape = jax.ShapeDtypeStruct
    gain = gain.reshape(1, width)

    sent = jnp.broadcast_to(passages.reshape(1, nyh, rows, feats), (nzh, nyh, rows, feats))
    got = exchange(sent.reshape(nzh * nyh, rows, feats), ("zh", "yh"))

    mine = jnp.concatenate([adapter_a.T, adapter_up_matrix], axis=0)
    slots = [mine]
    slots.append(swap_neighbours(mine, nyl, nyh, True))
    got, slots[1] = lax.optimization_barrier((got, slots[1]))
    if nyh == 4:
        slots.append(swap_neighbours(slots[1], nyl, nyh, False))
        slots.append(from_opposite(mine, nyl, nyh))
    own_mats = jnp.stack(slots)
    other_mats = swap_cores(own_mats)
    side = 1 - 2 * (1 - iyl)
    places = jnp.stack([iyh, iyh + side, iyh - side, iyh + 2][:nyh]).astype(jnp.int32) % nyh * nc
    ends = jnp.stack([ic, izl, iyl * nyh + iyh])
    place = jnp.concatenate([places + ic, places + 1 - ic, ends]).astype(jnp.int32)

    got = got.reshape(nzh, nyh, rows, feats).transpose(0, 2, 1, 3).reshape(nzh * rows, half)
    got = jnp.broadcast_to(got[None], (nzl * nx, nzh * rows, half))
    block = exchange(got, ("zl", "x")).reshape(members * rows, half)
    columns = block.shape[0]

    latent, latent_t = call(
        project,
        [shape((tokens, rank), bf16), shape((rank, tokens), bf16)],
        [place, adapter_in, own_mats, other_mats],
        spaces=[SMEM, VMEM, VMEM, VMEM],
        flops=4 * tokens * rank * width,
    )
    inv, unit, length, sent = call(
        functools.partial(forward, nyh, nc),
        [
            shape((tokens, 128), f32),
            shape((queries, width), f32),
            shape((queries, 128), f32),
            shape((ring, nyh * queries, feats), bf16),
        ],
        [place, latent, frozen, gain, own_mats, other_mats],
        spaces=[SMEM] + [VMEM] * 5,
        scratch=[((tokens, width), f32), ((nc, nyh * queries, feats), f32)],
        flops=2 * tokens * rank * width,
    )
    sent, block = lax.optimization_barrier((sent, block))
    query = exchange(sent, RING)

    count = ring * 8
    at = lax.iota(jnp.int32, columns)
    at_zl, at_x, at_zh, at_row = (
        at // (nx * nzh * rows), at // (nzh * rows) % nx, at // rows % nzh, at % rows
    )
    passage_id = ((at_zh * nzl + at_zl) * nyl + iyl) * nx + at_x
    passage_id = passage_id * group + iyh * rows + at_row
    own_pos = jnp.where(
        lax.iota(jnp.int32, nyl)[:, None] == iyl, positive[None, :], -1
    ).reshape(ring, 1, queries)
    own_pos = jnp.broadcast_to(own_pos, (ring, 8 // queries, queries)).reshape(count)
    onehot = (own_pos[:, None] == passage_id[None, :]).astype(f32)
    (own,) = call(
        functools.partial(score, nyh),
        [shape((count + 8, columns), f32)],
        [query, block],
        spaces=[VMEM, HBM],
        scratch=[((nyh, columns, feats), bf16)],
        copies=nyh,
        flops=4 * ring * nyh * queries * columns * half,
    )
    other = swap_cores(own)
    expo, aux, sent = call(
        exponentials,
        [
            shape((count, columns), f32),
            shape((8, columns), f32),
            shape((nzl * ny, 1, count + columns), f32),
        ],
        [own, other, onehot],
    )
    row, sent = call(
        functools.partial(combine, ny),
        [shape((1, count), f32), shape((nzh * nx, 1, columns), f32)],
        [place, exchange(sent, ("zl", *ROW))],
        spaces=[SMEM, VMEM],
    )
    sent, loss = call(
        functools.partial(weigh, nyh, ny, members),
        [shape((ring, nyh * queries, feats), bf16), shape((8, 128), f32)],
        [expo, aux, onehot, row, exchange(sent, ("zh", "x")), block],
        spaces=[VMEM] * 5 + [HBM],
        scratch=[((ring * nyh * queries, feats), f32), ((nyh, columns, feats), bf16)],
        copies=nyh,
        flops=2 * ring * nyh * queries * columns * half,
    )
    got = exchange(sent, RING)

    out_rows = rank // (nyh * nc)
    cols = width // (nzh * nzl * nyl * nx)
    blocks = nzh * nzl * nyh
    keep, send = call(
        functools.partial(backward, nyh, nc),
        [shape((nyl * nx, blocks, 2 * out_rows, cols), bf16)] * 2,
        [
            place, got, unit, length, inv, frozen, gain, adapter_in, own_mats, other_mats,
            latent, latent_t,
        ],
        spaces=[SMEM] + [VMEM] * 11,
        scratch=[
            ((nc, nyh * queries, feats), f32),
            ((queries, width), f32),
            ((rank, width), f32),
            ((tokens, feats), bf16),
            ((tokens, width), f32),
        ],
        flops=8 * tokens * rank * width,
    )
    (chip,) = call(
        join,
        [shape((nyl * nx, blocks + 1, 2 * out_rows, cols), bf16)],
        [keep, swap_cores(send), loss],
    )
    (line,) = call(
        add_line, [shape((blocks, 4 * out_rows, cols), bf16)], [exchange(chip, ("yl", "x"))]
    )
    adapter_grads, loss = call(
        functools.partial(add_last, group * nyl * members),
        [shape((2, out_rows, cols), f32), shape((1, 1), f32)],
        [exchange(line, ("zh", "zl", "yh"))],
        out_spaces=[VMEM, SMEM],
    )
    return (adapter_grads, loss.reshape(()))


def build(mesh, sizes):
    split = Mesh(mesh.devices.reshape(sizes), AXES)
    dp, fsdp = ("zh", "zl", "yl", "x"), ("yh", "c")
    placed = (
        P(AXES, None),
        P(AXES, None),
        P(),
        P(fsdp, None),
        P(None, fsdp),
        P(dp, fsdp),
        P(dp),
    )
    return jax.shard_map(
        lambda *args: shards(sizes, *args),
        mesh=split,
        in_specs=placed,
        out_specs=(P(None, fsdp, dp), P()),
        check_vma=False,
    )


def solution(mesh):
    return build(mesh, SIZES)
```

```python
import functools

import jax
import jax.numpy as jnp
from jax import lax
from jax.experimental import pallas as pl
from jax.experimental.pallas import tpu as pltpu
from jax.sharding import Mesh
from jax.sharding import PartitionSpec as P

LEN = 32


adapter_scale_factor = 0.25
inv_temp = 20.0
norm_eps = 1e-05

AXES = ("zh", "zl", "yl", "x", "yh", "c")
SIZES = (4, 2, 2, 4, 4, 2)
ROW, COLUMN, RING = ("yl", "yh"), ("zh", "zl", "x"), ("yl", "yh", "c")
MIB = 1 << 20
f32, bf16 = jnp.float32, jnp.bfloat16


def dot(left, right):
    return jnp.dot(left, right, preferred_element_type=f32)


def dot_rows(left, right):
    return lax.dot_general(left, right, (((1,), (1,)), ((), ())), preferred_element_type=f32)


def exchange(blocks, axes):
    return lax.all_to_all(blocks, axes, 0, 0, tiled=True)


def swap_cores(value):
    return lax.ppermute(value, "c", [(0, 1), (1, 0)])


def swap_neighbours(value, nyl, nyh, outer):
    pairs = []
    for yh in range(nyh):
        first, second = yh, nyh + yh
        if outer:
            first, second = nyh + yh, (yh + 1) % nyh
        pairs += [(first, second), (second, first)]
    return lax.ppermute(value, ("yl", "yh"), pairs)


def from_opposite(value, nyl, nyh):
    pairs = []
    for yh in range(nyh):
        for yl in range(nyl):
            pairs.append(((1 - yl) * nyh + (yh + 2) % nyh, yl * nyh + yh))
    return lax.ppermute(value, ("yl", "yh"), pairs)


VMEM = pl.BlockSpec(memory_space=pltpu.VMEM)
SMEM = pl.BlockSpec(memory_space=pltpu.SMEM)
HBM = pl.BlockSpec(memory_space=pltpu.HBM)


def call(kernel, outs, args, spaces=None, out_spaces=None, scratch=(), copies=0, flops=0):
    spaces = spaces or [VMEM] * len(args)
    out_spaces = out_spaces or [VMEM] * len(outs)
    size = sum(a.size * a.dtype.itemsize for a in list(args) + list(outs))
    spare = [pltpu.VMEM(shape, kind) for shape, kind in scratch]
    spare_size = sum(
        a.size * a.dtype.itemsize for a in (jax.ShapeDtypeStruct(*pair) for pair in scratch)
    )
    if copies:
        spare.append(pltpu.SemaphoreType.DMA((copies,)))
    return pl.pallas_call(
        kernel,
        out_shape=outs,
        in_specs=spaces,
        out_specs=out_spaces,
        scratch_shapes=spare,
        compiler_params=pltpu.CompilerParams(vmem_limit_bytes=spare_size + 8 * MIB),
        cost_estimate=pl.CostEstimate(flops=flops, bytes_accessed=size, transcendentals=0),
    )(*args)


def adapter_slices(place_ref, mats, first=0):
    slots = (place_ref.shape[0] - 3) // 2
    for own_ref, other_ref in zip(mats[::2], mats[1::2]):
        feats = own_ref.shape[2]
        for k in range(own_ref.shape[0]):
            for ref, at in ((own_ref, first + k), (other_ref, slots + first + k)):
                start = pl.multiple_of(place_ref[at] * feats, feats)
                yield ref.at[k], pl.ds(start, feats)
        first += own_ref.shape[0]


def project(first, place_ref, in_ref, *refs):
    mats, refs = refs[:2], refs[2:]
    rank = mats[0].shape[1] // 2
    tokens = in_ref.shape[0]
    if first == 0:
        acc, acc_t = jnp.zeros((tokens, rank), f32), jnp.zeros((rank, tokens), f32)
    else:
        acc, acc_t = refs[0][...], refs[1][...]
    for mats_ref, at in adapter_slices(place_ref, mats, first):
        part = in_ref[:, at]
        down = mats_ref[:rank]
        acc += dot_rows(part, down)
        acc_t += dot_rows(down, part)
    out_ref, out_t_ref = refs[-2:]
    out_ref[...] = acc.astype(out_ref.dtype)
    out_t_ref[...] = acc_t.astype(out_t_ref.dtype)


def hidden_slice(frozen_ref, latent, mats_ref, at):
    up = mats_ref[mats_ref.shape[0] // 2:]
    return frozen_ref[:, at].astype(f32) + adapter_scale_factor * dot(latent, up)


def forward(nyh, nc, place_ref, latent_ref, frozen_ref, gain_ref, *refs):
    *mats, inv_ref, unit_ref, length_ref, send_ref, hidden, part_ref = refs
    feats = part_ref.shape[2]
    slices = nyh * nc
    tokens, width = frozen_ref.shape
    queries = tokens // LEN
    latent = latent_ref[...]
    squares = jnp.zeros((tokens, 1), f32)
    for mats_ref, at in adapter_slices(place_ref, mats):
        value = hidden_slice(frozen_ref, latent, mats_ref, at)
        hidden[:, at] = value
        squares += jnp.sum(value * value, axis=1, keepdims=True)
    inv = lax.rsqrt(squares / width + norm_eps)
    inv_ref[...] = jnp.broadcast_to(inv, inv_ref.shape)
    total = jnp.zeros((queries, 1), f32)
    for f in range(slices):
        at = slice(f * feats, (f + 1) * feats)
        scaled = hidden[:, at] * inv
        for q in range(queries):
            one = jnp.sum(scaled[q * LEN:(q + 1) * LEN], axis=0, keepdims=True)
            unit_ref[q:q + 1, at] = one * gain_ref[:, at] / LEN
        pooled = unit_ref[:, at]
        total += jnp.sum(pooled * pooled, axis=1, keepdims=True)
    length = jnp.sqrt(total)
    length_ref[...] = jnp.broadcast_to(length, length_ref.shape)
    for f in range(slices):
        at = slice(f * feats, (f + 1) * feats)
        unit = unit_ref[:, at] / length
        unit_ref[:, at] = unit
        part_ref[f % nc, f // nc * queries:(f // nc + 1) * queries, :] = unit
    for c in range(nc):
        rows = part_ref[c].astype(bf16)
        for y in range(send_ref.shape[0] // nc):
            send_ref[y * nc + c] = rows


def row_index(shape):
    return lax.broadcasted_iota(jnp.int32, shape, 0)


def start_slices(block_ref, parts, sems):
    feats = parts.shape[2]
    copies = [
        pltpu.make_async_copy(
            block_ref.at[:, k * feats:(k + 1) * feats], parts.at[k], sems.at[k]
        )
        for k in range(parts.shape[0])
    ]
    for copy in copies:
        copy.start()
    return copies


def score(nyh, query_ref, block_ref, out_ref, parts, sems):
    ring, rows, feats = query_ref.shape
    queries = rows // nyh
    columns = block_ref.shape[0]
    copies = start_slices(block_ref, parts, sems)
    query = query_ref[...].reshape(ring * rows, feats)
    mine = row_index((ring * rows, columns)) // queries % nyh
    total = jnp.zeros((ring * rows, columns), f32)
    gram = jnp.zeros((columns, columns), f32)
    for k in range(nyh):
        copies[k].wait()
        part = parts[k]
        total = jnp.where(mine == k, dot_rows(query, part), total)
        gram += dot_rows(part, part)
    total = total.reshape(ring, rows // 8, 8, columns)
    total = functools.reduce(jnp.add, [total[:, i] for i in range(rows // 8)])
    total = total.reshape(ring * 8, columns)
    count = ring * 8
    upper = row_index(total.shape) % 8 < 4
    total += jnp.where(upper, pltpu.roll(total, count - 4, 0), pltpu.roll(total, 4, 0))
    same = row_index(gram.shape) == lax.broadcasted_iota(jnp.int32, gram.shape, 1)
    norms = jnp.sum(jnp.where(same, gram, 0.0), axis=0, keepdims=True)
    out_ref[:count] = total
    out_ref[count:] = jnp.broadcast_to(norms, (8, columns))


def across(row):
    n = row.size
    return jnp.transpose(jnp.broadcast_to(row, (n, n)))


def exponentials(own_ref, other_ref, onehot_ref, expo_ref, aux_ref, sums_ref):
    count, columns = expo_ref.shape
    inv_norm = 1.0 / jnp.sqrt(own_ref[count:count + 1] + other_ref[count:count + 1])
    scores = inv_temp * ((own_ref[:count] + other_ref[:count]) * inv_norm)
    expo = jnp.exp(scores - inv_temp)
    expo_ref[...] = expo
    hits = 0.5 * jnp.sum(scores * onehot_ref[...])
    aux_ref[0:1] = inv_norm
    aux_ref[1:2] = jnp.full((1, columns), hits)
    row = across(jnp.sum(expo, axis=1, keepdims=True))[0:1]
    col = 0.5 * jnp.sum(expo, axis=0, keepdims=True)
    sums = jnp.concatenate([row, col], axis=1)
    for i in range(sums_ref.shape[0]):
        sums_ref[i] = sums


def combine(ny, place_ref, got_ref, row_ref, cols_ref):
    count = row_ref.shape[1]
    last = place_ref.shape[0] - 1
    first = place_ref[last - 1] * ny
    row = functools.reduce(jnp.add, [got_ref[first + y] for y in range(ny)])
    row_ref[...] = row[:, :count]
    peers = range(got_ref.shape[0] // ny)
    col = functools.reduce(jnp.add, [got_ref[zl * ny + place_ref[last]] for zl in peers])
    for i in range(cols_ref.shape[0]):
        cols_ref[i] = col[:, count:]


def weigh(nyh, ny, members, expo_ref, aux_ref, onehot_ref, row_ref, cols_ref, block_ref,
          out_ref, loss_ref, total_ref, parts, sems):
    count, columns = expo_ref.shape
    ring, rows, feats = out_ref.shape
    queries = rows // nyh
    copies = start_slices(block_ref, parts, sems)
    row = row_ref[...]
    col = functools.reduce(jnp.add, [cols_ref[i] for i in range(cols_ref.shape[0])])
    loss = (
        0.5 * jnp.sum(jnp.log(row), axis=1, keepdims=True) / ny
        + jnp.sum(jnp.log(col), axis=1, keepdims=True) / members
        - 2.0 * aux_ref[1:2, 0:1]
    )
    loss_ref[...] = jnp.broadcast_to(loss, loss_ref.shape)
    expo = expo_ref[...]
    weights = 0.5 * (expo / across(row)[:, :1] + expo / col) - onehot_ref[...]
    weights = (weights * aux_ref[0:1]).reshape(ring, 1, 8, columns)
    weights = jnp.broadcast_to(weights, (ring, rows // 8, 8, columns))
    weights = weights.reshape(ring * rows, columns).astype(bf16)
    mine = row_index((ring * rows, feats)) // queries % nyh
    for k in range(nyh):
        copies[k].wait()
        part = inv_temp * dot(weights, parts[k])
        if k == 0:
            total_ref[...] = part
        else:
            total_ref[...] = jnp.where(mine == k, part, total_ref[...])
    out_ref[...] = total_ref[...].astype(bf16).reshape(out_ref.shape)


def backward(nyh, nc, place_ref, got_ref, unit_ref, length_ref, inv_ref, frozen_ref, gain_ref,
             in_ref, latent_ref, latent_t_ref, *refs):
    *mats, keep_ref, send_ref, grad_ref, scaled_ref, up_ref, hg_ref, hidden = refs
    _, both, feats = mats[0].shape
    slices = nyh * nc
    rank = both // 2
    tokens, width = in_ref.shape
    queries = tokens // LEN
    nx, _, pair_rows, cols = keep_ref.shape
    out_rows = pair_rows // 2
    for c in range(nc):
        total = got_ref[c].astype(f32)
        for y in range(1, got_ref.shape[0] // nc):
            total += got_ref[y * nc + c].astype(f32)
        grad_ref[c] = total
    inner = jnp.zeros((queries, 1), f32)
    for f in range(slices):
        at = slice(f * feats, (f + 1) * feats)
        grad = grad_ref[f % nc, f // nc * queries:(f // nc + 1) * queries, :]
        inner += jnp.sum(unit_ref[:, at] * grad, axis=1, keepdims=True)
    length = length_ref[:, :1]
    latent = latent_ref[...]
    for mats_ref, at in adapter_slices(place_ref, mats):
        hidden[:, at] = hidden_slice(frozen_ref, latent, mats_ref, at)
    mean = [jnp.zeros((LEN, 1), f32) for q in range(queries)]
    for f in range(slices):
        at = slice(f * feats, (f + 1) * feats)
        grad = grad_ref[f % nc, f // nc * queries:(f // nc + 1) * queries, :]
        pooled_grad = (grad - unit_ref[:, at] * inner) / length
        scaled_ref[:, at] = pooled_grad / LEN * gain_ref[:, at]
        for q in range(queries):
            product = hidden[q * LEN:(q + 1) * LEN, at] * scaled_ref[q:q + 1, at]
            mean[q] += jnp.sum(product, axis=1, keepdims=True)
    inv = inv_ref[:, :1]
    factor = inv * inv * inv * (jnp.concatenate(mean, axis=0) / width)
    latent_t = latent_t_ref[...]
    acc = jnp.zeros((rank, tokens), f32)
    for mats_ref, at in adapter_slices(place_ref, mats):
        for q in range(queries):
            of = slice(q * LEN, (q + 1) * LEN)
            hg_ref[of] = (
                inv[of] * scaled_ref[q:q + 1, at] - hidden[of, at] * factor[of]
            ).astype(bf16)
        hidden_grad = hg_ref[...]
        acc += dot_rows(mats_ref[rank:], hidden_grad)
        up_ref[:, at] = adapter_scale_factor * dot(latent_t, hidden_grad)
    latent_grad = (adapter_scale_factor * acc).astype(bf16)
    first = place_ref[place_ref.shape[0] - 3] == 0
    for f in range(slices):
        down = dot(latent_grad, in_ref[:, f * feats:(f + 1) * feats])
        for x in range(nx):
            lanes = slice(x * cols, (x + 1) * cols)
            spot = slice(f * feats + x * cols, f * feats + (x + 1) * cols)
            for yh in range(nyh):
                tiles = []
                for c in range(nc):
                    of = slice((yh * nc + c) * out_rows, (yh * nc + c + 1) * out_rows)
                    tiles.append(
                        jnp.concatenate([down[of, lanes], up_ref[of, spot]], axis=0).astype(bf16)
                    )
                keep_ref[x, f * nyh + yh] = jnp.where(first, tiles[0], tiles[1])
                send_ref[x, f * nyh + yh] = jnp.where(first, tiles[1], tiles[0])


def split_rows(value, rows, cols):
    high = value.astype(bf16).astype(f32)
    middle = (value - high).astype(bf16).astype(f32)
    low = value - high - middle
    at = row_index((rows, value.shape[1]))
    parts = jnp.where(at == 0, high, jnp.where(at == 1, middle, jnp.where(at == 2, low, 0.0)))
    return jnp.concatenate([parts] * (cols // value.shape[1]), axis=1).astype(bf16)


def join(keep_ref, got_ref, loss_ref, out_ref):
    nx, blocks, rows, cols = keep_ref.shape
    parts = split_rows(loss_ref[0:1], rows, cols)
    for x in range(nx):
        out_ref[x, :blocks] = (
            keep_ref[x].astype(f32) + got_ref[x].astype(f32)
        ).astype(bf16)
        out_ref[x, blocks] = parts


def add_line(got_ref, out_ref):
    total = got_ref[0].astype(f32)
    for x in range(1, got_ref.shape[0]):
        total += got_ref[x].astype(f32)
    blocks, _, cols = out_ref.shape
    rows = got_ref.shape[2]
    loss = jnp.sum(total[blocks], axis=0, keepdims=True)[:, :128]
    out_ref[:, :rows] = total[:blocks].astype(bf16)
    out_ref[:, rows:] = jnp.broadcast_to(split_rows(loss, rows, cols)[None], (blocks, rows, cols))


def add_last(total_pairs, got_ref, out_ref, loss_ref):
    total = got_ref[0].astype(f32)
    for i in range(1, got_ref.shape[0]):
        total += got_ref[i].astype(f32)
    rows = out_ref.shape[1]
    out_ref[0] = total[:rows]
    out_ref[1] = total[rows:2 * rows]
    loss_ref[0, 0] = jnp.sum(total[2 * rows:, :1]) / (2.0 * total_pairs) + inv_temp


def shards(sizes, adapter_in, frozen, gain, adapter_a, adapter_up_matrix, passages, positive):
    nzh, nzl, nyl, nx, nyh, nc = sizes
    izh, izl, iyl, ix, iyh, ic = (lax.axis_index(axis) for axis in AXES)
    rank = adapter_up_matrix.shape[0]
    feats = passages.shape[1]
    half = nyh * feats
    width = half * nc
    tokens = adapter_in.shape[0]
    queries = tokens // LEN
    group = passages.shape[0]
    rows = group // nyh
    ny = nyl * nyh
    ring = ny * nc
    members = nzh * nzl * nx
    shape = jax.ShapeDtypeStruct
    gain = gain.reshape(1, width)

    sent = jnp.broadcast_to(passages.reshape(1, nyh, rows, feats), (nzh, nyh, rows, feats))
    got = exchange(sent.reshape(nzh * nyh, rows, feats), ("zh", "yh"))

    mine = jnp.concatenate([adapter_a.T, adapter_up_matrix], axis=0)
    slots = [mine]
    slots.append(swap_neighbours(mine, nyl, nyh, True))
    got, slots[1] = lax.optimization_barrier((got, slots[1]))
    if nyh == 4:
        slots.append(swap_neighbours(slots[1], nyl, nyh, False))
        slots.append(from_opposite(mine, nyl, nyh))
    side = 1 - 2 * (1 - iyl)
    places = jnp.stack([iyh, iyh + side, iyh - side, iyh + 2][:nyh]).astype(jnp.int32) % nyh * nc
    ends = jnp.stack([ic, izl, iyl * nyh + iyh])
    place = jnp.concatenate([places + ic, places + 1 - ic, ends]).astype(jnp.int32)

    got = got.reshape(nzh, nyh, rows, feats).transpose(0, 2, 1, 3).reshape(nzh * rows, half)
    got = jnp.broadcast_to(got[None], (nzl * nx, nzh * rows, half))
    block = exchange(got, ("zl", "x")).reshape(members * rows, half)
    columns = block.shape[0]

    mats, sums = [], []
    for some in (slots[:2], slots[2:]):
        if not some:
            continue
        if mats:
            (some, sums) = lax.optimization_barrier((some, sums))
        mats.append(jnp.stack(some))
        mats.append(swap_cores(mats[-1]))
        kind = bf16 if len(mats) == 2 * nyh // 2 else f32
        sums = call(
            functools.partial(project, len(mats) - 2),
            [shape((tokens, rank), kind), shape((rank, tokens), kind)],
            [place, adapter_in, *mats[-2:], *sums],
            spaces=[SMEM] + [VMEM] * (3 + len(sums)),
            flops=2 * tokens * rank * width,
        )
    latent, latent_t = sums
    inv, unit, length, sent = call(
        functools.partial(forward, nyh, nc),
        [
            shape((tokens, 128), f32),
            shape((queries, width), f32),
            shape((queries, 128), f32),
            shape((ring, nyh * queries, feats), bf16),
        ],
        [place, latent, frozen, gain, *mats],
        spaces=[SMEM] + [VMEM] * (3 + len(mats)),
        scratch=[((tokens, width), f32), ((nc, nyh * queries, feats), f32)],
        flops=2 * tokens * rank * width,
    )
    sent, block = lax.optimization_barrier((sent, block))
    query = exchange(sent, RING)

    count = ring * 8
    at = lax.iota(jnp.int32, columns)
    at_zl, at_x, at_zh, at_row = (
        at // (nx * nzh * rows), at // (nzh * rows) % nx, at // rows % nzh, at % rows
    )
    passage_id = ((at_zh * nzl + at_zl) * nyl + iyl) * nx + at_x
    passage_id = passage_id * group + iyh * rows + at_row
    own_pos = jnp.where(
        lax.iota(jnp.int32, nyl)[:, None] == iyl, positive[None, :], -1
    ).reshape(ring, 1, queries)
    own_pos = jnp.broadcast_to(own_pos, (ring, 8 // queries, queries)).reshape(count)
    onehot = (own_pos[:, None] == passage_id[None, :]).astype(f32)
    (own,) = call(
        functools.partial(score, nyh),
        [shape((count + 8, columns), f32)],
        [query, block],
        spaces=[VMEM, HBM],
        scratch=[((nyh, columns, feats), bf16)],
        copies=nyh,
        flops=4 * ring * nyh * queries * columns * half,
    )
    other = swap_cores(own)
    expo, aux, sent = call(
        exponentials,
        [
            shape((count, columns), f32),
            shape((8, columns), f32),
            shape((nzl * ny, 1, count + columns), f32),
        ],
        [own, other, onehot],
    )
    row, sent = call(
        functools.partial(combine, ny),
        [shape((1, count), f32), shape((nzh * nx, 1, columns), f32)],
        [place, exchange(sent, ("zl", *ROW))],
        spaces=[SMEM, VMEM],
    )
    sent, loss = call(
        functools.partial(weigh, nyh, ny, members),
        [shape((ring, nyh * queries, feats), bf16), shape((8, 128), f32)],
        [expo, aux, onehot, row, exchange(sent, ("zh", "x")), block],
        spaces=[VMEM] * 5 + [HBM],
        scratch=[((ring * nyh * queries, feats), f32), ((nyh, columns, feats), bf16)],
        copies=nyh,
        flops=2 * ring * nyh * queries * columns * half,
    )
    got = exchange(sent, RING)

    out_rows = rank // (nyh * nc)
    cols = width // (nzh * nzl * nyl * nx)
    blocks = nzh * nzl * nyh
    keep, send = call(
        functools.partial(backward, nyh, nc),
        [shape((nyl * nx, blocks, 2 * out_rows, cols), bf16)] * 2,
        [
            place, got, unit, length, inv, frozen, gain, adapter_in, latent, latent_t, *mats,
        ],
        spaces=[SMEM] + [VMEM] * (9 + len(mats)),
        scratch=[
            ((nc, nyh * queries, feats), f32),
            ((queries, width), f32),
            ((rank, width), f32),
            ((tokens, feats), bf16),
            ((tokens, width), f32),
        ],
        flops=8 * tokens * rank * width,
    )
    (chip,) = call(
        join,
        [shape((nyl * nx, blocks + 1, 2 * out_rows, cols), bf16)],
        [keep, swap_cores(send), loss],
    )
    (line,) = call(
        add_line, [shape((blocks, 4 * out_rows, cols), bf16)], [exchange(chip, ("yl", "x"))]
    )
    adapter_grads, loss = call(
        functools.partial(add_last, group * nyl * members),
        [shape((2, out_rows, cols), f32), shape((1, 1), f32)],
        [exchange(line, ("zh", "zl", "yh"))],
        out_spaces=[VMEM, SMEM],
    )
    return (adapter_grads, loss.reshape(()))


def build(mesh, sizes):
    split = Mesh(mesh.devices.reshape(sizes), AXES)
    dp, fsdp = ("zh", "zl", "yl", "x"), ("yh", "c")
    placed = (
        P(AXES, None),
        P(AXES, None),
        P(),
        P(fsdp, None),
        P(None, fsdp),
        P(dp, fsdp),
        P(dp),
    )
    return jax.shard_map(
        lambda *args: shards(sizes, *args),
        mesh=split,
        in_specs=placed,
        out_specs=(P(None, fsdp, dp), P()),
        check_vma=False,
    )


def solution(mesh):
    return build(mesh, SIZES)
```

```python
import functools

import jax
import jax.numpy as jnp
from jax import lax
from jax.experimental import pallas as pl
from jax.experimental.pallas import tpu as pltpu
from jax.sharding import Mesh
from jax.sharding import PartitionSpec as P

LEN = 32


adapter_scale_factor = 0.25
inv_temp = 20.0
norm_eps = 1e-05

AXES = ("zh", "zl", "yl", "x", "yh", "c")
SIZES = (4, 2, 2, 4, 4, 2)
ROW, COLUMN, RING = ("yl", "yh"), ("zh", "zl", "x"), ("yl", "yh", "c")
MIB = 1 << 20
f32, bf16 = jnp.float32, jnp.bfloat16


def dot(left, right):
    return jnp.dot(left, right, preferred_element_type=f32)


def dot_rows(left, right):
    return lax.dot_general(left, right, (((1,), (1,)), ((), ())), preferred_element_type=f32)


def exchange(blocks, axes):
    return lax.all_to_all(blocks, axes, 0, 0, tiled=True)


def swap_cores(value):
    return lax.ppermute(value, "c", [(0, 1), (1, 0)])


def swap_neighbours(value, nyl, nyh, outer):
    pairs = []
    for yh in range(nyh):
        first, second = yh, nyh + yh
        if outer:
            first, second = nyh + yh, (yh + 1) % nyh
        pairs += [(first, second), (second, first)]
    return lax.ppermute(value, ("yl", "yh"), pairs)


def from_opposite(value, nyl, nyh):
    pairs = []
    for yh in range(nyh):
        for yl in range(nyl):
            pairs.append(((1 - yl) * nyh + (yh + 2) % nyh, yl * nyh + yh))
    return lax.ppermute(value, ("yl", "yh"), pairs)


VMEM = pl.BlockSpec(memory_space=pltpu.VMEM)
SMEM = pl.BlockSpec(memory_space=pltpu.SMEM)
HBM = pl.BlockSpec(memory_space=pltpu.HBM)


def call(kernel, outs, args, spaces=None, out_spaces=None, scratch=(), copies=0, flops=0):
    spaces = spaces or [VMEM] * len(args)
    out_spaces = out_spaces or [VMEM] * len(outs)
    size = sum(a.size * a.dtype.itemsize for a in list(args) + list(outs))
    spare = [pltpu.VMEM(shape, kind) for shape, kind in scratch]
    spare_size = sum(
        a.size * a.dtype.itemsize for a in (jax.ShapeDtypeStruct(*pair) for pair in scratch)
    )
    if copies:
        spare.append(pltpu.SemaphoreType.DMA((copies,)))
    return pl.pallas_call(
        kernel,
        out_shape=outs,
        in_specs=spaces,
        out_specs=out_spaces,
        scratch_shapes=spare,
        compiler_params=pltpu.CompilerParams(vmem_limit_bytes=spare_size + 8 * MIB),
        cost_estimate=pl.CostEstimate(flops=flops, bytes_accessed=size, transcendentals=0),
    )(*args)


def adapter_slices(place_ref, own_ref, other_ref):
    slots, _, feats = own_ref.shape
    for k in range(slots):
        for ref, place in ((own_ref, place_ref[k]), (other_ref, place_ref[slots + k])):
            yield ref.at[k], pl.ds(pl.multiple_of(place * feats, feats), feats)


def project(place_ref, in_ref, own_ref, other_ref, latent_ref, latent_t_ref):
    rank = own_ref.shape[1] // 2
    tokens = in_ref.shape[0]
    acc = jnp.zeros((tokens, rank), f32)
    acc_t = jnp.zeros((rank, tokens), f32)
    for mats_ref, at in adapter_slices(place_ref, own_ref, other_ref):
        part = in_ref[:, at]
        down = mats_ref[:rank]
        acc += dot_rows(part, down)
        acc_t += dot_rows(down, part)
    latent_ref[...] = acc.astype(bf16)
    latent_t_ref[...] = acc_t.astype(bf16)


def hidden_slice(frozen_ref, latent, mats_ref, at):
    up = mats_ref[mats_ref.shape[0] // 2:]
    return frozen_ref[:, at].astype(f32) + adapter_scale_factor * dot(latent, up)


def forward(nyh, nc, place_ref, latent_ref, frozen_ref, gain_ref, own_ref, other_ref,
            inv_ref, unit_ref, length_ref, send_ref, hidden, part_ref):
    feats = own_ref.shape[2]
    slices = nyh * nc
    tokens, width = frozen_ref.shape
    queries = tokens // LEN
    latent = latent_ref[...]
    squares = jnp.zeros((tokens, 1), f32)
    for mats_ref, at in adapter_slices(place_ref, own_ref, other_ref):
        value = hidden_slice(frozen_ref, latent, mats_ref, at)
        hidden[:, at] = value
        squares += jnp.sum(value * value, axis=1, keepdims=True)
    inv = lax.rsqrt(squares / width + norm_eps)
    inv_ref[...] = jnp.broadcast_to(inv, inv_ref.shape)
    total = jnp.zeros((queries, 1), f32)
    for f in range(slices):
        at = slice(f * feats, (f + 1) * feats)
        scaled = hidden[:, at] * inv
        for q in range(queries):
            one = jnp.sum(scaled[q * LEN:(q + 1) * LEN], axis=0, keepdims=True)
            unit_ref[q:q + 1, at] = one * gain_ref[:, at] / LEN
        pooled = unit_ref[:, at]
        total += jnp.sum(pooled * pooled, axis=1, keepdims=True)
    length = jnp.sqrt(total)
    length_ref[...] = jnp.broadcast_to(length, length_ref.shape)
    for f in range(slices):
        at = slice(f * feats, (f + 1) * feats)
        unit = unit_ref[:, at] / length
        unit_ref[:, at] = unit
        part_ref[f % nc, f // nc * queries:(f // nc + 1) * queries, :] = unit
    for c in range(nc):
        rows = part_ref[c].astype(bf16)
        for y in range(send_ref.shape[0] // nc):
            send_ref[y * nc + c] = rows


def row_index(shape):
    return lax.broadcasted_iota(jnp.int32, shape, 0)


def start_slices(block_ref, parts, sems):
    feats = parts.shape[2]
    copies = [
        pltpu.make_async_copy(
            block_ref.at[:, k * feats:(k + 1) * feats], parts.at[k], sems.at[k]
        )
        for k in range(parts.shape[0])
    ]
    for copy in copies:
        copy.start()
    return copies


def score(nyh, query_ref, block_ref, out_ref, parts, sems):
    ring, rows, feats = query_ref.shape
    queries = rows // nyh
    columns = block_ref.shape[0]
    copies = start_slices(block_ref, parts, sems)
    query = query_ref[...].reshape(ring * rows, feats)
    mine = row_index((ring * rows, columns)) // queries % nyh
    total = jnp.zeros((ring * rows, columns), f32)
    gram = jnp.zeros((columns, columns), f32)
    for k in range(nyh):
        copies[k].wait()
        part = parts[k]
        total = jnp.where(mine == k, dot_rows(query, part), total)
        gram += dot_rows(part, part)
    total = total.reshape(ring, rows // 8, 8, columns)
    total = functools.reduce(jnp.add, [total[:, i] for i in range(rows // 8)])
    total = total.reshape(ring * 8, columns)
    count = ring * 8
    upper = row_index(total.shape) % 8 < 4
    total += jnp.where(upper, pltpu.roll(total, count - 4, 0), pltpu.roll(total, 4, 0))
    same = row_index(gram.shape) == lax.broadcasted_iota(jnp.int32, gram.shape, 1)
    norms = jnp.sum(jnp.where(same, gram, 0.0), axis=0, keepdims=True)
    out_ref[:count] = total
    out_ref[count:] = jnp.broadcast_to(norms, (8, columns))


def across(row):
    n = row.size
    return jnp.transpose(jnp.broadcast_to(row, (n, n)))


def exponentials(own_ref, other_ref, onehot_ref, expo_ref, aux_ref, rows_ref, cols_ref):
    count, columns = expo_ref.shape
    inv_norm = 1.0 / jnp.sqrt(own_ref[count:count + 1] + other_ref[count:count + 1])
    scores = inv_temp * ((own_ref[:count] + other_ref[:count]) * inv_norm)
    expo = jnp.exp(scores - inv_temp)
    expo_ref[...] = expo
    hits = 0.5 * jnp.sum(scores * onehot_ref[...])
    aux_ref[0:1] = inv_norm
    aux_ref[1:2] = jnp.full((1, columns), hits)
    row = across(jnp.sum(expo, axis=1, keepdims=True))[0:1]
    for y in range(rows_ref.shape[0]):
        rows_ref[y] = row
    col = 0.5 * jnp.sum(expo, axis=0, keepdims=True)
    for i in range(cols_ref.shape[0]):
        cols_ref[i] = col


def weigh(nyh, expo_ref, aux_ref, onehot_ref, rows_ref, cols_ref, block_ref,
          out_ref, loss_ref, total_ref, parts, sems):
    count, columns = expo_ref.shape
    ring, rows, feats = out_ref.shape
    queries = rows // nyh
    copies = start_slices(block_ref, parts, sems)
    ny, members = rows_ref.shape[0], cols_ref.shape[0]
    row = functools.reduce(jnp.add, [rows_ref[y] for y in range(ny)])
    col = functools.reduce(jnp.add, [cols_ref[i] for i in range(members)])
    loss = (
        0.5 * jnp.sum(jnp.log(row), axis=1, keepdims=True) / ny
        + jnp.sum(jnp.log(col), axis=1, keepdims=True) / members
        - 2.0 * aux_ref[1:2, 0:1]
    )
    loss_ref[...] = jnp.broadcast_to(loss, loss_ref.shape)
    expo = expo_ref[...]
    weights = 0.5 * (expo / across(row)[:, :1] + expo / col) - onehot_ref[...]
    weights = (weights * aux_ref[0:1]).reshape(ring, 1, 8, columns)
    weights = jnp.broadcast_to(weights, (ring, rows // 8, 8, columns))
    weights = weights.reshape(ring * rows, columns).astype(bf16)
    mine = row_index((ring * rows, feats)) // queries % nyh
    for k in range(nyh):
        copies[k].wait()
        part = inv_temp * dot(weights, parts[k])
        if k == 0:
            total_ref[...] = part
        else:
            total_ref[...] = jnp.where(mine == k, part, total_ref[...])
    out_ref[...] = total_ref[...].astype(bf16).reshape(out_ref.shape)


def backward(nyh, nc, place_ref, got_ref, unit_ref, length_ref, inv_ref, frozen_ref, gain_ref,
             in_ref, own_ref, other_ref, latent_ref, latent_t_ref, keep_ref, send_ref,
             grad_ref, scaled_ref, up_ref, hg_ref, hidden):
    _, both, feats = own_ref.shape
    slices = nyh * nc
    rank = both // 2
    tokens, width = in_ref.shape
    queries = tokens // LEN
    nx, _, pair_rows, cols = keep_ref.shape
    out_rows = pair_rows // 2
    for c in range(nc):
        total = got_ref[c].astype(f32)
        for y in range(1, got_ref.shape[0] // nc):
            total += got_ref[y * nc + c].astype(f32)
        grad_ref[c] = total
    inner = jnp.zeros((queries, 1), f32)
    for f in range(slices):
        at = slice(f * feats, (f + 1) * feats)
        grad = grad_ref[f % nc, f // nc * queries:(f // nc + 1) * queries, :]
        inner += jnp.sum(unit_ref[:, at] * grad, axis=1, keepdims=True)
    length = length_ref[:, :1]
    latent = latent_ref[...]
    for mats_ref, at in adapter_slices(place_ref, own_ref, other_ref):
        hidden[:, at] = hidden_slice(frozen_ref, latent, mats_ref, at)
    mean = [jnp.zeros((LEN, 1), f32) for q in range(queries)]
    for f in range(slices):
        at = slice(f * feats, (f + 1) * feats)
        grad = grad_ref[f % nc, f // nc * queries:(f // nc + 1) * queries, :]
        pooled_grad = (grad - unit_ref[:, at] * inner) / length
        scaled_ref[:, at] = pooled_grad / LEN * gain_ref[:, at]
        for q in range(queries):
            product = hidden[q * LEN:(q + 1) * LEN, at] * scaled_ref[q:q + 1, at]
            mean[q] += jnp.sum(product, axis=1, keepdims=True)
    inv = inv_ref[:, :1]
    factor = inv * inv * inv * (jnp.concatenate(mean, axis=0) / width)
    latent_t = latent_t_ref[...]
    acc = jnp.zeros((rank, tokens), f32)
    for mats_ref, at in adapter_slices(place_ref, own_ref, other_ref):
        for q in range(queries):
            of = slice(q * LEN, (q + 1) * LEN)
            hg_ref[of] = (
                inv[of] * scaled_ref[q:q + 1, at] - hidden[of, at] * factor[of]
            ).astype(bf16)
        hidden_grad = hg_ref[...]
        acc += dot_rows(mats_ref[rank:], hidden_grad)
        up_ref[:, at] = adapter_scale_factor * dot(latent_t, hidden_grad)
    latent_grad = (adapter_scale_factor * acc).astype(bf16)
    first = place_ref[2 * own_ref.shape[0]] == 0
    for f in range(slices):
        down = dot(latent_grad, in_ref[:, f * feats:(f + 1) * feats])
        for x in range(nx):
            lanes = slice(x * cols, (x + 1) * cols)
            spot = slice(f * feats + x * cols, f * feats + (x + 1) * cols)
            for yh in range(nyh):
                tiles = []
                for c in range(nc):
                    of = slice((yh * nc + c) * out_rows, (yh * nc + c + 1) * out_rows)
                    tiles.append(
                        jnp.concatenate([down[of, lanes], up_ref[of, spot]], axis=0).astype(bf16)
                    )
                keep_ref[x, f * nyh + yh] = jnp.where(first, tiles[0], tiles[1])
                send_ref[x, f * nyh + yh] = jnp.where(first, tiles[1], tiles[0])


def split_rows(value, rows, cols):
    high = value.astype(bf16).astype(f32)
    middle = (value - high).astype(bf16).astype(f32)
    low = value - high - middle
    at = row_index((rows, value.shape[1]))
    parts = jnp.where(at == 0, high, jnp.where(at == 1, middle, jnp.where(at == 2, low, 0.0)))
    return jnp.concatenate([parts] * (cols // value.shape[1]), axis=1).astype(bf16)


def join(keep_ref, got_ref, loss_ref, out_ref):
    nx, blocks, rows, cols = keep_ref.shape
    parts = split_rows(loss_ref[0:1], rows, cols)
    for x in range(nx):
        out_ref[x, :blocks] = (
            keep_ref[x].astype(f32) + got_ref[x].astype(f32)
        ).astype(bf16)
        out_ref[x, blocks] = parts


def add_line(got_ref, out_ref):
    total = got_ref[0].astype(f32)
    for x in range(1, got_ref.shape[0]):
        total += got_ref[x].astype(f32)
    blocks, _, cols = out_ref.shape
    rows = got_ref.shape[2]
    loss = jnp.sum(total[blocks], axis=0, keepdims=True)[:, :128]
    out_ref[:, :rows] = total[:blocks].astype(bf16)
    out_ref[:, rows:] = jnp.broadcast_to(split_rows(loss, rows, cols)[None], (blocks, rows, cols))


def add_last(total_pairs, got_ref, out_ref, loss_ref):
    total = got_ref[0].astype(f32)
    for i in range(1, got_ref.shape[0]):
        total += got_ref[i].astype(f32)
    rows = out_ref.shape[1]
    out_ref[0] = total[:rows]
    out_ref[1] = total[rows:2 * rows]
    loss_ref[0, 0] = jnp.sum(total[2 * rows:, :1]) / (2.0 * total_pairs) + inv_temp


def shards(sizes, adapter_in, frozen, gain, adapter_a, adapter_up_matrix, passages, positive):
    nzh, nzl, nyl, nx, nyh, nc = sizes
    izh, izl, iyl, ix, iyh, ic = (lax.axis_index(axis) for axis in AXES)
    rank = adapter_up_matrix.shape[0]
    feats = passages.shape[1]
    half = nyh * feats
    width = half * nc
    tokens = adapter_in.shape[0]
    queries = tokens // LEN
    group = passages.shape[0]
    rows = group // nyh
    ny = nyl * nyh
    ring = ny * nc
    members = nzh * nzl * nx
    shape = jax.ShapeDtypeStruct
    gain = gain.reshape(1, width)

    sent = jnp.broadcast_to(passages.reshape(1, nyh, rows, feats), (nzh, nyh, rows, feats))
    got = exchange(sent.reshape(nzh * nyh, rows, feats), ("zh", "yh"))

    mine = jnp.concatenate([adapter_a.T, adapter_up_matrix], axis=0)
    slots = [mine]
    slots.append(swap_neighbours(mine, nyl, nyh, True))
    got, slots[1] = lax.optimization_barrier((got, slots[1]))
    if nyh == 4:
        slots.append(swap_neighbours(slots[1], nyl, nyh, False))
        slots.append(from_opposite(mine, nyl, nyh))
    own_mats = jnp.stack(slots)
    other_mats = swap_cores(own_mats)
    side = 1 - 2 * (1 - iyl)
    places = jnp.stack([iyh, iyh + side, iyh - side, iyh + 2][:nyh]).astype(jnp.int32) % nyh * nc
    place = jnp.concatenate([places + ic, places + 1 - ic, ic.reshape(1)]).astype(jnp.int32)

    got = got.reshape(nzh, nyh, rows, feats).transpose(0, 2, 1, 3).reshape(nzh * rows, half)
    got = jnp.broadcast_to(got[None], (nzl * nx, nzh * rows, half))
    block = exchange(got, ("zl", "x")).reshape(members * rows, half)
    columns = block.shape[0]

    latent, latent_t = call(
        project,
        [shape((tokens, rank), bf16), shape((rank, tokens), bf16)],
        [place, adapter_in, own_mats, other_mats],
        spaces=[SMEM, VMEM, VMEM, VMEM],
        flops=4 * tokens * rank * width,
    )
    inv, unit, length, sent = call(
        functools.partial(forward, nyh, nc),
        [
            shape((tokens, 128), f32),
            shape((queries, width), f32),
            shape((queries, 128), f32),
            shape((ring, nyh * queries, feats), bf16),
        ],
        [place, latent, frozen, gain, own_mats, other_mats],
        spaces=[SMEM] + [VMEM] * 5,
        scratch=[((tokens, width), f32), ((nc, nyh * queries, feats), f32)],
        flops=2 * tokens * rank * width,
    )
    sent, block = lax.optimization_barrier((sent, block))
    query = exchange(sent, RING)

    count = ring * 8
    at = lax.iota(jnp.int32, columns)
    at_zl, at_x, at_zh, at_row = (
        at // (nx * nzh * rows), at // (nzh * rows) % nx, at // rows % nzh, at % rows
    )
    passage_id = ((at_zh * nzl + at_zl) * nyl + iyl) * nx + at_x
    passage_id = passage_id * group + iyh * rows + at_row
    own_pos = jnp.where(
        lax.iota(jnp.int32, nyl)[:, None] == iyl, positive[None, :], -1
    ).reshape(ring, 1, queries)
    own_pos = jnp.broadcast_to(own_pos, (ring, 8 // queries, queries)).reshape(count)
    onehot = (own_pos[:, None] == passage_id[None, :]).astype(f32)
    (own,) = call(
        functools.partial(score, nyh),
        [shape((count + 8, columns), f32)],
        [query, block],
        spaces=[VMEM, HBM],
        scratch=[((nyh, columns, feats), bf16)],
        copies=nyh,
        flops=4 * ring * nyh * queries * columns * half,
    )
    other = swap_cores(own)
    expo, aux, by_row, by_col = call(
        exponentials,
        [
            shape((count, columns), f32),
            shape((8, columns), f32),
            shape((ny, 1, count), f32),
            shape((members, 1, columns), f32),
        ],
        [own, other, onehot],
    )
    by_row = exchange(by_row, ROW)
    by_col = exchange(by_col, COLUMN)
    sent, loss = call(
        functools.partial(weigh, nyh),
        [shape((ring, nyh * queries, feats), bf16), shape((8, 128), f32)],
        [expo, aux, onehot, by_row, by_col, block],
        spaces=[VMEM] * 5 + [HBM],
        scratch=[((ring * nyh * queries, feats), f32), ((nyh, columns, feats), bf16)],
        copies=nyh,
        flops=2 * ring * nyh * queries * columns * half,
    )
    got = exchange(sent, RING)

    out_rows = rank // (nyh * nc)
    cols = width // (nzh * nzl * nyl * nx)
    blocks = nzh * nzl * nyh
    keep, send = call(
        functools.partial(backward, nyh, nc),
        [shape((nyl * nx, blocks, 2 * out_rows, cols), bf16)] * 2,
        [
            place, got, unit, length, inv, frozen, gain, adapter_in, own_mats, other_mats,
            latent, latent_t,
        ],
        spaces=[SMEM] + [VMEM] * 11,
        scratch=[
            ((nc, nyh * queries, feats), f32),
            ((queries, width), f32),
            ((rank, width), f32),
            ((tokens, feats), bf16),
            ((tokens, width), f32),
        ],
        flops=8 * tokens * rank * width,
    )
    (chip,) = call(
        join,
        [shape((nyl * nx, blocks + 1, 2 * out_rows, cols), bf16)],
        [keep, swap_cores(send), loss],
    )
    (line,) = call(
        add_line, [shape((blocks, 4 * out_rows, cols), bf16)], [exchange(chip, ("yl", "x"))]
    )
    adapter_grads, loss = call(
        functools.partial(add_last, group * nyl * members),
        [shape((2, out_rows, cols), f32), shape((1, 1), f32)],
        [exchange(line, ("zh", "zl", "yh"))],
        out_spaces=[VMEM, SMEM],
    )
    return (adapter_grads, loss.reshape(()))


def build(mesh, sizes):
    split = Mesh(mesh.devices.reshape(sizes), AXES)
    dp, fsdp = ("zh", "zl", "yl", "x"), ("yh", "c")
    placed = (
        P(AXES, None),
        P(AXES, None),
        P(),
        P(fsdp, None),
        P(None, fsdp),
        P(dp, fsdp),
        P(dp),
    )
    return jax.shard_map(
        lambda *args: shards(sizes, *args),
        mesh=split,
        in_specs=placed,
        out_specs=(P(None, fsdp, dp), P()),
        check_vma=False,
    )


def solution(mesh):
    return build(mesh, SIZES)
```

```python
import functools

import jax
import jax.numpy as jnp
from jax import lax
from jax.experimental import pallas as pl
from jax.experimental.pallas import tpu as pltpu
from jax.sharding import Mesh
from jax.sharding import PartitionSpec as P

LEN = 32


adapter_scale_factor = 0.25
inv_temp = 20.0
norm_eps = 1e-05

AXES = ("zh", "zl", "yl", "x", "yh", "c")
SIZES = (4, 2, 2, 4, 4, 2)
ROW, COLUMN, RING = ("yl", "yh"), ("zh", "zl", "x"), ("yl", "yh", "c")
MIB = 1 << 20
f32, bf16 = jnp.float32, jnp.bfloat16


def dot(left, right):
    return jnp.dot(left, right, preferred_element_type=f32)


def dot_rows(left, right):
    return lax.dot_general(left, right, (((1,), (1,)), ((), ())), preferred_element_type=f32)


def exchange(blocks, axes):
    return lax.all_to_all(blocks, axes, 0, 0, tiled=True)


def swap_cores(value):
    return lax.ppermute(value, "c", [(0, 1), (1, 0)])


def swap_neighbours(value, nyl, nyh, outer):
    pairs = []
    for yh in range(nyh):
        first, second = yh, nyh + yh
        if outer:
            first, second = nyh + yh, (yh + 1) % nyh
        pairs += [(first, second), (second, first)]
    return lax.ppermute(value, ("yl", "yh"), pairs)


def from_opposite(value, nyl, nyh):
    pairs = []
    for yh in range(nyh):
        for yl in range(nyl):
            pairs.append(((1 - yl) * nyh + (yh + 2) % nyh, yl * nyh + yh))
    return lax.ppermute(value, ("yl", "yh"), pairs)


VMEM = pl.BlockSpec(memory_space=pltpu.VMEM)
SMEM = pl.BlockSpec(memory_space=pltpu.SMEM)
HBM = pl.BlockSpec(memory_space=pltpu.HBM)


def call(kernel, outs, args, spaces=None, out_spaces=None, scratch=(), copies=0, flops=0):
    spaces = spaces or [VMEM] * len(args)
    out_spaces = out_spaces or [VMEM] * len(outs)
    size = sum(a.size * a.dtype.itemsize for a in list(args) + list(outs))
    spare = [pltpu.VMEM(shape, kind) for shape, kind in scratch]
    spare_size = sum(
        a.size * a.dtype.itemsize for a in (jax.ShapeDtypeStruct(*pair) for pair in scratch)
    )
    if copies:
        spare.append(pltpu.SemaphoreType.DMA((copies,)))
    return pl.pallas_call(
        kernel,
        out_shape=outs,
        in_specs=spaces,
        out_specs=out_spaces,
        scratch_shapes=spare,
        compiler_params=pltpu.CompilerParams(vmem_limit_bytes=spare_size + 8 * MIB),
        cost_estimate=pl.CostEstimate(flops=flops, bytes_accessed=size, transcendentals=0),
    )(*args)


def adapter_slices(place_ref, own_ref, other_ref):
    slots, _, feats = own_ref.shape
    for k in range(slots):
        for ref, place in ((own_ref, place_ref[k]), (other_ref, place_ref[slots + k])):
            yield ref.at[k], pl.ds(pl.multiple_of(place * feats, feats), feats)


def project(place_ref, in_ref, own_ref, other_ref, latent_ref, latent_t_ref):
    rank = own_ref.shape[1] // 2
    tokens = in_ref.shape[0]
    acc = jnp.zeros((tokens, rank), f32)
    acc_t = jnp.zeros((rank, tokens), f32)
    for mats_ref, at in adapter_slices(place_ref, own_ref, other_ref):
        part = in_ref[:, at]
        down = mats_ref[:rank]
        acc += dot_rows(part, down)
        acc_t += dot_rows(down, part)
    latent_ref[...] = acc.astype(bf16)
    latent_t_ref[...] = acc_t.astype(bf16)


def hidden_slice(frozen_ref, latent, mats_ref, at):
    up = mats_ref[mats_ref.shape[0] // 2:]
    return frozen_ref[:, at].astype(f32) + adapter_scale_factor * dot(latent, up)


def forward(nyh, nc, place_ref, latent_ref, frozen_ref, gain_ref, own_ref, other_ref,
            inv_ref, unit_ref, length_ref, send_ref, hidden, part_ref):
    feats = own_ref.shape[2]
    slices = nyh * nc
    tokens, width = frozen_ref.shape
    queries = tokens // LEN
    latent = latent_ref[...]
    squares = jnp.zeros((tokens, 1), f32)
    for mats_ref, at in adapter_slices(place_ref, own_ref, other_ref):
        value = hidden_slice(frozen_ref, latent, mats_ref, at)
        hidden[:, at] = value
        squares += jnp.sum(value * value, axis=1, keepdims=True)
    inv = lax.rsqrt(squares / width + norm_eps)
    inv_ref[...] = jnp.broadcast_to(inv, inv_ref.shape)
    total = jnp.zeros((queries, 1), f32)
    for f in range(slices):
        at = slice(f * feats, (f + 1) * feats)
        scaled = hidden[:, at] * inv
        for q in range(queries):
            one = jnp.sum(scaled[q * LEN:(q + 1) * LEN], axis=0, keepdims=True)
            unit_ref[q:q + 1, at] = one * gain_ref[:, at] / LEN
        pooled = unit_ref[:, at]
        total += jnp.sum(pooled * pooled, axis=1, keepdims=True)
    length = jnp.sqrt(total)
    length_ref[...] = jnp.broadcast_to(length, length_ref.shape)
    for f in range(slices):
        at = slice(f * feats, (f + 1) * feats)
        unit = unit_ref[:, at] / length
        unit_ref[:, at] = unit
        part_ref[f % nc, f // nc * queries:(f // nc + 1) * queries, :] = unit
    for c in range(nc):
        rows = part_ref[c].astype(bf16)
        for y in range(send_ref.shape[0] // nc):
            send_ref[y * nc + c] = rows


def row_index(shape):
    return lax.broadcasted_iota(jnp.int32, shape, 0)


def start_slices(block_ref, parts, sems):
    feats = parts.shape[2]
    copies = [
        pltpu.make_async_copy(
            block_ref.at[:, k * feats:(k + 1) * feats], parts.at[k], sems.at[k]
        )
        for k in range(parts.shape[0])
    ]
    for copy in copies:
        copy.start()
    return copies


def score(nyh, query_ref, block_ref, out_ref, parts, sems):
    ring, rows, feats = query_ref.shape
    queries = rows // nyh
    columns = block_ref.shape[0]
    copies = start_slices(block_ref, parts, sems)
    query = query_ref[...].reshape(ring * rows, feats)
    mine = row_index((ring * rows, columns)) // queries % nyh
    total = jnp.zeros((ring * rows, columns), f32)
    gram = jnp.zeros((columns, columns), f32)
    for k in range(nyh):
        copies[k].wait()
        part = parts[k]
        total = jnp.where(mine == k, dot_rows(query, part), total)
        gram += dot_rows(part, part)
    total = total.reshape(ring, rows // 8, 8, columns)
    total = functools.reduce(jnp.add, [total[:, i] for i in range(rows // 8)])
    total = total.reshape(ring * 8, columns)
    count = ring * 8
    upper = row_index(total.shape) % 8 < 4
    total += jnp.where(upper, pltpu.roll(total, count - 4, 0), pltpu.roll(total, 4, 0))
    same = row_index(gram.shape) == lax.broadcasted_iota(jnp.int32, gram.shape, 1)
    norms = jnp.sum(jnp.where(same, gram, 0.0), axis=0, keepdims=True)
    out_ref[:count] = total
    out_ref[count:] = jnp.broadcast_to(norms, (8, columns))


def across(row):
    n = row.size
    return jnp.transpose(jnp.broadcast_to(row, (n, n)))


def exponentials(own_ref, other_ref, onehot_ref, expo_ref, aux_ref, rows_ref, cols_ref):
    count, columns = expo_ref.shape
    inv_norm = 1.0 / jnp.sqrt(own_ref[count:count + 1] + other_ref[count:count + 1])
    scores = inv_temp * ((own_ref[:count] + other_ref[:count]) * inv_norm)
    expo = jnp.exp(scores - inv_temp)
    expo_ref[...] = expo
    hits = 0.5 * jnp.sum(scores * onehot_ref[...])
    aux_ref[0:1] = inv_norm
    aux_ref[1:2] = jnp.full((1, columns), hits)
    row = across(jnp.sum(expo, axis=1, keepdims=True))[0:1]
    for y in range(rows_ref.shape[0]):
        rows_ref[y] = row
    col = 0.5 * jnp.sum(expo, axis=0, keepdims=True)
    for i in range(cols_ref.shape[0]):
        cols_ref[i] = col


def weigh(nyh, expo_ref, aux_ref, onehot_ref, rows_ref, cols_ref, block_ref,
          out_ref, loss_ref, total_ref, parts, sems):
    count, columns = expo_ref.shape
    ring, rows, feats = out_ref.shape
    queries = rows // nyh
    copies = start_slices(block_ref, parts, sems)
    ny, members = rows_ref.shape[0], cols_ref.shape[0]
    row = functools.reduce(jnp.add, [rows_ref[y] for y in range(ny)])
    col = functools.reduce(jnp.add, [cols_ref[i] for i in range(members)])
    loss = (
        0.5 * jnp.sum(jnp.log(row), axis=1, keepdims=True) / ny
        + jnp.sum(jnp.log(col), axis=1, keepdims=True) / members
        - 2.0 * aux_ref[1:2, 0:1]
    )
    loss_ref[...] = jnp.broadcast_to(loss, loss_ref.shape)
    expo = expo_ref[...]
    weights = 0.5 * (expo / across(row)[:, :1] + expo / col) - onehot_ref[...]
    weights = (weights * aux_ref[0:1]).reshape(ring, 1, 8, columns)
    weights = jnp.broadcast_to(weights, (ring, rows // 8, 8, columns))
    weights = weights.reshape(ring * rows, columns).astype(bf16)
    mine = row_index((ring * rows, feats)) // queries % nyh
    for k in range(nyh):
        copies[k].wait()
        part = inv_temp * dot(weights, parts[k])
        if k == 0:
            total_ref[...] = part
        else:
            total_ref[...] = jnp.where(mine == k, part, total_ref[...])
    out_ref[...] = total_ref[...].astype(bf16).reshape(out_ref.shape)


def backward(nyh, nc, nzl, place_ref, got_ref, unit_ref, length_ref, inv_ref, frozen_ref, gain_ref,
             in_ref, own_ref, other_ref, latent_ref, latent_t_ref, keep_ref, send_ref,
             grad_ref, scaled_ref, up_ref, hg_ref, hidden):
    _, both, feats = own_ref.shape
    slices = nyh * nc
    rank = both // 2
    tokens, width = in_ref.shape
    queries = tokens // LEN
    peers, _, pair_rows, cols = keep_ref.shape
    line = peers // nzl
    out_rows = pair_rows // 2
    for c in range(nc):
        total = got_ref[c].astype(f32)
        for y in range(1, got_ref.shape[0] // nc):
            total += got_ref[y * nc + c].astype(f32)
        grad_ref[c] = total
    inner = jnp.zeros((queries, 1), f32)
    for f in range(slices):
        at = slice(f * feats, (f + 1) * feats)
        grad = grad_ref[f % nc, f // nc * queries:(f // nc + 1) * queries, :]
        inner += jnp.sum(unit_ref[:, at] * grad, axis=1, keepdims=True)
    length = length_ref[:, :1]
    latent = latent_ref[...]
    for mats_ref, at in adapter_slices(place_ref, own_ref, other_ref):
        hidden[:, at] = hidden_slice(frozen_ref, latent, mats_ref, at)
    mean = [jnp.zeros((LEN, 1), f32) for q in range(queries)]
    for f in range(slices):
        at = slice(f * feats, (f + 1) * feats)
        grad = grad_ref[f % nc, f // nc * queries:(f // nc + 1) * queries, :]
        pooled_grad = (grad - unit_ref[:, at] * inner) / length
        scaled_ref[:, at] = pooled_grad / LEN * gain_ref[:, at]
        for q in range(queries):
            product = hidden[q * LEN:(q + 1) * LEN, at] * scaled_ref[q:q + 1, at]
            mean[q] += jnp.sum(product, axis=1, keepdims=True)
    inv = inv_ref[:, :1]
    factor = inv * inv * inv * (jnp.concatenate(mean, axis=0) / width)
    latent_t = latent_t_ref[...]
    acc = jnp.zeros((rank, tokens), f32)
    for mats_ref, at in adapter_slices(place_ref, own_ref, other_ref):
        for q in range(queries):
            of = slice(q * LEN, (q + 1) * LEN)
            hg_ref[of] = (
                inv[of] * scaled_ref[q:q + 1, at] - hidden[of, at] * factor[of]
            ).astype(bf16)
        hidden_grad = hg_ref[...]
        acc += dot_rows(mats_ref[rank:], hidden_grad)
        up_ref[:, at] = adapter_scale_factor * dot(latent_t, hidden_grad)
    latent_grad = (adapter_scale_factor * acc).astype(bf16)
    first = place_ref[2 * own_ref.shape[0]] == 0
    for f in range(slices):
        down = dot(latent_grad, in_ref[:, f * feats:(f + 1) * feats])
        for x in range(line):
            lanes = slice(x * cols, (x + 1) * cols)
            spot = slice(f * feats + x * cols, f * feats + (x + 1) * cols)
            for yh in range(nyh):
                tiles = []
                for c in range(nc):
                    of = slice((yh * nc + c) * out_rows, (yh * nc + c + 1) * out_rows)
                    tiles.append(
                        jnp.concatenate([down[of, lanes], up_ref[of, spot]], axis=0).astype(bf16)
                    )
                keep_ref[f % nzl * line + x, f // nzl * nyh + yh] = jnp.where(first, tiles[0], tiles[1])
                send_ref[f % nzl * line + x, f // nzl * nyh + yh] = jnp.where(first, tiles[1], tiles[0])


def split_rows(value, rows, cols):
    high = value.astype(bf16).astype(f32)
    middle = (value - high).astype(bf16).astype(f32)
    low = value - high - middle
    at = row_index((rows, value.shape[1]))
    parts = jnp.where(at == 0, high, jnp.where(at == 1, middle, jnp.where(at == 2, low, 0.0)))
    return jnp.concatenate([parts] * (cols // value.shape[1]), axis=1).astype(bf16)


def join(keep_ref, got_ref, loss_ref, out_ref):
    nx, blocks, rows, cols = keep_ref.shape
    parts = split_rows(loss_ref[0:1], rows, cols)
    for x in range(nx):
        out_ref[x, :blocks] = (
            keep_ref[x].astype(f32) + got_ref[x].astype(f32)
        ).astype(bf16)
        out_ref[x, blocks] = parts


def add_line(got_ref, out_ref):
    total = got_ref[0].astype(f32)
    for x in range(1, got_ref.shape[0]):
        total += got_ref[x].astype(f32)
    blocks, _, cols = out_ref.shape
    rows = got_ref.shape[2]
    loss = jnp.sum(total[blocks], axis=0, keepdims=True)[:, :128]
    out_ref[:, :rows] = total[:blocks].astype(bf16)
    out_ref[:, rows:] = jnp.broadcast_to(split_rows(loss, rows, cols)[None], (blocks, rows, cols))


def add_last(total_pairs, got_ref, out_ref, loss_ref):
    total = got_ref[0].astype(f32)
    for i in range(1, got_ref.shape[0]):
        total += got_ref[i].astype(f32)
    rows = out_ref.shape[1]
    out_ref[0] = total[:rows]
    out_ref[1] = total[rows:2 * rows]
    loss_ref[0, 0] = jnp.sum(total[2 * rows:, :1]) / (2.0 * total_pairs) + inv_temp


def shards(sizes, adapter_in, frozen, gain, adapter_a, adapter_up_matrix, passages, positive):
    nzh, nzl, nyl, nx, nyh, nc = sizes
    izh, izl, iyl, ix, iyh, ic = (lax.axis_index(axis) for axis in AXES)
    rank = adapter_up_matrix.shape[0]
    feats = passages.shape[1]
    half = nyh * feats
    width = half * nc
    tokens = adapter_in.shape[0]
    queries = tokens // LEN
    group = passages.shape[0]
    rows = group // nyh
    ny = nyl * nyh
    ring = ny * nc
    members = nzh * nzl * nx
    shape = jax.ShapeDtypeStruct
    gain = gain.reshape(1, width)

    sent = jnp.broadcast_to(passages.reshape(1, nyh, rows, feats), (nzh, nyh, rows, feats))
    got = exchange(sent.reshape(nzh * nyh, rows, feats), ("zh", "yh"))

    mine = jnp.concatenate([adapter_a.T, adapter_up_matrix], axis=0)
    slots = [mine]
    slots.append(swap_neighbours(mine, nyl, nyh, True))
    got, slots[1] = lax.optimization_barrier((got, slots[1]))
    if nyh == 4:
        slots.append(swap_neighbours(slots[1], nyl, nyh, False))
        slots.append(from_opposite(mine, nyl, nyh))
    own_mats = jnp.stack(slots)
    other_mats = swap_cores(own_mats)
    side = 1 - 2 * (1 - iyl)
    places = jnp.stack([iyh, iyh + side, iyh - side, iyh + 2][:nyh]).astype(jnp.int32) % nyh * nc
    place = jnp.concatenate([places + ic, places + 1 - ic, ic.reshape(1)]).astype(jnp.int32)

    got = got.reshape(nzh, nyh, rows, feats).transpose(0, 2, 1, 3).reshape(nzh * rows, half)
    got = jnp.broadcast_to(got[None], (nzl * nx, nzh * rows, half))
    block = exchange(got, ("zl", "x")).reshape(members * rows, half)
    columns = block.shape[0]

    latent, latent_t = call(
        project,
        [shape((tokens, rank), bf16), shape((rank, tokens), bf16)],
        [place, adapter_in, own_mats, other_mats],
        spaces=[SMEM, VMEM, VMEM, VMEM],
        flops=4 * tokens * rank * width,
    )
    inv, unit, length, sent = call(
        functools.partial(forward, nyh, nc),
        [
            shape((tokens, 128), f32),
            shape((queries, width), f32),
            shape((queries, 128), f32),
            shape((ring, nyh * queries, feats), bf16),
        ],
        [place, latent, frozen, gain, own_mats, other_mats],
        spaces=[SMEM] + [VMEM] * 5,
        scratch=[((tokens, width), f32), ((nc, nyh * queries, feats), f32)],
        flops=2 * tokens * rank * width,
    )
    sent, block = lax.optimization_barrier((sent, block))
    query = exchange(sent, RING)

    count = ring * 8
    at = lax.iota(jnp.int32, columns)
    at_zl, at_x, at_zh, at_row = (
        at // (nx * nzh * rows), at // (nzh * rows) % nx, at // rows % nzh, at % rows
    )
    passage_id = ((at_zh * nzl + at_zl) * nyl + iyl) * nx + at_x
    passage_id = passage_id * group + iyh * rows + at_row
    own_pos = jnp.where(
        lax.iota(jnp.int32, nyl)[:, None] == iyl, positive[None, :], -1
    ).reshape(ring, 1, queries)
    own_pos = jnp.broadcast_to(own_pos, (ring, 8 // queries, queries)).reshape(count)
    onehot = (own_pos[:, None] == passage_id[None, :]).astype(f32)
    (own,) = call(
        functools.partial(score, nyh),
        [shape((count + 8, columns), f32)],
        [query, block],
        spaces=[VMEM, HBM],
        scratch=[((nyh, columns, feats), bf16)],
        copies=nyh,
        flops=4 * ring * nyh * queries * columns * half,
    )
    other = swap_cores(own)
    expo, aux, by_row, by_col = call(
        exponentials,
        [
            shape((count, columns), f32),
            shape((8, columns), f32),
            shape((ny, 1, count), f32),
            shape((members, 1, columns), f32),
        ],
        [own, other, onehot],
    )
    by_row = exchange(by_row, ROW)
    by_col = exchange(by_col, COLUMN)
    sent, loss = call(
        functools.partial(weigh, nyh),
        [shape((ring, nyh * queries, feats), bf16), shape((8, 128), f32)],
        [expo, aux, onehot, by_row, by_col, block],
        spaces=[VMEM] * 5 + [HBM],
        scratch=[((ring * nyh * queries, feats), f32), ((nyh, columns, feats), bf16)],
        copies=nyh,
        flops=2 * ring * nyh * queries * columns * half,
    )
    got = exchange(sent, RING)

    out_rows = rank // (nyh * nc)
    cols = width // (nzh * nzl * nyl * nx)
    blocks = nzh * nyh
    peers = nzl * nyl * nx
    keep, send = call(
        functools.partial(backward, nyh, nc, nzl),
        [shape((peers, blocks, 2 * out_rows, cols), bf16)] * 2,
        [
            place, got, unit, length, inv, frozen, gain, adapter_in, own_mats, other_mats,
            latent, latent_t,
        ],
        spaces=[SMEM] + [VMEM] * 11,
        scratch=[
            ((nc, nyh * queries, feats), f32),
            ((queries, width), f32),
            ((rank, width), f32),
            ((tokens, feats), bf16),
            ((tokens, width), f32),
        ],
        flops=8 * tokens * rank * width,
    )
    (chip,) = call(
        join,
        [shape((peers, blocks + 1, 2 * out_rows, cols), bf16)],
        [keep, swap_cores(send), loss],
    )
    (line,) = call(
        add_line, [shape((blocks, 4 * out_rows, cols), bf16)], [exchange(chip, ("zl", "yl", "x"))]
    )
    adapter_grads, loss = call(
        functools.partial(add_last, group * nyl * members),
        [shape((2, out_rows, cols), f32), shape((1, 1), f32)],
        [exchange(line, ("zh", "yh"))],
        out_spaces=[VMEM, SMEM],
    )
    return (adapter_grads, loss.reshape(()))


def build(mesh, sizes):
    split = Mesh(mesh.devices.reshape(sizes), AXES)
    dp, fsdp = ("zh", "zl", "yl", "x"), ("yh", "c")
    placed = (
        P(AXES, None),
        P(AXES, None),
        P(),
        P(fsdp, None),
        P(None, fsdp),
        P(dp, fsdp),
        P(dp),
    )
    return jax.shard_map(
        lambda *args: shards(sizes, *args),
        mesh=split,
        in_specs=placed,
        out_specs=(P(None, fsdp, dp), P()),
        check_vma=False,
    )


def solution(mesh):
    return build(mesh, SIZES)
```
